256 devices in a mesh: section: 4 (over z_hi, core), dp: 64 (over x, y, z_lo).
Axes of the slice: x: 4, y: 4, z: 8 (z_hi: 2, z_lo: 4; z = z_hi * 4 + z_lo), core: 2. Of those that a mesh axis runs over, the one named last changes fastest.
Arguments:
- qkv_a: bfloat16 [4, 8192, 5120], P('section', 'dp'), may hold values from -4 to 4
- qkv_b: bfloat16 [4, 8192, 5120], P('section', 'dp'), may hold values from -4 to 4
- slot_grad_b: bfloat16 [4, 24576, 4096], P('section', 'dp'), may hold values from -16 to 16
- adapter_down: bfloat16 [4, 4096, 64], P('section'), may hold values from -0.09375 to 0.09375
- adapter_up: bfloat16 [4, 64, 4096], P('section'), may hold values from -0.75 to 0.75
- lang_scale: float32 [102], replicated, may hold values from 0.25 to 1
- languages: int32 [2, 64], replicated, may hold values from 0 to 101
- lengths: int32 [2, 64, 8], replicated, may hold values from 1 to 64, 128 in all within a row
- destination: int32 [2, 64], replicated, may hold values from 0 to 63, as said below
Outputs:
- handed_forward: bfloat16 [4, 24576, 4096], P('section', 'dp')
- handed_back: bfloat16 [4, 8192, 5120], P('section', 'dp')
- adapter_grad: float32 [4, 4096, 128], P('section', 'dp')
The draws below stay inside these ranges and needn't reach their ends.
Inputs may be any that keep to these rules, and one draw needn't show every extreme that they name: `destination`: of each micro-batch, a data rank's first tile goes to that rank or the rank before it, its last tile to that rank or the rank after it, its other tiles stay; at most one tile of a rank leaves.
All inputs are finite; a program needn't handle non-finite values.
Results may differ from the reference program's by a relative error of at most 0.014.
Values may be sent and summed in bfloat16 or wider, within the bound.
No kernel may reach another device: no remote copies, remote signals or barrier semaphores. Data moves between devices by JAX's collectives and lax.ppermute only.
A program may use at most 128 MiB of HBM per device.

```python
import math
import jax
import jax.numpy as jnp
import numpy as np
from jax import lax

HEADS = 32
KV = 4
HEAD_DIM = 128
RANK = 64
TILE = 128
SEGS = 8
MOST = 64
LANGS = 102
TILES = 1
QW = 4096
KW = 512
TILES_ALL = 64
ROWS = 8192
SLOT_ROWS = 24576
N_SECTION = 4
N_DP = 64


def joined_values(key):
    shape = (N_SECTION, ROWS, QW + 2 * KW)
    return jnp.clip(jax.random.normal(key, shape, jnp.float32), -4.0, 4.0)


def draw_qkv_a(key, part):
    key = jax.random.fold_in(key, 11)
    return joined_values(key).astype(jnp.bfloat16)


def draw_qkv_b(key, part):
    key = jax.random.fold_in(key, 23)
    return joined_values(key).astype(jnp.bfloat16)


def draw_destination(key, part):
    key = jax.random.fold_in(key, 37)
    modes = jax.random.randint(key, (2, N_DP, 1), 0, 3)
    group = jnp.arange(N_DP, dtype=jnp.int32)[None, :, None]
    middle = N_DP // 2
    modes = jnp.where(group == 0, 2, modes)
    modes = jnp.where((group == middle) | (group == middle + 1), 1, modes)
    place = jnp.arange(TILES, dtype=jnp.int32)[None, None, :]
    go_left = (modes == 1) & (group > 0) & (place == 0)
    go_right = (modes == 2) & (group < N_DP - 1) & (place == TILES - 1)
    target = jnp.where(go_left, group - 1, jnp.where(go_right, group + 1, group))
    return target.reshape(2, N_DP * TILES).astype(jnp.int32)


def place_ends(values, own_key, smallest, top_value):
    shape = values.shape
    spot = [jax.random.randint(jax.random.fold_in(own_key, axis), (), 0, shape[axis]) for axis in range(len(shape))]
    values = values.at[tuple(spot)].set(smallest)
    longest = shape.index(max(shape))
    spot[longest] = (spot[longest] + 1) % shape[longest]
    return values.at[tuple(spot)].set(top_value)


def strengthened(values, stream_key, source, target, parts, factor):
    def block_of(axis_at):
        return (jnp.arange(values.shape[axis_at]) // (values.shape[axis_at] // parts)).reshape((-1,) + (1,) * (values.ndim - 1 - axis_at))

    first = jax.random.permutation(stream_key, parts)[block_of(target)]
    other_side = (block_of(target) + parts // 2) % parts
    return jnp.where((block_of(source) == first) | (block_of(source) == other_side), factor * values, values)


def block_scale(key, extent, shards, least, top_value):
    gain = 1.0
    for position, shards_of in shards:
        steps = jax.random.uniform(jax.random.fold_in(jax.random.fold_in(key, 6), position), (shards_of,), jnp.float32, least / len(shards), top_value / len(shards))
        gain = gain * jnp.repeat(jnp.exp(steps), extent[position] // shards_of).reshape((-1,) + (1,) * (len(extent) - 1 - position))
    return gain


def split_up(amount, total, bound, slope):
    weights = [(1 << 20) // math.isqrt(rank ** slope) + 1 for rank in range(2, amount + 1)]
    spare, holding = total - bound - (amount - 1), [1] * (amount - 1)
    while spare > 0:
        movable = [i for i in range(amount - 1) if holding[i] < bound]
        mass, left = sum([weights[i] for i in movable]), spare
        for i in movable:
            extra = min(bound - holding[i], max(1, left * weights[i] // mass), spare)
            holding[i] = holding[i] + extra
            spare = spare - extra
    return np.array([bound] + holding)


def uneven(rng, count, total, most, lean):
    if count == 2:
        one = jax.random.randint(rng, (), max(1, total - most), min(most, total - 1) + 1)
        return jnp.stack([one, total - one])
    tallies = jnp.asarray(split_up(count, total, most, lean), jnp.int32)
    twos = (count - 1) // 2
    donor, receiver = tallies[1:1 + 2 * twos:2], tallies[2:2 + 2 * twos:2]
    slack = jnp.minimum(donor - 1, most - receiver)
    passed = jax.random.randint(jax.random.fold_in(rng, 1), (twos,), 0, 1 << 20) % (slack + 1)
    tallies = tallies.at[1:1 + 2 * twos:2].set(donor - passed).at[2:2 + 2 * twos:2].set(receiver + passed)
    return tallies[jax.random.permutation(jax.random.fold_in(rng, 2), count)]


def scatter_about(own_key, extent, scale, limit, pieces=(), held_as=jnp.bfloat16):
    loudness = block_scale(own_key, extent, pieces, -0.22, 0.18) if pieces else 1.0
    values = jax.random.normal(own_key, extent, jnp.float32) * scale * loudness
    return jnp.minimum(jnp.maximum(values, -limit), limit).astype(held_as)


def bell_draw_with(rng, extent, scale, reach, shards, heavy, kind=jnp.bfloat16):
    entries = scale * jax.random.normal(rng, extent, jnp.float32)
    if shards:
        entries = entries * block_scale(rng, extent, shards, -0.22, 0.18)
    return jnp.clip(strengthened(entries, jax.random.fold_in(rng, 3), *heavy), -reach, reach).astype(kind)


def setup_inputs(seed: int = 0) -> dict:
    arg_keys = jax.random.split(jax.random.key(seed), 10)
    return {
        "qkv_a": draw_qkv_a(jax.random.fold_in(arg_keys[9], 71), 0),
        "qkv_b": draw_qkv_b(jax.random.fold_in(arg_keys[9], 71), 0),
        "slot_grad_b": bell_draw_with(arg_keys[2], (N_SECTION, SLOT_ROWS, QW), 1.0, 16.0, ((0, 4), (1, 64)), (1, 2, 64, 4.0)),
        "adapter_down": scatter_about(arg_keys[3], (N_SECTION, QW, RANK), QW ** -0.5, 0.09375, ((0, 4),)),
        "adapter_up": scatter_about(arg_keys[4], (N_SECTION, RANK, QW), RANK ** -0.5, 0.75, ((0, 4),)),
        "lang_scale": jnp.clip(jnp.exp(jax.random.uniform(arg_keys[5], (LANGS,), jnp.float32, math.log(0.25), math.log(1.0))), 0.25, 1.0),
        "languages": place_ends(jax.random.randint(arg_keys[6], (2, TILES_ALL), 0, LANGS), jax.random.fold_in(arg_keys[6], 1), 0, LANGS - 1).astype(jnp.int32),
        "lengths": jax.vmap(lambda own: uneven(own, SEGS, TILE, MOST, 2))(jax.random.split(arg_keys[7], 2 * TILES_ALL)).reshape((2, TILES_ALL, SEGS)).astype(jnp.int32),
        "destination": draw_destination(jax.random.fold_in(arg_keys[9], 71), 0),
    }


def mix(form, left, right):
    return jnp.einsum(form, left.astype(jnp.float32), right.astype(jnp.float32))

def segment_mask(lens):
    ends = jnp.cumsum(lens, axis=-1).astype(jnp.int32)
    place = jnp.arange(TILE, dtype=jnp.int32)
    segment = lax.optimization_barrier(jnp.sum((place[None, :, None] >= ends[:, None, :]).astype(jnp.int32), axis=-1))
    causal = place[:, None] >= place[None, :]
    return (segment[:, :, None] == segment[:, None, :]) & causal[None]

def split_heads(joined):
    count = joined.shape[0]
    group = HEADS // KV
    queries = joined[:, :, :HEADS * HEAD_DIM].reshape(count, TILE, KV, group, HEAD_DIM)
    keys = joined[:, :, HEADS * HEAD_DIM:(HEADS + KV) * HEAD_DIM].reshape(count, TILE, KV, HEAD_DIM)
    values = joined[:, :, (HEADS + KV) * HEAD_DIM:].reshape(count, TILE, KV, HEAD_DIM)
    return (queries, keys, values)

def attend(joined, mask):
    count = joined.shape[0]
    queries, keys, values = split_heads(joined)
    scale = 1.0 / math.sqrt(HEAD_DIM)
    scores = mix('nqhgd,nkhd->nhgqk', queries, keys) * scale
    allowed = mask[:, None, None]
    masked = jnp.where(allowed, scores, -1e+30)
    top = lax.optimization_barrier(jnp.max(masked, axis=-1, keepdims=True))
    weights = jnp.where(allowed, jnp.exp(masked - top), 0.0)
    probs = weights / lax.optimization_barrier(jnp.sum(weights, axis=-1, keepdims=True))
    probs_low = probs.astype(jnp.bfloat16)
    attn = mix('nhgqk,nkhd->nqhgd', probs_low, values).astype(jnp.bfloat16)
    return (attn.reshape(count, TILE, HEADS * HEAD_DIM), probs, probs_low)

def adapt(attn, rate, down, up):
    width = HEADS * HEAD_DIM
    rows = attn.reshape(-1, width)
    low = jnp.dot(rows, down, preferred_element_type=jnp.float32).astype(jnp.bfloat16)
    lift = jnp.dot(low, up, preferred_element_type=jnp.float32).reshape(attn.shape)
    return (attn.astype(jnp.float32) + rate[:, None, None] * lift).astype(jnp.bfloat16)

def backward(joined, mask, grad_in, rate, down, up):
    count = joined.shape[0]
    group = HEADS // KV
    width = HEADS * HEAD_DIM
    scale = 1.0 / math.sqrt(HEAD_DIM)
    queries, keys, values = split_heads(joined)
    attn, probs, probs_low = attend(joined, mask)
    rows = attn.reshape(-1, width)
    low = jnp.dot(rows, down, preferred_element_type=jnp.float32).astype(jnp.bfloat16)
    scaled = (rate[:, None, None] * grad_in.astype(jnp.float32)).astype(jnp.bfloat16).reshape(-1, width)
    back_low = jnp.dot(scaled, up.T, preferred_element_type=jnp.float32).astype(jnp.bfloat16)
    grad_attn = (grad_in.reshape(-1, width).astype(jnp.float32) + jnp.dot(back_low, down.T, preferred_element_type=jnp.float32)).astype(jnp.bfloat16)
    grad_heads = grad_attn.reshape(count, TILE, KV, group, HEAD_DIM)
    attn_heads = attn.reshape(count, TILE, KV, group, HEAD_DIM)
    grad_probs = mix('nqhgd,nkhd->nhgqk', grad_heads, values)
    delta = lax.optimization_barrier(jnp.sum(grad_heads.astype(jnp.float32) * attn_heads.astype(jnp.float32), axis=-1))
    delta = jnp.transpose(delta, (0, 2, 3, 1))[..., None]
    grad_scores = (probs * (grad_probs - delta) * scale).astype(jnp.bfloat16)
    grad_queries = mix('nhgqk,nkhd->nqhgd', grad_scores, keys).astype(jnp.bfloat16)
    grad_keys = mix('nhgqk,nqhgd->nkhd', grad_scores, queries).astype(jnp.bfloat16)
    grad_values = mix('nhgqk,nqhgd->nkhd', probs_low, grad_heads).astype(jnp.bfloat16)
    grad_qkv = jnp.concatenate([grad_queries.reshape(count, TILE, -1), grad_keys.reshape(count, TILE, -1), grad_values.reshape(count, TILE, -1)], axis=-1)
    return (grad_qkv, rows, back_low, scaled, low)

def reference(qkv_a, qkv_b, slot_grad_b, adapter_down, adapter_up, lang_scale, languages, lengths, destination):
    tiles_all = N_DP * TILES
    width = HEADS * HEAD_DIM
    joined_width = qkv_a.shape[-1]
    table = jnp.arange(LANGS, dtype=jnp.int32)
    rates = lax.optimization_barrier(jnp.sum(jnp.where(languages[:, :, None] == table[None, None, :], lang_scale[None, None, :], 0.0), axis=-1))
    group = jnp.arange(N_DP, dtype=jnp.int32)
    offsets = jnp.arange(-1, TILES + 1, dtype=jnp.int32)
    source = group[:, None] * TILES + offsets[None, :]
    clipped = jnp.clip(source, 0, tiles_all - 1).reshape(-1).astype(jnp.int32)
    inside = ((source >= 0) & (source < tiles_all)).reshape(-1)
    owner = jnp.repeat(group, TILES + 2)
    live_a = inside & (destination[0][clipped] == owner)
    tile_ids = jnp.arange(tiles_all, dtype=jnp.int32)
    home_group = tile_ids // TILES
    home_place = tile_ids % TILES
    dest_b = destination[1]
    slot = jnp.where(dest_b == home_group, home_place + 1, jnp.where(dest_b < home_group, TILES + 1, 0))
    slot_row = (dest_b * (TILES + 2) + slot).astype(jnp.int32)
    mask_a = segment_mask(lengths[0]).reshape(N_DP, TILES, TILE, TILE)
    mask_b = segment_mask(lengths[1]).reshape(N_DP, TILES, TILE, TILE)
    rate_a = rates[0].reshape(N_DP, TILES)
    rate_b = rates[1].reshape(N_DP, TILES)
    forward_parts = []
    back_parts = []
    grad_parts = []
    for section in range(N_SECTION):
        down = adapter_down[section]
        up = adapter_up[section]
        joined_a = qkv_a[section].reshape(N_DP, TILES, TILE, joined_width)

        def forward_group(items):
            joined, mask, rate = items
            attn, probs, probs_low = attend(joined, mask)
            return adapt(attn, rate, down, up)
        result = lax.map(forward_group, (joined_a, mask_a, rate_a)).reshape(tiles_all, TILE, width)
        placed = jnp.where(live_a[:, None, None], result[clipped], jnp.zeros((), result.dtype))
        forward_parts.append(placed.reshape(-1, width))
        grad_slots = slot_grad_b[section].reshape(N_DP * (TILES + 2), TILE, width)
        grad_home = grad_slots[slot_row].reshape(N_DP, TILES, TILE, width)
        joined_b = qkv_b[section].reshape(N_DP, TILES, TILE, joined_width)

        def backward_group(items):
            joined, mask, grad_in, rate = items
            grad_qkv, rows, back_low, scaled, low = backward(joined, mask, grad_in, rate, down, up)
            terms = jnp.concatenate([mix('rq,rk->qk', rows, back_low), mix('rq,rk->qk', scaled, low)], axis=1)
            return (grad_qkv, terms)
        grad_qkv, terms = lax.map(backward_group, (joined_b, mask_b, grad_home, rate_b))
        back_parts.append(grad_qkv.reshape(-1, joined_width))
        grad_parts.append(lax.optimization_barrier(jnp.sum(terms, axis=0)))
    handed_forward = jnp.stack([jnp.zeros_like(forward_parts[0])] + forward_parts[:-1])
    handed_back = jnp.stack(back_parts[1:] + [jnp.zeros_like(back_parts[0])])
    adapter_grad = jnp.stack(grad_parts)
    return (handed_forward, handed_back, adapter_grad)
```

```python
import functools
import math

import jax
import jax.numpy as jnp
from jax import lax
from jax.experimental import pallas as pl
from jax.experimental.pallas import tpu as pltpu
from jax.sharding import PartitionSpec as P

HEADS = 32
KV = 4
GROUP = HEADS // KV
HEAD_DIM = 128
TILE = 128
SEGS = 8
RANK = 64
QW = HEADS * HEAD_DIM
KW = KV * HEAD_DIM
GW = GROUP * HEAD_DIM
SCALE = 1.0 / math.sqrt(HEAD_DIM)
AXES = ("section", "dp")
BF16 = jnp.bfloat16
F32 = jnp.float32


def dot(a, b, dims):
    return lax.dot_general(a, b, (dims, ((), ())), preferred_element_type=F32)


NN = ((1,), (0,))
NT = ((1,), (1,))
TN = ((0,), (0,))


def mask_bias(lens_ref, m, rank):
    shape = (TILE, TILE)
    row = lax.broadcasted_iota(jnp.int32, shape, 0)
    col = lax.broadcasted_iota(jnp.int32, shape, 1)
    seg_row = jnp.zeros(shape, jnp.int32)
    seg_col = jnp.zeros(shape, jnp.int32)
    end = jnp.int32(0)
    for k in range(SEGS):
        end = end + lens_ref[m, rank, k]
        seg_row = seg_row + (row >= end).astype(jnp.int32)
        seg_col = seg_col + (col >= end).astype(jnp.int32)
    allowed = (seg_row == seg_col) & (row >= col)
    return jnp.where(allowed, 0.0, -1e30).astype(F32)


def stacked(ref, base):
    return jnp.concatenate(
        [ref[:, base + h * HEAD_DIM : base + (h + 1) * HEAD_DIM] for h in range(GROUP)], axis=0
    )


def softmax(scores, bias):
    masked = scores + bias
    top = jnp.max(masked, axis=-1, keepdims=True)
    weights = jnp.exp2((masked - top) * (SCALE * math.log2(math.e)))
    return weights * (1.0 / jnp.sum(weights, axis=-1, keepdims=True))


def attend_group(j, qkv_ref, bias, probs_ref):
    keys = qkv_ref[:, QW + j * HEAD_DIM : QW + (j + 1) * HEAD_DIM]
    values = qkv_ref[:, QW + KW + j * HEAD_DIM : QW + KW + (j + 1) * HEAD_DIM]
    queries = stacked(qkv_ref, j * GW)
    probs_ref[...] = dot(queries, keys, NT)
    lows = []
    for h in range(GROUP):
        rows = slice(h * TILE, (h + 1) * TILE)
        probs = softmax(probs_ref[rows, :], bias)
        probs_ref[rows, :] = probs
        lows.append(probs.astype(BF16))
    probs_low = jnp.concatenate(lows, axis=0)
    attn = dot(probs_low, values, NN).astype(BF16)
    return queries, keys, values, probs_low, attn


def forward_kernel(rank_ref, lens_ref, langs_ref, table_ref, qkv_ref, down_ref, up_ref, out_ref, probs_ref):
    rank = rank_ref[0]
    rate = table_ref[langs_ref[0, rank]]
    bias = mask_bias(lens_ref, 0, rank)
    low = jnp.zeros((TILE, RANK), F32)
    for j in range(KV):
        attn = attend_group(j, qkv_ref, bias, probs_ref)[-1]
        for h in range(GROUP):
            cols = slice(j * GW + h * HEAD_DIM, j * GW + (h + 1) * HEAD_DIM)
            out_ref[:, cols] = attn[h * TILE : (h + 1) * TILE]
        low = low + dot(out_ref[:, j * GW : (j + 1) * GW], down_ref[j * GW : (j + 1) * GW, :], NN)
    low = low.astype(BF16)
    for c in range(0, QW, 512):
        lift = dot(low, up_ref[:, c : c + 512], NN)
        out_ref[:, c : c + 512] = (out_ref[:, c : c + 512].astype(F32) + rate * lift).astype(BF16)


def backward_kernel(
    rank_ref, lens_ref, langs_ref, dest_ref, table_ref, qkv_ref, left_ref, mid_ref, right_ref,
    down_ref, up_ref, grad_ref, terms_ref, probs_ref, attn_ref, scaled_ref, gattn_ref,
):
    rank = rank_ref[0]
    rate = table_ref[langs_ref[1, rank]]
    went = dest_ref[1, rank] - rank
    bias = mask_bias(lens_ref, 1, rank)
    back = jnp.zeros((TILE, RANK), F32)
    for c in range(0, QW, 512):
        cols = slice(c, c + 512)
        grad = jnp.where(
            went < 0, left_ref[:, cols], jnp.where(went > 0, right_ref[:, cols], mid_ref[:, cols])
        )
        gattn_ref[:, cols] = grad
        scaled = (rate * grad.astype(F32)).astype(BF16)
        scaled_ref[:, cols] = scaled
        back = back + dot(scaled, up_ref[:, cols], NT)
    back = back.astype(BF16)
    low = jnp.zeros((TILE, RANK), F32)
    for j in range(KV):
        block = slice(j * GW, (j + 1) * GW)
        gattn = gattn_ref[:, block].astype(F32) + dot(back, down_ref[block, :], NT)
        gattn_ref[:, block] = gattn.astype(BF16)
        queries, keys, values, probs_low, attn = attend_group(j, qkv_ref, bias, probs_ref)
        for h in range(GROUP):
            cols = slice(j * GW + h * HEAD_DIM, j * GW + (h + 1) * HEAD_DIM)
            attn_ref[:, cols] = attn[h * TILE : (h + 1) * TILE]
        low = low + dot(attn_ref[:, block], down_ref[block, :], NN)
        grads = stacked(gattn_ref, j * GW)
        grad_probs = dot(grads, values, NT)
        scores = []
        for h in range(GROUP):
            rows = slice(h * TILE, (h + 1) * TILE)
            probs = probs_ref[rows, :]
            weighed = probs * grad_probs[rows]
            delta = jnp.sum(weighed, axis=-1, keepdims=True)
            scores.append(((weighed - probs * delta) * SCALE).astype(BF16))
        grad_scores = jnp.concatenate(scores, axis=0)
        grad_queries = dot(grad_scores, keys, NN).astype(BF16)
        for h in range(GROUP):
            cols = slice(j * GW + h * HEAD_DIM, j * GW + (h + 1) * HEAD_DIM)
            grad_ref[:, cols] = grad_queries[h * TILE : (h + 1) * TILE]
        cols = slice(QW + j * HEAD_DIM, QW + (j + 1) * HEAD_DIM)
        grad_ref[:, cols] = dot(grad_scores, queries, TN).astype(BF16)
        cols = slice(QW + KW + j * HEAD_DIM, QW + KW + (j + 1) * HEAD_DIM)
        grad_ref[:, cols] = dot(probs_low, grads, TN).astype(BF16)
    low = low.astype(BF16)
    for c in range(0, QW, 512):
        cols = slice(c, c + 512)
        one = dot(attn_ref[:, cols], back, TN)
        two = dot(scaled_ref[:, cols], low, TN)
        terms_ref[cols, :] = jnp.concatenate([one, two], axis=1).astype(terms_ref.dtype)


SMEM = pl.BlockSpec(memory_space=pltpu.SMEM)
VMEM = pl.BlockSpec(memory_space=pltpu.VMEM)


def run_forward(rank, lengths, languages, table, qkv, down, up):
    return pl.pallas_call(
        forward_kernel,
        out_shape=jax.ShapeDtypeStruct((TILE, QW), BF16),
        in_specs=[SMEM] * 4 + [VMEM] * 3,
        out_specs=VMEM,
        scratch_shapes=[pltpu.VMEM((GROUP * TILE, TILE), F32)],
        compiler_params=pltpu.CompilerParams(vmem_limit_bytes=24 * 2**20),
        name="forward_tile",
    )(rank, lengths, languages, table, qkv, down, up)


def run_backward(rank, lengths, languages, dest, table, qkv, left, mid, right, down, up):
    return pl.pallas_call(
        backward_kernel,
        out_shape=(
            jax.ShapeDtypeStruct((TILE, QW + 2 * KW), BF16),
            jax.ShapeDtypeStruct((QW, 2 * RANK), BF16),
        ),
        in_specs=[SMEM] * 5 + [VMEM] * 6,
        out_specs=(VMEM, VMEM),
        scratch_shapes=[
            pltpu.VMEM((GROUP * TILE, TILE), F32),
            pltpu.VMEM((TILE, QW), BF16),
            pltpu.VMEM((TILE, QW), BF16),
            pltpu.VMEM((TILE, QW), BF16),
        ],
        compiler_params=pltpu.CompilerParams(vmem_limit_bytes=40 * 2**20),
        name="backward_tile",
    )(rank, lengths, languages, dest, table, qkv, left, mid, right, down, up)


def shift_dp(x, step):
    size = lax.axis_size("dp")
    return lax.ppermute(x, "dp", [(t, t + step) for t in range(size) if 0 <= t + step < size])


def shift_section(x, step):
    size = lax.axis_size("section")
    return lax.ppermute(
        x, "section", [(s, s + step) for s in range(size) if 0 <= s + step < size]
    )


def exchange(x, stride, count):
    size = lax.axis_size("dp")
    place = (lax.axis_index("dp") // stride) % count
    total = lax.dynamic_index_in_dim(x, place, 0, keepdims=False).astype(F32)
    for step in range(1, count):
        piece = lax.dynamic_index_in_dim(x, (place + step) % count, 0, keepdims=False)
        route = []
        for t in range(size):
            at = (t // stride) % count
            route.append((t, t + ((at + step) % count - at) * stride))
        total = total + lax.ppermute(piece, "dp", route).astype(F32)
    return total


def shards(
    qkv_a, qkv_b, slot_grad_b, adapter_down, adapter_up, lang_scale, languages, lengths, destination
):
    rank = lax.axis_index("dp")
    rank_word = jnp.reshape(rank.astype(jnp.int32), (1,))
    down, up = adapter_down[0], adapter_up[0]
    slots = slot_grad_b[0]
    from_left = shift_dp(slots[2 * TILE :], 1)
    from_right = shift_dp(slots[:TILE], -1)
    out = run_forward(rank_word, lengths, languages, lang_scale, qkv_a[0], down, up)
    hop = shift_section(out, 1)
    to_right = shift_dp(hop, 1)
    to_left = shift_dp(hop, -1)
    dest = destination[0]
    size = lax.axis_size("dp")
    zero = jnp.zeros((), BF16)
    slot0 = jnp.where(dest[jnp.maximum(rank - 1, 0)] == rank, to_right, zero)
    slot1 = jnp.where(dest[rank] == rank, hop, zero)
    slot2 = jnp.where(dest[jnp.minimum(rank + 1, size - 1)] == rank, to_left, zero)
    first, last = rank == 0, rank == size - 1
    slot0 = jnp.where(first, zero, slot0)
    slot2 = jnp.where(last, zero, slot2)
    handed_forward = jnp.concatenate([slot0, slot1, slot2], axis=0)[None]
    grad_qkv, terms = run_backward(
        rank_word, lengths, languages, destination, lang_scale, qkv_b[0],
        from_left, slots[TILE : 2 * TILE], from_right, down, up,
    )
    handed_back = shift_section(grad_qkv, -1)[None]
    terms = exchange(terms.reshape(4, 1024, 128), 16, 4).astype(BF16)
    terms = exchange(terms.reshape(4, 256, 128), 4, 4).astype(BF16)
    terms = exchange(terms.reshape(4, 64, 128), 1, 4)
    return (handed_forward, handed_back, terms[None])


def solution(mesh):
    return jax.shard_map(
        shards,
        mesh=mesh,
        in_specs=(
            P("section", "dp", None),
            P("section", "dp", None),
            P("section", "dp", None),
            P("section", None, None),
            P("section", None, None),
            P(),
            P(),
            P(),
            P(),
        ),
        out_specs=(P("section", "dp", None), P("section", "dp", None), P("section", "dp", None)),
        check_vma=False,
    )
```

```python
import functools
import math

import jax
import jax.numpy as jnp
from jax import lax
from jax.experimental import pallas as pl
from jax.experimental.pallas import tpu as pltpu
from jax.sharding import PartitionSpec as P

HEADS = 32
KV = 4
GROUP = HEADS // KV
HEAD_DIM = 128
TILE = 128
SEGS = 8
RANK = 64
QW = HEADS * HEAD_DIM
KW = KV * HEAD_DIM
GW = GROUP * HEAD_DIM
SCALE = 1.0 / math.sqrt(HEAD_DIM)
AXES = ("section", "dp")
BF16 = jnp.bfloat16
F32 = jnp.float32


def dot(a, b, dims):
    return lax.dot_general(a, b, (dims, ((), ())), preferred_element_type=F32)


NN = ((1,), (0,))
NT = ((1,), (1,))
TN = ((0,), (0,))


def mask_bias(lens_ref, m, rank):
    shape = (TILE, TILE)
    row = lax.broadcasted_iota(jnp.int32, shape, 0)
    col = lax.broadcasted_iota(jnp.int32, shape, 1)
    seg_row = jnp.zeros(shape, jnp.int32)
    seg_col = jnp.zeros(shape, jnp.int32)
    end = jnp.int32(0)
    for k in range(SEGS):
        end = end + lens_ref[m, rank, k]
        seg_row = seg_row + (row >= end).astype(jnp.int32)
        seg_col = seg_col + (col >= end).astype(jnp.int32)
    allowed = (seg_row == seg_col) & (row >= col)
    return jnp.where(allowed, 0.0, -1e30).astype(F32)


def stacked(ref, base):
    return jnp.concatenate(
        [ref[:, base + h * HEAD_DIM : base + (h + 1) * HEAD_DIM] for h in range(GROUP)], axis=0
    )


def softmax(scores, bias):
    masked = scores + bias
    top = jnp.max(masked, axis=-1, keepdims=True)
    weights = jnp.exp2((masked - top) * (SCALE * math.log2(math.e)))
    return weights * (1.0 / jnp.sum(weights, axis=-1, keepdims=True))


def attend_group(j, qkv_ref, bias, probs_ref):
    keys = qkv_ref[:, QW + j * HEAD_DIM : QW + (j + 1) * HEAD_DIM]
    values = qkv_ref[:, QW + KW + j * HEAD_DIM : QW + KW + (j + 1) * HEAD_DIM]
    queries = stacked(qkv_ref, j * GW)
    probs_ref[...] = dot(queries, keys, NT)
    lows = []
    for h in range(GROUP):
        rows = slice(h * TILE, (h + 1) * TILE)
        probs = softmax(probs_ref[rows, :], bias)
        probs_ref[rows, :] = probs
        lows.append(probs.astype(BF16))
    probs_low = jnp.concatenate(lows, axis=0)
    attn = dot(probs_low, values, NN).astype(BF16)
    return queries, keys, values, probs_low, attn


def forward_kernel(rank_ref, lens_ref, langs_ref, table_ref, qkv_ref, down_ref, up_ref, out_ref, probs_ref):
    rank = rank_ref[0]
    rate = table_ref[langs_ref[0, rank]]
    bias = mask_bias(lens_ref, 0, rank)
    low = jnp.zeros((TILE, RANK), F32)
    for j in range(KV):
        attn = attend_group(j, qkv_ref, bias, probs_ref)[-1]
        for h in range(GROUP):
            cols = slice(j * GW + h * HEAD_DIM, j * GW + (h + 1) * HEAD_DIM)
            out_ref[:, cols] = attn[h * TILE : (h + 1) * TILE]
        low = low + dot(out_ref[:, j * GW : (j + 1) * GW], down_ref[j * GW : (j + 1) * GW, :], NN)
    low = low.astype(BF16)
    for c in range(0, QW, 512):
        lift = dot(low, up_ref[:, c : c + 512], NN)
        out_ref[:, c : c + 512] = (out_ref[:, c : c + 512].astype(F32) + rate * lift).astype(BF16)


def prepare_kernel(
    rank_ref, lens_ref, langs_ref, dest_ref, table_ref, qkv_ref, slots_ref, down_ref, up_ref,
    probs_ref, attn_ref, scaled_ref, left_ref, own_ref, right_ref,
):
    rank = rank_ref[0]
    tiles = lens_ref.shape[1]
    bias = mask_bias(lens_ref, 1, rank)
    low = jnp.zeros((TILE, RANK), F32)
    for j in range(KV):
        block = slice(j * GW, (j + 1) * GW)
        attn = attend_group(j, qkv_ref, bias, probs_ref.at[block, :])[-1]
        for h in range(GROUP):
            cols = slice(j * GW + h * HEAD_DIM, j * GW + (h + 1) * HEAD_DIM)
            attn_ref[:, cols] = attn[h * TILE : (h + 1) * TILE]
        low = low + dot(attn_ref[:, block], down_ref[block, :], NN)
    for k, out_ref in enumerate((left_ref, own_ref, right_ref)):
        tile = rank + (k - 1)
        near = jnp.clip(tile, 0, tiles - 1)
        live = (tile == near) & (dest_ref[1, near] == rank)
        rate = jnp.where(live, table_ref[langs_ref[1, near]], 0.0)
        rows = slice(k * TILE, (k + 1) * TILE)
        back = jnp.zeros((TILE, RANK), F32)
        for c in range(0, QW, 512):
            cols = slice(c, c + 512)
            scaled = (rate * slots_ref[rows, cols].astype(F32)).astype(BF16)
            scaled_ref[rows, cols] = scaled
            back = back + dot(scaled, up_ref[:, cols], NT)
        out_ref[...] = jnp.concatenate([low, back], axis=1).astype(BF16)


def terms_kernel(
    rank_ref, dest_ref, attn_ref, scaled_ref, left_ref, own_ref, right_ref, terms_ref, back_ref
):
    rank = rank_ref[0]
    went = dest_ref[1, rank] - rank
    back = jnp.where(went < 0, left_ref[...], jnp.where(went > 0, right_ref[...], own_ref[...]))
    back_ref[...] = back
    lows = jnp.concatenate([left_ref[...], own_ref[...], right_ref[...]], axis=0)
    for c in range(0, QW, 512):
        cols = slice(c, c + 512)
        one = dot(attn_ref[:, cols], back, TN)
        two = dot(scaled_ref[:, cols], lows, TN)
        terms = jnp.concatenate([one[:, RANK:], two[:, :RANK]], axis=1)
        terms_ref[cols, :] = terms.astype(terms_ref.dtype)


def backward_kernel(
    rank_ref, dest_ref, qkv_ref, left_ref, mid_ref, right_ref, back_ref, probs_ref, down_ref,
    grad_ref, gattn_ref,
):
    rank = rank_ref[0]
    went = dest_ref[1, rank] - rank
    back = back_ref[...][:, RANK:]
    for j in range(KV):
        block = slice(j * GW, (j + 1) * GW)
        grad = jnp.where(
            went < 0, left_ref[:, block], jnp.where(went > 0, right_ref[:, block], mid_ref[:, block])
        )
        gattn = grad.astype(F32) + dot(back, down_ref[block, :], NT)
        gattn_ref[:, block] = gattn.astype(BF16)
        queries = stacked(qkv_ref, j * GW)
        keys = qkv_ref[:, QW + j * HEAD_DIM : QW + (j + 1) * HEAD_DIM]
        values = qkv_ref[:, QW + KW + j * HEAD_DIM : QW + KW + (j + 1) * HEAD_DIM]
        grads = stacked(gattn_ref, j * GW)
        grad_probs = dot(grads, values, NT)
        lows, scores = [], []
        for h in range(GROUP):
            probs = probs_ref[j * GW + h * TILE : j * GW + (h + 1) * TILE, :]
            lows.append(probs.astype(BF16))
            weighed = probs * grad_probs[h * TILE : (h + 1) * TILE]
            delta = jnp.sum(weighed, axis=-1, keepdims=True)
            scores.append(((weighed - probs * delta) * SCALE).astype(BF16))
        probs_low = jnp.concatenate(lows, axis=0)
        grad_scores = jnp.concatenate(scores, axis=0)
        grad_queries = dot(grad_scores, keys, NN).astype(BF16)
        for h in range(GROUP):
            cols = slice(j * GW + h * HEAD_DIM, j * GW + (h + 1) * HEAD_DIM)
            grad_ref[:, cols] = grad_queries[h * TILE : (h + 1) * TILE]
        cols = slice(QW + j * HEAD_DIM, QW + (j + 1) * HEAD_DIM)
        grad_ref[:, cols] = dot(grad_scores, queries, TN).astype(BF16)
        cols = slice(QW + KW + j * HEAD_DIM, QW + KW + (j + 1) * HEAD_DIM)
        grad_ref[:, cols] = dot(probs_low, grads, TN).astype(BF16)


SMEM = pl.BlockSpec(memory_space=pltpu.SMEM)
VMEM = pl.BlockSpec(memory_space=pltpu.VMEM)


def run_forward(rank, lengths, languages, table, qkv, down, up):
    return pl.pallas_call(
        forward_kernel,
        out_shape=jax.ShapeDtypeStruct((TILE, QW), BF16),
        in_specs=[SMEM] * 4 + [VMEM] * 3,
        out_specs=VMEM,
        scratch_shapes=[pltpu.VMEM((GROUP * TILE, TILE), F32)],
        compiler_params=pltpu.CompilerParams(vmem_limit_bytes=24 * 2**20),
        name="forward_tile",
    )(rank, lengths, languages, table, qkv, down, up)


def run_prepare(rank, lengths, languages, dest, table, qkv, slots, down, up):
    message = jax.ShapeDtypeStruct((TILE, 2 * RANK), BF16)
    return pl.pallas_call(
        prepare_kernel,
        out_shape=(
            jax.ShapeDtypeStruct((QW, TILE), F32),
            jax.ShapeDtypeStruct((TILE, QW), BF16),
            jax.ShapeDtypeStruct((3 * TILE, QW), BF16),
            message,
            message,
            message,
        ),
        in_specs=[SMEM] * 5 + [VMEM] * 4,
        out_specs=(VMEM,) * 6,
        compiler_params=pltpu.CompilerParams(vmem_limit_bytes=40 * 2**20),
        name="prepare_tile",
    )(rank, lengths, languages, dest, table, qkv, slots, down, up)


def run_terms(rank, dest, attn, scaled, left, own, right):
    return pl.pallas_call(
        terms_kernel,
        out_shape=(
            jax.ShapeDtypeStruct((QW, 2 * RANK), BF16),
            jax.ShapeDtypeStruct((TILE, 2 * RANK), BF16),
        ),
        in_specs=[SMEM] * 2 + [VMEM] * 5,
        out_specs=(VMEM, VMEM),
        compiler_params=pltpu.CompilerParams(vmem_limit_bytes=24 * 2**20),
        name="adapter_terms",
    )(rank, dest, attn, scaled, left, own, right)


def run_backward(rank, dest, qkv, left, mid, right, back, probs, down):
    return pl.pallas_call(
        backward_kernel,
        out_shape=jax.ShapeDtypeStruct((TILE, QW + 2 * KW), BF16),
        in_specs=[SMEM] * 2 + [VMEM] * 7,
        out_specs=VMEM,
        scratch_shapes=[pltpu.VMEM((TILE, QW), BF16)],
        compiler_params=pltpu.CompilerParams(vmem_limit_bytes=40 * 2**20),
        name="backward_tile",
    )(rank, dest, qkv, left, mid, right, back, probs, down)


def sections():
    return lax.axis_size("section")


def shift(x, moves):
    size = lax.axis_size("dp")
    route = []
    for s_list, up, step, keep in moves:
        for s in s_list:
            for t in range(size):
                if 0 <= s + up < sections() and 0 <= t + step < size and keep(t):
                    route.append((s * size + t, (s + up) * size + t + step))
    return lax.ppermute(x, AXES, route)


def anywhere(t):
    return True


def exchange(x, stride, count):
    size = lax.axis_size("dp")
    place = (lax.axis_index("dp") // stride) % count
    total = lax.dynamic_index_in_dim(x, place, 0, keepdims=False).astype(F32)
    for step in range(1, count):
        piece = lax.dynamic_index_in_dim(x, (place + step) % count, 0, keepdims=False)
        route = []
        for t in range(size):
            at = (t // stride) % count
            route.append((t, t + ((at + step) % count - at) * stride))
        total = total + lax.ppermute(piece, "dp", route).astype(F32)
    return total


def shards(
    qkv_a, qkv_b, slot_grad_b, adapter_down, adapter_up, lang_scale, languages, lengths, destination
):
    rank = lax.axis_index("dp")
    size = lax.axis_size("dp")
    rank_word = jnp.reshape(rank.astype(jnp.int32), (1,))
    down, up = adapter_down[0], adapter_up[0]
    slots = slot_grad_b[0]
    every = range(sections())
    later = range(1, sections())
    from_left = shift(slots[2 * TILE :], [(later, 0, 1, anywhere)])
    from_right = shift(slots[:TILE], [(later, 0, -1, anywhere)])
    out = run_forward(rank_word, lengths, languages, lang_scale, qkv_a[0], down, up)
    hop = shift(out, [(every, 1, 0, anywhere)])
    probs, attn, scaled, to_left, own, to_right = run_prepare(
        rank_word, lengths, languages, destination, lang_scale, qkv_b[0], slots, down, up
    )
    left = shift(to_right, [(every, 0, 1, anywhere)])
    right = shift(to_left, [(every, 0, -1, anywhere)])
    terms, back = run_terms(rank_word, destination, attn, scaled, left, own, right)
    terms = exchange(terms.reshape(4, 1024, 128), 16, 4).astype(BF16)
    terms = exchange(terms.reshape(4, 256, 128), 4, 4).astype(BF16)
    terms = exchange(terms.reshape(4, 64, 128), 1, 4)
    terms, back, hop = lax.optimization_barrier((terms, back, hop))
    grad_qkv = run_backward(
        rank_word, destination, qkv_b[0], from_left, slots[TILE : 2 * TILE], from_right, back,
        probs, down,
    )
    handed_back = shift(grad_qkv, [(every, -1, 0, anywhere)])[None]
    before = shift(hop, [(later, 0, 1, anywhere)])
    after = shift(hop, [(later, 0, -1, anywhere)])
    dest = destination[0]
    zero = jnp.zeros((), BF16)
    slot0 = jnp.where((dest[jnp.maximum(rank - 1, 0)] == rank) & (rank > 0), before, zero)
    slot1 = jnp.where(dest[rank] == rank, hop, zero)
    slot2 = jnp.where(
        (dest[jnp.minimum(rank + 1, size - 1)] == rank) & (rank < size - 1), after, zero
    )
    handed_forward = jnp.concatenate([slot0, slot1, slot2], axis=0)[None]
    return (handed_forward, handed_back, terms[None])


def solution(mesh):
    return jax.shard_map(
        shards,
        mesh=mesh,
        in_specs=(
            P("section", "dp", None),
            P("section", "dp", None),
            P("section", "dp", None),
            P("section", None, None),
            P("section", None, None),
            P(),
            P(),
            P(),
            P(),
        ),
        out_specs=(P("section", "dp", None), P("section", "dp", None), P("section", "dp", None)),
        check_vma=False,
    )
```

```python
import functools
import math

import jax
import jax.numpy as jnp
from jax import lax
from jax.experimental import pallas as pl
from jax.experimental.pallas import tpu as pltpu
from jax.sharding import PartitionSpec as P

HEADS = 32
KV = 4
GROUP = HEADS // KV
HEAD_DIM = 128
TILE = 128
SEGS = 8
RANK = 64
QW = HEADS * HEAD_DIM
KW = KV * HEAD_DIM
GW = GROUP * HEAD_DIM
SCALE = 1.0 / math.sqrt(HEAD_DIM)
HALF = QW // 2
AXES = ("section", "dp")
BF16 = jnp.bfloat16
F32 = jnp.float32


def dot(a, b, dims):
    return lax.dot_general(a, b, (dims, ((), ())), preferred_element_type=F32)


NN = ((1,), (0,))
NT = ((1,), (1,))
TN = ((0,), (0,))


def mask_bias(lens_ref, m, rank):
    shape = (TILE, TILE)
    row = lax.broadcasted_iota(jnp.int32, shape, 0)
    col = lax.broadcasted_iota(jnp.int32, shape, 1)
    seg_row = jnp.zeros(shape, jnp.int32)
    seg_col = jnp.zeros(shape, jnp.int32)
    end = jnp.int32(0)
    for k in range(SEGS):
        end = end + lens_ref[m, rank, k]
        seg_row = seg_row + (row >= end).astype(jnp.int32)
        seg_col = seg_col + (col >= end).astype(jnp.int32)
    allowed = (seg_row == seg_col) & (row >= col)
    return jnp.where(allowed, 0.0, -1e30).astype(F32)


def stacked(ref, base):
    return jnp.concatenate(
        [ref[:, base + h * HEAD_DIM : base + (h + 1) * HEAD_DIM] for h in range(GROUP)], axis=0
    )


def softmax(scores, bias):
    masked = scores + bias
    top = jnp.max(masked, axis=-1, keepdims=True)
    weights = jnp.exp2((masked - top) * (SCALE * math.log2(math.e)))
    return weights * (1.0 / jnp.sum(weights, axis=-1, keepdims=True))


def attend_group(j, qkv_ref, bias, probs_ref):
    keys = qkv_ref[:, QW + j * HEAD_DIM : QW + (j + 1) * HEAD_DIM]
    values = qkv_ref[:, QW + KW + j * HEAD_DIM : QW + KW + (j + 1) * HEAD_DIM]
    queries = stacked(qkv_ref, j * GW)
    probs_ref[...] = dot(queries, keys, NT)
    lows = []
    for h in range(GROUP):
        rows = slice(h * TILE, (h + 1) * TILE)
        probs = softmax(probs_ref[rows, :], bias)
        probs_ref[rows, :] = probs
        lows.append(probs.astype(BF16))
    probs_low = jnp.concatenate(lows, axis=0)
    attn = dot(probs_low, values, NN).astype(BF16)
    return queries, keys, values, probs_low, attn


def forward_kernel(rank_ref, lens_ref, langs_ref, table_ref, qkv_ref, down_ref, up_ref, out_ref, probs_ref):
    rank = rank_ref[0]
    rate = table_ref[langs_ref[0, rank]]
    bias = mask_bias(lens_ref, 0, rank)
    low = jnp.zeros((TILE, RANK), F32)
    for j in range(KV):
        attn = attend_group(j, qkv_ref, bias, probs_ref)[-1]
        for h in range(GROUP):
            cols = slice(j * GW + h * HEAD_DIM, j * GW + (h + 1) * HEAD_DIM)
            out_ref[:, cols] = attn[h * TILE : (h + 1) * TILE]
        low = low + dot(out_ref[:, j * GW : (j + 1) * GW], down_ref[j * GW : (j + 1) * GW, :], NN)
    low = low.astype(BF16)
    for c in range(0, QW, 512):
        lift = dot(low, up_ref[:, c : c + 512], NN)
        out_ref[:, c : c + 512] = (out_ref[:, c : c + 512].astype(F32) + rate * lift).astype(BF16)


def prepare_kernel(
    rank_ref, lens_ref, langs_ref, dest_ref, table_ref, qkv_ref, slots_ref, down_ref, up_ref,
    probs_ref, attn_ref, scaled_ref, left_ref, own_ref, right_ref,
):
    rank = rank_ref[0]
    tiles = lens_ref.shape[1]
    bias = mask_bias(lens_ref, 1, rank)
    low = jnp.zeros((TILE, RANK), F32)
    for j in range(KV):
        block = slice(j * GW, (j + 1) * GW)
        attn = attend_group(j, qkv_ref, bias, probs_ref.at[block, :])[-1]
        for h in range(GROUP):
            cols = slice(j * GW + h * HEAD_DIM, j * GW + (h + 1) * HEAD_DIM)
            attn_ref[:, cols] = attn[h * TILE : (h + 1) * TILE]
        low = low + dot(attn_ref[:, block], down_ref[block, :], NN)
    for k, out_ref in enumerate((left_ref, own_ref, right_ref)):
        tile = rank + (k - 1)
        near = jnp.clip(tile, 0, tiles - 1)
        live = (tile == near) & (dest_ref[1, near] == rank)
        rate = jnp.where(live, table_ref[langs_ref[1, near]], 0.0)
        rows = slice(k * TILE, (k + 1) * TILE)
        back = jnp.zeros((TILE, RANK), F32)
        for c in range(0, QW, 512):
            cols = slice(c, c + 512)
            scaled = (rate * slots_ref[rows, cols].astype(F32)).astype(BF16)
            scaled_ref[rows, cols] = scaled
            back = back + dot(scaled, up_ref[:, cols], NT)
        out_ref[...] = jnp.concatenate([low, back], axis=1).astype(BF16)


def terms_kernel(
    rank_ref, dest_ref, attn_ref, scaled_ref, left_ref, own_ref, right_ref, terms_ref, back_ref
):
    rank = rank_ref[0]
    went = dest_ref[1, rank] - rank
    back = jnp.where(went < 0, left_ref[...], jnp.where(went > 0, right_ref[...], own_ref[...]))
    back_ref[...] = back
    lows = jnp.concatenate([left_ref[...], own_ref[...], right_ref[...]], axis=0)
    for c in range(0, QW, 512):
        cols = slice(c, c + 512)
        one = dot(attn_ref[:, cols], back, TN)
        two = dot(scaled_ref[:, cols], lows, TN)
        terms = jnp.concatenate([one[:, RANK:], two[:, :RANK]], axis=1)
        terms_ref[cols, :] = terms.astype(terms_ref.dtype)


def backward_kernel(
    rank_ref, dest_ref, qkv_ref, left_a_ref, left_b_ref, mid_ref, right_a_ref, right_b_ref, back_ref,
    probs_ref, down_ref, grad_ref, gattn_ref,
):
    rank = rank_ref[0]
    went = dest_ref[1, rank] - rank
    back = back_ref[...][:, RANK:]
    for j in range(KV):
        block = slice(j * GW, (j + 1) * GW)
        left_ref, right_ref = ((left_a_ref, right_a_ref), (left_b_ref, right_b_ref))[2 * j // KV]
        part = slice(j * GW % HALF, j * GW % HALF + GW)
        grad = jnp.where(
            went < 0, left_ref[:, part], jnp.where(went > 0, right_ref[:, part], mid_ref[:, block])
        )
        gattn = grad.astype(F32) + dot(back, down_ref[block, :], NT)
        gattn_ref[:, block] = gattn.astype(BF16)
        queries = stacked(qkv_ref, j * GW)
        keys = qkv_ref[:, QW + j * HEAD_DIM : QW + (j + 1) * HEAD_DIM]
        values = qkv_ref[:, QW + KW + j * HEAD_DIM : QW + KW + (j + 1) * HEAD_DIM]
        grads = stacked(gattn_ref, j * GW)
        grad_probs = dot(grads, values, NT)
        lows, scores = [], []
        for h in range(GROUP):
            probs = probs_ref[j * GW + h * TILE : j * GW + (h + 1) * TILE, :]
            lows.append(probs.astype(BF16))
            weighed = probs * grad_probs[h * TILE : (h + 1) * TILE]
            delta = jnp.sum(weighed, axis=-1, keepdims=True)
            scores.append(((weighed - probs * delta) * SCALE).astype(BF16))
        probs_low = jnp.concatenate(lows, axis=0)
        grad_scores = jnp.concatenate(scores, axis=0)
        grad_queries = dot(grad_scores, keys, NN).astype(BF16)
        for h in range(GROUP):
            cols = slice(j * GW + h * HEAD_DIM, j * GW + (h + 1) * HEAD_DIM)
            grad_ref[:, cols] = grad_queries[h * TILE : (h + 1) * TILE]
        cols = slice(QW + j * HEAD_DIM, QW + (j + 1) * HEAD_DIM)
        grad_ref[:, cols] = dot(grad_scores, queries, TN).astype(BF16)
        cols = slice(QW + KW + j * HEAD_DIM, QW + KW + (j + 1) * HEAD_DIM)
        grad_ref[:, cols] = dot(probs_low, grads, TN).astype(BF16)


COST = pl.CostEstimate(flops=2**20, bytes_accessed=2**20, transcendentals=0)
SMEM = pl.BlockSpec(memory_space=pltpu.SMEM)
VMEM = pl.BlockSpec(memory_space=pltpu.VMEM)


def run_forward(rank, lengths, languages, table, qkv, down, up):
    return pl.pallas_call(
        forward_kernel,
        out_shape=jax.ShapeDtypeStruct((TILE, QW), BF16),
        in_specs=[SMEM] * 4 + [VMEM] * 3,
        out_specs=VMEM,
        scratch_shapes=[pltpu.VMEM((GROUP * TILE, TILE), F32)],
        compiler_params=pltpu.CompilerParams(vmem_limit_bytes=24 * 2**20),
        cost_estimate=COST,
        name="forward_tile",
    )(rank, lengths, languages, table, qkv, down, up)


def run_prepare(rank, lengths, languages, dest, table, qkv, slots, down, up):
    message = jax.ShapeDtypeStruct((TILE, 2 * RANK), BF16)
    return pl.pallas_call(
        prepare_kernel,
        out_shape=(
            jax.ShapeDtypeStruct((QW, TILE), F32),
            jax.ShapeDtypeStruct((TILE, QW), BF16),
            jax.ShapeDtypeStruct((3 * TILE, QW), BF16),
            message,
            message,
            message,
        ),
        in_specs=[SMEM] * 5 + [VMEM] * 4,
        out_specs=(VMEM,) * 6,
        compiler_params=pltpu.CompilerParams(vmem_limit_bytes=40 * 2**20),
        cost_estimate=COST,
        name="prepare_tile",
    )(rank, lengths, languages, dest, table, qkv, slots, down, up)


def run_terms(rank, dest, attn, scaled, left, own, right):
    return pl.pallas_call(
        terms_kernel,
        out_shape=(
            jax.ShapeDtypeStruct((QW, 2 * RANK), BF16),
            jax.ShapeDtypeStruct((TILE, 2 * RANK), BF16),
        ),
        in_specs=[SMEM] * 2 + [VMEM] * 5,
        out_specs=(VMEM, VMEM),
        compiler_params=pltpu.CompilerParams(vmem_limit_bytes=24 * 2**20),
        cost_estimate=COST,
        name="adapter_terms",
    )(rank, dest, attn, scaled, left, own, right)


def run_backward(rank, dest, qkv, left, mid, right, back, probs, down):
    return pl.pallas_call(
        backward_kernel,
        out_shape=jax.ShapeDtypeStruct((TILE, QW + 2 * KW), BF16),
        in_specs=[SMEM] * 2 + [VMEM] * 9,
        out_specs=VMEM,
        scratch_shapes=[pltpu.VMEM((TILE, QW), BF16)],
        compiler_params=pltpu.CompilerParams(vmem_limit_bytes=40 * 2**20),
        cost_estimate=COST,
        name="backward_tile",
    )(rank, dest, qkv, *left, mid, *right, back, probs, down)


def sections():
    return lax.axis_size("section")


def shift(x, moves):
    size = lax.axis_size("dp")
    route = []
    for s_list, up, step, keep in moves:
        for s in s_list:
            for t in range(size):
                if 0 <= s + up < sections() and 0 <= t + step < size and keep(t):
                    route.append((s * size + t, (s + up) * size + t + step))
    return lax.ppermute(x, AXES, route)


def anywhere(t):
    return True


def exchange(x, stride, count):
    size = lax.axis_size("dp")
    place = (lax.axis_index("dp") // stride) % count
    total = lax.dynamic_index_in_dim(x, place, 0, keepdims=False)
    for step in range(1, count):
        piece = lax.dynamic_index_in_dim(x, (place + step) % count, 0, keepdims=False)
        route = []
        for t in range(size):
            at = (t // stride) % count
            route.append((t, t + ((at + step) % count - at) * stride))
        total = total + lax.ppermute(piece, "dp", route)
    return total


def shards(
    qkv_a, qkv_b, slot_grad_b, adapter_down, adapter_up, lang_scale, languages, lengths, destination
):
    rank = lax.axis_index("dp")
    size = lax.axis_size("dp")
    rank_word = jnp.reshape(rank.astype(jnp.int32), (1,))
    down, up = adapter_down[0], adapter_up[0]
    slots = slot_grad_b[0]
    every = range(sections())
    later = range(1, sections())
    first, second = slice(0, HALF), slice(HALF, QW)
    to_up, to_down = slots[2 * TILE :], slots[:TILE]
    left_a = shift(to_up[:, first], [(later, 0, 1, anywhere)])
    right_a = shift(to_down[:, first], [(later, 0, -1, anywhere)])
    left_b = shift(to_up[:, second], [(later, 0, 1, anywhere)])
    right_b = shift(to_down[:, second], [(later, 0, -1, anywhere)])
    out = run_forward(rank_word, lengths, languages, lang_scale, qkv_a[0], down, up)
    hop = shift(out, [(every, 1, 0, anywhere)])
    probs, attn, scaled, to_left, own, to_right = run_prepare(
        rank_word, lengths, languages, destination, lang_scale, qkv_b[0], slots, down, up
    )
    left = shift(to_right, [(every, 0, 1, anywhere)])
    right = shift(to_left, [(every, 0, -1, anywhere)])
    terms, back = run_terms(rank_word, destination, attn, scaled, left, own, right)
    terms, left_a, right_a = lax.optimization_barrier((terms, left_a, right_a))
    planes = [[4 * k + z for k in range(size // 4)] for z in range(4)]
    terms = lax.all_to_all(
        terms.reshape(size // 4, 256, 128), "dp", 0, 0, axis_index_groups=planes, tiled=True
    )
    terms = jnp.sum(terms.astype(F32), axis=0)
    terms, back, hop = lax.optimization_barrier((terms, back, hop))
    grad_qkv = run_backward(
        rank_word, destination, qkv_b[0], (left_a, left_b), slots[TILE : 2 * TILE],
        (right_a, right_b), back, probs, down,
    )
    terms = exchange(terms.reshape(4, 64, 128), 1, 4)
    handed_back = shift(grad_qkv, [(every, -1, 0, anywhere)])[None]
    before = shift(hop, [(later, 0, 1, anywhere)])
    after = shift(hop, [(later, 0, -1, anywhere)])
    dest = destination[0]
    zero = jnp.zeros((), BF16)
    slot0 = jnp.where((dest[jnp.maximum(rank - 1, 0)] == rank) & (rank > 0), before, zero)
    slot1 = jnp.where(dest[rank] == rank, hop, zero)
    slot2 = jnp.where(
        (dest[jnp.minimum(rank + 1, size - 1)] == rank) & (rank < size - 1), after, zero
    )
    handed_forward = jnp.concatenate([slot0, slot1, slot2], axis=0)[None]
    return (handed_forward, handed_back, terms[None])


def solution(mesh):
    return jax.shard_map(
        shards,
        mesh=mesh,
        in_specs=(
            P("section", "dp", None),
            P("section", "dp", None),
            P("section", "dp", None),
            P("section", None, None),
            P("section", None, None),
            P(),
            P(),
            P(),
            P(),
        ),
        out_specs=(P("section", "dp", None), P("section", "dp", None), P("section", "dp", None)),
        check_vma=False,
    )
```

```python
import functools
import math

import jax
import jax.numpy as jnp
from jax import lax
from jax.experimental import pallas as pl
from jax.experimental.pallas import tpu as pltpu
from jax.sharding import PartitionSpec as P

HEADS = 32
KV = 4
GROUP = HEADS // KV
HEAD_DIM = 128
TILE = 128
SEGS = 8
RANK = 64
QW = HEADS * HEAD_DIM
KW = KV * HEAD_DIM
GW = GROUP * HEAD_DIM
SCALE = 1.0 / math.sqrt(HEAD_DIM)
AXES = ("section", "dp")
BF16 = jnp.bfloat16
F32 = jnp.float32


def dot(a, b, dims):
    return lax.dot_general(a, b, (dims, ((), ())), preferred_element_type=F32)


NN = ((1,), (0,))
NT = ((1,), (1,))
TN = ((0,), (0,))


def mask_bias(lens_ref, m, rank):
    shape = (TILE, TILE)
    row = lax.broadcasted_iota(jnp.int32, shape, 0)
    col = lax.broadcasted_iota(jnp.int32, shape, 1)
    seg_row = jnp.zeros(shape, jnp.int32)
    seg_col = jnp.zeros(shape, jnp.int32)
    end = jnp.int32(0)
    for k in range(SEGS):
        end = end + lens_ref[m, rank, k]
        seg_row = seg_row + (row >= end).astype(jnp.int32)
        seg_col = seg_col + (col >= end).astype(jnp.int32)
    allowed = (seg_row == seg_col) & (row >= col)
    return jnp.where(allowed, 0.0, -1e30).astype(F32)


def stacked(ref, base):
    return jnp.concatenate(
        [ref[:, base + h * HEAD_DIM : base + (h + 1) * HEAD_DIM] for h in range(GROUP)], axis=0
    )


def softmax(scores, bias):
    masked = scores + bias
    top = jnp.max(masked, axis=-1, keepdims=True)
    weights = jnp.exp2((masked - top) * (SCALE * math.log2(math.e)))
    return weights * (1.0 / jnp.sum(weights, axis=-1, keepdims=True))


def attend_group(j, qkv_ref, bias, probs_ref):
    keys = qkv_ref[:, QW + j * HEAD_DIM : QW + (j + 1) * HEAD_DIM]
    values = qkv_ref[:, QW + KW + j * HEAD_DIM : QW + KW + (j + 1) * HEAD_DIM]
    queries = stacked(qkv_ref, j * GW)
    probs_ref[...] = dot(queries, keys, NT)
    lows = []
    for h in range(GROUP):
        rows = slice(h * TILE, (h + 1) * TILE)
        probs = softmax(probs_ref[rows, :], bias)
        probs_ref[rows, :] = probs
        lows.append(probs.astype(BF16))
    probs_low = jnp.concatenate(lows, axis=0)
    attn = dot(probs_low, values, NN).astype(BF16)
    return queries, keys, values, probs_low, attn


def forward_kernel(rank_ref, lens_ref, langs_ref, table_ref, qkv_ref, down_ref, up_ref, out_ref, probs_ref):
    rank = rank_ref[0]
    rate = table_ref[langs_ref[0, rank]]
    bias = mask_bias(lens_ref, 0, rank)
    low = jnp.zeros((TILE, RANK), F32)
    for j in range(KV):
        attn = attend_group(j, qkv_ref, bias, probs_ref)[-1]
        for h in range(GROUP):
            cols = slice(j * GW + h * HEAD_DIM, j * GW + (h + 1) * HEAD_DIM)
            out_ref[:, cols] = attn[h * TILE : (h + 1) * TILE]
        low = low + dot(out_ref[:, j * GW : (j + 1) * GW], down_ref[j * GW : (j + 1) * GW, :], NN)
    low = low.astype(BF16)
    for c in range(0, QW, 512):
        lift = dot(low, up_ref[:, c : c + 512], NN)
        out_ref[:, c : c + 512] = (out_ref[:, c : c + 512].astype(F32) + rate * lift).astype(BF16)


def prepare_kernel(
    rank_ref, lens_ref, langs_ref, dest_ref, table_ref, qkv_ref, slots_ref, down_ref, up_ref,
    probs_ref, attn_ref, scaled_ref, left_ref, own_ref, right_ref,
):
    rank = rank_ref[0]
    tiles = lens_ref.shape[1]
    bias = mask_bias(lens_ref, 1, rank)
    low = jnp.zeros((TILE, RANK), F32)
    for j in range(KV):
        block = slice(j * GW, (j + 1) * GW)
        attn = attend_group(j, qkv_ref, bias, probs_ref.at[block, :])[-1]
        for h in range(GROUP):
            cols = slice(j * GW + h * HEAD_DIM, j * GW + (h + 1) * HEAD_DIM)
            attn_ref[:, cols] = attn[h * TILE : (h + 1) * TILE]
        low = low + dot(attn_ref[:, block], down_ref[block, :], NN)
    for k, out_ref in enumerate((left_ref, own_ref, right_ref)):
        tile = rank + (k - 1)
        near = jnp.clip(tile, 0, tiles - 1)
        live = (tile == near) & (dest_ref[1, near] == rank)
        rate = jnp.where(live, table_ref[langs_ref[1, near]], 0.0)
        rows = slice(k * TILE, (k + 1) * TILE)
        back = jnp.zeros((TILE, RANK), F32)
        for c in range(0, QW, 512):
            cols = slice(c, c + 512)
            scaled = (rate * slots_ref[rows, cols].astype(F32)).astype(BF16)
            scaled_ref[rows, cols] = scaled
            back = back + dot(scaled, up_ref[:, cols], NT)
        out_ref[...] = jnp.concatenate([low, back], axis=1).astype(BF16)


def terms_kernel(
    rank_ref, dest_ref, attn_ref, scaled_ref, left_ref, own_ref, right_ref, terms_ref, back_ref
):
    rank = rank_ref[0]
    went = dest_ref[1, rank] - rank
    back = jnp.where(went < 0, left_ref[...], jnp.where(went > 0, right_ref[...], own_ref[...]))
    back_ref[...] = back
    lows = jnp.concatenate([left_ref[...], own_ref[...], right_ref[...]], axis=0)
    for c in range(0, QW, 512):
        cols = slice(c, c + 512)
        one = dot(attn_ref[:, cols], back, TN)
        two = dot(scaled_ref[:, cols], lows, TN)
        terms = jnp.concatenate([one[:, RANK:], two[:, :RANK]], axis=1)
        terms_ref[cols, :] = terms.astype(terms_ref.dtype)


def backward_kernel(
    rank_ref, dest_ref, qkv_ref, left_ref, mid_ref, right_ref, back_ref, probs_ref, down_ref,
    grad_ref, gattn_ref,
):
    rank = rank_ref[0]
    went = dest_ref[1, rank] - rank
    back = back_ref[...][:, RANK:]
    for j in range(KV):
        block = slice(j * GW, (j + 1) * GW)
        grad = jnp.where(
            went < 0, left_ref[:, block], jnp.where(went > 0, right_ref[:, block], mid_ref[:, block])
        )
        gattn = grad.astype(F32) + dot(back, down_ref[block, :], NT)
        gattn_ref[:, block] = gattn.astype(BF16)
        queries = stacked(qkv_ref, j * GW)
        keys = qkv_ref[:, QW + j * HEAD_DIM : QW + (j + 1) * HEAD_DIM]
        values = qkv_ref[:, QW + KW + j * HEAD_DIM : QW + KW + (j + 1) * HEAD_DIM]
        grads = stacked(gattn_ref, j * GW)
        grad_probs = dot(grads, values, NT)
        lows, scores = [], []
        for h in range(GROUP):
            probs = probs_ref[j * GW + h * TILE : j * GW + (h + 1) * TILE, :]
            lows.append(probs.astype(BF16))
            weighed = probs * grad_probs[h * TILE : (h + 1) * TILE]
            delta = jnp.sum(weighed, axis=-1, keepdims=True)
            scores.append(((weighed - probs * delta) * SCALE).astype(BF16))
        probs_low = jnp.concatenate(lows, axis=0)
        grad_scores = jnp.concatenate(scores, axis=0)
        grad_queries = dot(grad_scores, keys, NN).astype(BF16)
        for h in range(GROUP):
            cols = slice(j * GW + h * HEAD_DIM, j * GW + (h + 1) * HEAD_DIM)
            grad_ref[:, cols] = grad_queries[h * TILE : (h + 1) * TILE]
        cols = slice(QW + j * HEAD_DIM, QW + (j + 1) * HEAD_DIM)
        grad_ref[:, cols] = dot(grad_scores, queries, TN).astype(BF16)
        cols = slice(QW + KW + j * HEAD_DIM, QW + KW + (j + 1) * HEAD_DIM)
        grad_ref[:, cols] = dot(probs_low, grads, TN).astype(BF16)


COST = pl.CostEstimate(flops=2**20, bytes_accessed=2**20, transcendentals=0)
SMEM = pl.BlockSpec(memory_space=pltpu.SMEM)
VMEM = pl.BlockSpec(memory_space=pltpu.VMEM)


def run_forward(rank, lengths, languages, table, qkv, down, up):
    return pl.pallas_call(
        forward_kernel,
        out_shape=jax.ShapeDtypeStruct((TILE, QW), BF16),
        in_specs=[SMEM] * 4 + [VMEM] * 3,
        out_specs=VMEM,
        scratch_shapes=[pltpu.VMEM((GROUP * TILE, TILE), F32)],
        compiler_params=pltpu.CompilerParams(vmem_limit_bytes=24 * 2**20),
        cost_estimate=COST,
        name="forward_tile",
    )(rank, lengths, languages, table, qkv, down, up)


def run_prepare(rank, lengths, languages, dest, table, qkv, slots, down, up):
    message = jax.ShapeDtypeStruct((TILE, 2 * RANK), BF16)
    return pl.pallas_call(
        prepare_kernel,
        out_shape=(
            jax.ShapeDtypeStruct((QW, TILE), F32),
            jax.ShapeDtypeStruct((TILE, QW), BF16),
            jax.ShapeDtypeStruct((3 * TILE, QW), BF16),
            message,
            message,
            message,
        ),
        in_specs=[SMEM] * 5 + [VMEM] * 4,
        out_specs=(VMEM,) * 6,
        compiler_params=pltpu.CompilerParams(vmem_limit_bytes=40 * 2**20),
        cost_estimate=COST,
        name="prepare_tile",
    )(rank, lengths, languages, dest, table, qkv, slots, down, up)


def run_terms(rank, dest, attn, scaled, left, own, right):
    return pl.pallas_call(
        terms_kernel,
        out_shape=(
            jax.ShapeDtypeStruct((QW, 2 * RANK), BF16),
            jax.ShapeDtypeStruct((TILE, 2 * RANK), BF16),
        ),
        in_specs=[SMEM] * 2 + [VMEM] * 5,
        out_specs=(VMEM, VMEM),
        compiler_params=pltpu.CompilerParams(vmem_limit_bytes=24 * 2**20),
        cost_estimate=COST,
        name="adapter_terms",
    )(rank, dest, attn, scaled, left, own, right)


def run_backward(rank, dest, qkv, left, mid, right, back, probs, down):
    return pl.pallas_call(
        backward_kernel,
        out_shape=jax.ShapeDtypeStruct((TILE, QW + 2 * KW), BF16),
        in_specs=[SMEM] * 2 + [VMEM] * 7,
        out_specs=VMEM,
        scratch_shapes=[pltpu.VMEM((TILE, QW), BF16)],
        compiler_params=pltpu.CompilerParams(vmem_limit_bytes=40 * 2**20),
        cost_estimate=COST,
        name="backward_tile",
    )(rank, dest, qkv, left, mid, right, back, probs, down)


def sections():
    return lax.axis_size("section")


def shift(x, moves):
    size = lax.axis_size("dp")
    route = []
    for s_list, up, step, keep in moves:
        for s in s_list:
            for t in range(size):
                if 0 <= s + up < sections() and 0 <= t + step < size and keep(t):
                    route.append((s * size + t, (s + up) * size + t + step))
    return lax.ppermute(x, AXES, route)


def anywhere(t):
    return True


def spread(x, groups):
    pieces = lax.all_to_all(x, "dp", 0, 0, axis_index_groups=groups, tiled=True)
    return jnp.sum(pieces.astype(F32), axis=0)


def shards(
    qkv_a, qkv_b, slot_grad_b, adapter_down, adapter_up, lang_scale, languages, lengths, destination
):
    rank = lax.axis_index("dp")
    size = lax.axis_size("dp")
    rank_word = jnp.reshape(rank.astype(jnp.int32), (1,))
    down, up = adapter_down[0], adapter_up[0]
    slots = slot_grad_b[0]
    every = range(sections())
    later = range(1, sections())
    from_left = shift(slots[2 * TILE :], [(later, 0, 1, anywhere)])
    from_right = shift(slots[:TILE], [(later, 0, -1, anywhere)])
    out = run_forward(rank_word, lengths, languages, lang_scale, qkv_a[0], down, up)
    out, rank_word = lax.optimization_barrier((out, rank_word))
    hop = shift(out, [(every, 1, 0, anywhere)])
    probs, attn, scaled, to_left, own, to_right = run_prepare(
        rank_word, lengths, languages, destination, lang_scale, qkv_b[0], slots, down, up
    )
    left = shift(to_right, [(every, 0, 1, anywhere)])
    right = shift(to_left, [(every, 0, -1, anywhere)])
    terms, back = run_terms(rank_word, destination, attn, scaled, left, own, right)
    terms, back, from_left, from_right = lax.optimization_barrier(
        (terms, back, from_left, from_right)
    )
    terms, back, hop = lax.optimization_barrier((terms, back, hop))
    planes = [[4 * k + z for k in range(size // 4)] for z in range(4)]
    columns = [[4 * k + z for z in range(4)] for k in range(size // 4)]
    terms = spread(terms.reshape(size // 4, 256, 128), planes)
    terms = spread(terms.reshape(4, 64, 128), columns)
    grad_qkv = run_backward(
        rank_word, destination, qkv_b[0], from_left, slots[TILE : 2 * TILE], from_right, back,
        probs, down,
    )
    handed_back = shift(grad_qkv, [(every, -1, 0, anywhere)])[None]
    before = shift(hop, [(later, 0, 1, anywhere)])
    after = shift(hop, [(later, 0, -1, anywhere)])
    dest = destination[0]
    zero = jnp.zeros((), BF16)
    slot0 = jnp.where((dest[jnp.maximum(rank - 1, 0)] == rank) & (rank > 0), before, zero)
    slot1 = jnp.where(dest[rank] == rank, hop, zero)
    slot2 = jnp.where(
        (dest[jnp.minimum(rank + 1, size - 1)] == rank) & (rank < size - 1), after, zero
    )
    handed_forward = jnp.concatenate([slot0, slot1, slot2], axis=0)[None]
    return (handed_forward, handed_back, terms[None])


def solution(mesh):
    return jax.shard_map(
        shards,
        mesh=mesh,
        in_specs=(
            P("section", "dp", None),
            P("section", "dp", None),
            P("section", "dp", None),
            P("section", None, None),
            P("section", None, None),
            P(),
            P(),
            P(),
            P(),
        ),
        out_specs=(P("section", "dp", None), P("section", "dp", None), P("section", "dp", None)),
        check_vma=False,
    )
```

```python
import functools
import math

import jax
import jax.numpy as jnp
from jax import lax
from jax.experimental import pallas as pl
from jax.experimental.pallas import tpu as pltpu
from jax.sharding import PartitionSpec as P

HEADS = 32
KV = 4
GROUP = HEADS // KV
HEAD_DIM = 128
TILE = 128
SEGS = 8
RANK = 64
QW = HEADS * HEAD_DIM
KW = KV * HEAD_DIM
GW = GROUP * HEAD_DIM
SCALE = 1.0 / math.sqrt(HEAD_DIM)
RUN = 4
AXES = ("section", "dp")
BF16 = jnp.bfloat16
F32 = jnp.float32


def dot(a, b, dims):
    return lax.dot_general(a, b, (dims, ((), ())), preferred_element_type=F32)


NN = ((1,), (0,))
NT = ((1,), (1,))
TN = ((0,), (0,))


def mask_bias(lens_ref, m, rank):
    shape = (TILE, TILE)
    row = lax.broadcasted_iota(jnp.int32, shape, 0)
    col = lax.broadcasted_iota(jnp.int32, shape, 1)
    seg_row = jnp.zeros(shape, jnp.int32)
    seg_col = jnp.zeros(shape, jnp.int32)
    end = jnp.int32(0)
    for k in range(SEGS):
        end = end + lens_ref[m, rank, k]
        seg_row = seg_row + (row >= end).astype(jnp.int32)
        seg_col = seg_col + (col >= end).astype(jnp.int32)
    allowed = (seg_row == seg_col) & (row >= col)
    return jnp.where(allowed, 0.0, -1e30).astype(F32)


def stacked(ref, base):
    return jnp.concatenate(
        [ref[:, base + h * HEAD_DIM : base + (h + 1) * HEAD_DIM] for h in range(GROUP)], axis=0
    )


def softmax(scores, bias):
    masked = scores + bias
    top = jnp.max(masked, axis=-1, keepdims=True)
    weights = jnp.exp2((masked - top) * (SCALE * math.log2(math.e)))
    return weights * (1.0 / jnp.sum(weights, axis=-1, keepdims=True))


def attend_group(j, qkv_ref, bias, probs_ref):
    keys = qkv_ref[:, QW + j * HEAD_DIM : QW + (j + 1) * HEAD_DIM]
    values = qkv_ref[:, QW + KW + j * HEAD_DIM : QW + KW + (j + 1) * HEAD_DIM]
    queries = stacked(qkv_ref, j * GW)
    probs_ref[...] = dot(queries, keys, NT)
    lows = []
    for h in range(GROUP):
        rows = slice(h * TILE, (h + 1) * TILE)
        probs = softmax(probs_ref[rows, :], bias)
        probs_ref[rows, :] = probs
        lows.append(probs.astype(BF16))
    probs_low = jnp.concatenate(lows, axis=0)
    attn = dot(probs_low, values, NN).astype(BF16)
    return queries, keys, values, probs_low, attn


def forward_kernel(rank_ref, lens_ref, langs_ref, table_ref, qkv_ref, down_ref, up_ref, out_ref, probs_ref):
    rank = rank_ref[0]
    rate = table_ref[langs_ref[0, rank]]
    bias = mask_bias(lens_ref, 0, rank)
    low = jnp.zeros((TILE, RANK), F32)
    for j in range(KV):
        attn = attend_group(j, qkv_ref, bias, probs_ref)[-1]
        for h in range(GROUP):
            cols = slice(j * GW + h * HEAD_DIM, j * GW + (h + 1) * HEAD_DIM)
            out_ref[:, cols] = attn[h * TILE : (h + 1) * TILE]
        low = low + dot(out_ref[:, j * GW : (j + 1) * GW], down_ref[j * GW : (j + 1) * GW, :], NN)
    low = low.astype(BF16)
    for c in range(0, QW, 512):
        lift = dot(low, up_ref[:, c : c + 512], NN)
        out_ref[:, c : c + 512] = (out_ref[:, c : c + 512].astype(F32) + rate * lift).astype(BF16)


def slot_rate(k, rank, tiles, langs_ref, dest_ref, table_ref):
    tile = rank + (k - 1)
    near = jnp.clip(tile, 0, tiles - 1)
    live = (tile == near) & (dest_ref[1, near] == rank)
    return jnp.where(live, table_ref[langs_ref[1, near]], 0.0)


def prepare_kernel(
    place_ref, lens_ref, langs_ref, dest_ref, table_ref, qkv_ref, slots_ref, down_ref, up_ref,
    probs_ref, attn_ref, low_ref, left_ref, own_ref, right_ref,
):
    rank = place_ref[0]
    tiles = lens_ref.shape[1]
    bias = mask_bias(lens_ref, 1, rank)
    low = jnp.zeros((TILE, RANK), F32)
    for j in range(KV):
        block = slice(j * GW, (j + 1) * GW)
        attn = attend_group(j, qkv_ref, bias, probs_ref.at[block, :])[-1]
        for h in range(GROUP):
            cols = slice(j * GW + h * HEAD_DIM, j * GW + (h + 1) * HEAD_DIM)
            attn_ref[:, cols] = attn[h * TILE : (h + 1) * TILE]
        low = low + dot(attn_ref[:, block], down_ref[block, :], NN)
    low_ref[...] = low.astype(BF16)

    @pl.when(place_ref[1] == 0)
    def _():
        for k, out_ref in enumerate((left_ref, own_ref, right_ref)):
            rate = slot_rate(k, rank, tiles, langs_ref, dest_ref, table_ref)
            back = jnp.zeros((TILE, RANK), F32)
            for c in range(0, QW, 512):
                cols = slice(c, c + 512)
                grad = slots_ref[k * TILE : (k + 1) * TILE, cols]
                scaled = (rate * grad.astype(F32)).astype(BF16)
                back = back + dot(scaled, up_ref[:, cols], NT)
            out_ref[...] = jnp.concatenate([low, back], axis=1).astype(BF16)

    @pl.when(place_ref[1] != 0)
    def _():
        for out_ref in (left_ref, own_ref, right_ref):
            out_ref[...] = jnp.zeros(out_ref.shape, BF16)


def terms_kernel(
    place_ref, langs_ref, dest_ref, table_ref, attn_ref, slots_ref, left_ref, own_ref, right_ref,
    scaled_ref, back_ref, low_ref, terms_ref, slot_scaled_ref,
):
    rank = place_ref[0]
    tiles = dest_ref.shape[1]

    @pl.when(place_ref[1] == 0)
    def _():
        went = dest_ref[1, rank] - rank
        back = jnp.where(went < 0, left_ref[...], jnp.where(went > 0, right_ref[...], own_ref[...]))
        lows = jnp.concatenate([left_ref[...], own_ref[...], right_ref[...]], axis=0)
        for c in range(0, QW, 512):
            cols = slice(c, c + 512)
            for k in range(3):
                rows = slice(k * TILE, (k + 1) * TILE)
                rate = slot_rate(k, rank, tiles, langs_ref, dest_ref, table_ref)
                slot_scaled_ref[rows, :] = (rate * slots_ref[rows, cols].astype(F32)).astype(BF16)
            one = dot(attn_ref[:, cols], back, TN)
            two = dot(slot_scaled_ref[...], lows, TN)
            terms = jnp.concatenate([one[:, RANK:], two[:, :RANK]], axis=1)
            terms_ref[cols, :] = terms.astype(terms_ref.dtype)

    @pl.when(place_ref[1] != 0)
    def _():
        for c in range(0, QW, 512):
            cols = slice(c, c + 512)
            one = dot(attn_ref[:, cols], back_ref[...], TN)
            two = dot(scaled_ref[:, cols], low_ref[...], TN)
            terms_ref[cols, :] = jnp.concatenate([one, two], axis=1).astype(terms_ref.dtype)


def backward_kernel(
    place_ref, langs_ref, dest_ref, table_ref, qkv_ref, left_ref, right_ref, last_left_ref,
    last_right_ref, slots_ref, probs_ref, down_ref, up_ref, grad_ref, scaled_ref, back_ref,
    gattn_ref,
):
    rank = place_ref[0]
    rate = table_ref[langs_ref[1, rank]]
    went = dest_ref[1, rank] - rank
    last = place_ref[1] == place_ref[2] - 1

    def chosen():
        back = jnp.zeros((TILE, RANK), F32)
        for c in range(0, QW, 512):
            cols = slice(c, c + 512)
            left = jnp.where(last, last_left_ref[:, cols], left_ref[:, cols])
            right = jnp.where(last, last_right_ref[:, cols], right_ref[:, cols])
            mid = slots_ref[TILE : 2 * TILE, cols]
            grad = jnp.where(went < 0, left, jnp.where(went > 0, right, mid))
            gattn_ref[:, cols] = grad
            scaled = (rate * grad.astype(F32)).astype(BF16)
            scaled_ref[:, cols] = scaled
            back = back + dot(scaled, up_ref[:, cols], NT)
        return back.astype(BF16)

    @pl.when(place_ref[1] != 0)
    def _():
        back = chosen()
        back_ref[...] = back
        for j in range(KV):
            block = slice(j * GW, (j + 1) * GW)
            gattn = gattn_ref[:, block].astype(F32) + dot(back, down_ref[block, :], NT)
            gattn_ref[:, block] = gattn.astype(BF16)
            queries = stacked(qkv_ref, j * GW)
            keys = qkv_ref[:, QW + j * HEAD_DIM : QW + (j + 1) * HEAD_DIM]
            values = qkv_ref[:, QW + KW + j * HEAD_DIM : QW + KW + (j + 1) * HEAD_DIM]
            grads = stacked(gattn_ref, j * GW)
            grad_probs = dot(grads, values, NT)
            lows, scores = [], []
            for h in range(GROUP):
                probs = probs_ref[j * GW + h * TILE : j * GW + (h + 1) * TILE, :]
                lows.append(probs.astype(BF16))
                weighed = probs * grad_probs[h * TILE : (h + 1) * TILE]
                delta = jnp.sum(weighed, axis=-1, keepdims=True)
                scores.append(((weighed - probs * delta) * SCALE).astype(BF16))
            probs_low = jnp.concatenate(lows, axis=0)
            grad_scores = jnp.concatenate(scores, axis=0)
            grad_queries = dot(grad_scores, keys, NN).astype(BF16)
            for h in range(GROUP):
                cols = slice(j * GW + h * HEAD_DIM, j * GW + (h + 1) * HEAD_DIM)
                grad_ref[:, cols] = grad_queries[h * TILE : (h + 1) * TILE]
            cols = slice(QW + j * HEAD_DIM, QW + (j + 1) * HEAD_DIM)
            grad_ref[:, cols] = dot(grad_scores, queries, TN).astype(BF16)
            cols = slice(QW + KW + j * HEAD_DIM, QW + KW + (j + 1) * HEAD_DIM)
            grad_ref[:, cols] = dot(probs_low, grads, TN).astype(BF16)

    @pl.when(place_ref[1] == 0)
    def _():
        grad_ref[...] = jnp.zeros(grad_ref.shape, BF16)
        scaled_ref[...] = jnp.zeros(scaled_ref.shape, BF16)
        back_ref[...] = jnp.zeros(back_ref.shape, BF16)


COST = pl.CostEstimate(flops=2**20, bytes_accessed=2**20, transcendentals=0)
SMEM = pl.BlockSpec(memory_space=pltpu.SMEM)
VMEM = pl.BlockSpec(memory_space=pltpu.VMEM)


def run_forward(rank, lengths, languages, table, qkv, down, up):
    return pl.pallas_call(
        forward_kernel,
        out_shape=jax.ShapeDtypeStruct((TILE, QW), BF16),
        in_specs=[SMEM] * 4 + [VMEM] * 3,
        out_specs=VMEM,
        scratch_shapes=[pltpu.VMEM((GROUP * TILE, TILE), F32)],
        compiler_params=pltpu.CompilerParams(vmem_limit_bytes=24 * 2**20),
        cost_estimate=COST,
        name="forward_tile",
    )(rank, lengths, languages, table, qkv, down, up)


def run_prepare(place, lengths, languages, dest, table, qkv, slots, down, up):
    message = jax.ShapeDtypeStruct((TILE, 2 * RANK), BF16)
    return pl.pallas_call(
        prepare_kernel,
        out_shape=(
            jax.ShapeDtypeStruct((QW, TILE), F32),
            jax.ShapeDtypeStruct((TILE, QW), BF16),
            jax.ShapeDtypeStruct((TILE, RANK), BF16),
            message,
            message,
            message,
        ),
        in_specs=[SMEM] * 5 + [VMEM] * 4,
        out_specs=(VMEM,) * 6,
        compiler_params=pltpu.CompilerParams(vmem_limit_bytes=40 * 2**20),
        cost_estimate=COST,
        name="prepare_tile",
    )(place, lengths, languages, dest, table, qkv, slots, down, up)


def run_terms(place, languages, dest, table, attn, slots, left, own, right, scaled, back, low):
    return pl.pallas_call(
        terms_kernel,
        out_shape=jax.ShapeDtypeStruct((QW, 2 * RANK), BF16),
        in_specs=[SMEM] * 4 + [VMEM] * 8,
        out_specs=VMEM,
        scratch_shapes=[pltpu.VMEM((3 * TILE, 512), BF16)],
        compiler_params=pltpu.CompilerParams(vmem_limit_bytes=40 * 2**20),
        cost_estimate=COST,
        name="adapter_terms",
    )(place, languages, dest, table, attn, slots, left, own, right, scaled, back, low)


def run_backward(place, languages, dest, table, qkv, moved, slots, probs, down, up):
    return pl.pallas_call(
        backward_kernel,
        out_shape=(
            jax.ShapeDtypeStruct((TILE, QW + 2 * KW), BF16),
            jax.ShapeDtypeStruct((TILE, QW), BF16),
            jax.ShapeDtypeStruct((TILE, RANK), BF16),
        ),
        in_specs=[SMEM] * 4 + [VMEM] * 9,
        out_specs=(VMEM,) * 3,
        scratch_shapes=[pltpu.VMEM((TILE, QW), BF16)],
        compiler_params=pltpu.CompilerParams(vmem_limit_bytes=48 * 2**20),
        cost_estimate=COST,
        name="backward_tile",
    )(place, languages, dest, table, qkv, *moved, slots, probs, down, up)


def sections():
    return lax.axis_size("section")


def shift(x, moves):
    size = lax.axis_size("dp")
    route = []
    for s_list, up, step, keep in moves:
        for s in s_list:
            for t in range(size):
                if 0 <= s + up < sections() and 0 <= t + step < size and keep(t):
                    route.append((s * size + t, (s + up) * size + t + step))
    return lax.ppermute(x, AXES, route)


def anywhere(t):
    return True


def run_start(t):
    return t % RUN == 0


def run_end(t):
    return t % RUN == RUN - 1


def not_run_start(t):
    return t % RUN != 0


def not_run_end(t):
    return t % RUN != RUN - 1


def spread(x, groups):
    pieces = lax.all_to_all(x, "dp", 0, 0, axis_index_groups=groups, tiled=True)
    return jnp.sum(pieces.astype(F32), axis=0)


def shards(
    qkv_a, qkv_b, slot_grad_b, adapter_down, adapter_up, lang_scale, languages, lengths, destination
):
    rank, size = lax.axis_index("dp"), lax.axis_size("dp")
    section, last = lax.axis_index("section"), sections() - 1
    place = jnp.stack([rank, section, jnp.int32(sections())]).astype(jnp.int32)
    down, up = adapter_down[0], adapter_up[0]
    slots = slot_grad_b[0]
    every, early = range(sections()), range(1, last)
    to_up, to_down = slots[2 * TILE :], slots[:TILE]
    from_left = shift(to_up, [(early, 0, 1, anywhere)])
    from_right = shift(to_down, [(early, 0, -1, anywhere)])
    out = run_forward(place, lengths, languages, lang_scale, qkv_a[0], down, up)
    out, place = lax.optimization_barrier((out, place))
    near = shift(out, [([0, 2], 1, 0, anywhere)])
    far = shift(out, [([1], 1, 0, anywhere)])
    probs, attn, low, to_left, own, to_right = run_prepare(
        place, lengths, languages, destination, lang_scale, qkv_b[0], slots, down, up
    )
    from_left, from_right, low = lax.optimization_barrier((from_left, from_right, low))
    to_up, to_down, near, low = lax.optimization_barrier((to_up, to_down, near, low))
    last_left = shift(to_up, [([last], 0, 1, anywhere)])
    last_right = shift(to_down, [([last], 0, -1, anywhere)])
    grad_qkv, scaled, back = run_backward(
        place, languages, destination, lang_scale, qkv_b[0],
        (from_left, from_right, last_left, last_right), slots, probs, down, up,
    )
    grad_qkv, near, to_left, to_right = lax.optimization_barrier(
        (grad_qkv, near, to_left, to_right)
    )
    handed_back = shift(grad_qkv, [(every, -1, 0, anywhere)])[None]
    before = shift(near, [([1, 3], 0, 1, anywhere)])
    after = shift(near, [([1, 3], 0, -1, anywhere)])
    left = shift(to_right, [([0], 0, 1, anywhere)])
    right = shift(to_left, [([0], 0, -1, anywhere)])
    terms = run_terms(
        place, languages, destination, lang_scale, attn, slots, left, own, right, scaled, back, low
    )
    planes = [[RUN * k + z for k in range(size // RUN)] for z in range(RUN)]
    columns = [[RUN * k + z for z in range(RUN)] for k in range(size // RUN)]
    terms = spread(terms.reshape(size // RUN, -1, 2 * RANK), planes)
    far, terms = lax.optimization_barrier((far, terms))
    crossed = section == 2
    sent = jnp.where(crossed, far, out)
    far_before = shift(sent, [([1], 1, 1, run_end), ([2], 0, 1, not_run_end)])
    far_after = shift(sent, [([1], 1, -1, run_start), ([2], 0, -1, not_run_start)])
    terms, handed_back, before, after = lax.optimization_barrier(
        (terms, handed_back, before, after)
    )
    terms = spread(terms.reshape(RUN, -1, 2 * RANK), columns)
    hop = jnp.where(crossed, far, near)
    slot0 = jnp.where(crossed, far_before, before)
    slot2 = jnp.where(crossed, far_after, after)
    dest = destination[0]
    zero = jnp.zeros((), BF16)
    slot0 = jnp.where((dest[jnp.maximum(rank - 1, 0)] == rank) & (rank > 0), slot0, zero)
    slot1 = jnp.where(dest[rank] == rank, hop, zero)
    slot2 = jnp.where(
        (dest[jnp.minimum(rank + 1, size - 1)] == rank) & (rank < size - 1), slot2, zero
    )
    handed_forward = jnp.concatenate([slot0, slot1, slot2], axis=0)[None]
    return (handed_forward, handed_back, terms[None])


def solution(mesh):
    return jax.shard_map(
        shards,
        mesh=mesh,
        in_specs=(
            P("section", "dp", None),
            P("section", "dp", None),
            P("section", "dp", None),
            P("section", None, None),
            P("section", None, None),
            P(),
            P(),
            P(),
            P(),
        ),
        out_specs=(P("section", "dp", None), P("section", "dp", None), P("section", "dp", None)),
        check_vma=False,
    )
```

```python
import functools
import math

import jax
import jax.numpy as jnp
from jax import lax
from jax.experimental import pallas as pl
from jax.experimental.pallas import tpu as pltpu
from jax.sharding import PartitionSpec as P

HEADS = 32
KV = 4
GROUP = HEADS // KV
HEAD_DIM = 128
TILE = 128
SEGS = 8
RANK = 64
QW = HEADS * HEAD_DIM
KW = KV * HEAD_DIM
GW = GROUP * HEAD_DIM
SCALE = 1.0 / math.sqrt(HEAD_DIM)
RUN = 4
AXES = ("section", "dp")
BF16 = jnp.bfloat16
F32 = jnp.float32


def dot(a, b, dims):
    return lax.dot_general(a, b, (dims, ((), ())), preferred_element_type=F32)


NN = ((1,), (0,))
NT = ((1,), (1,))
TN = ((0,), (0,))


def mask_bias(lens_ref, m, rank):
    shape = (TILE, TILE)
    row = lax.broadcasted_iota(jnp.int32, shape, 0)
    col = lax.broadcasted_iota(jnp.int32, shape, 1)
    seg_row = jnp.zeros(shape, jnp.int32)
    seg_col = jnp.zeros(shape, jnp.int32)
    end = jnp.int32(0)
    for k in range(SEGS):
        end = end + lens_ref[m, rank, k]
        seg_row = seg_row + (row >= end).astype(jnp.int32)
        seg_col = seg_col + (col >= end).astype(jnp.int32)
    allowed = (seg_row == seg_col) & (row >= col)
    return jnp.where(allowed, 0.0, -1e30).astype(F32)


def stacked(ref, base):
    return jnp.concatenate(
        [ref[:, base + h * HEAD_DIM : base + (h + 1) * HEAD_DIM] for h in range(GROUP)], axis=0
    )


def softmax(scores, bias):
    masked = scores + bias
    top = jnp.max(masked, axis=-1, keepdims=True)
    weights = jnp.exp2((masked - top) * (SCALE * math.log2(math.e)))
    return weights * (1.0 / jnp.sum(weights, axis=-1, keepdims=True))


def attend_group(j, qkv_ref, bias, probs_ref):
    keys = qkv_ref[:, QW + j * HEAD_DIM : QW + (j + 1) * HEAD_DIM]
    values = qkv_ref[:, QW + KW + j * HEAD_DIM : QW + KW + (j + 1) * HEAD_DIM]
    queries = stacked(qkv_ref, j * GW)
    probs_ref[...] = dot(queries, keys, NT)
    lows = []
    for h in range(GROUP):
        rows = slice(h * TILE, (h + 1) * TILE)
        probs = softmax(probs_ref[rows, :], bias)
        probs_ref[rows, :] = probs
        lows.append(probs.astype(BF16))
    probs_low = jnp.concatenate(lows, axis=0)
    attn = dot(probs_low, values, NN).astype(BF16)
    return queries, keys, values, probs_low, attn


def forward_kernel(rank_ref, lens_ref, langs_ref, table_ref, qkv_ref, down_ref, up_ref, out_ref, probs_ref):
    rank = rank_ref[0]
    rate = table_ref[langs_ref[0, rank]]
    bias = mask_bias(lens_ref, 0, rank)
    low = jnp.zeros((TILE, RANK), F32)
    for j in range(KV):
        attn = attend_group(j, qkv_ref, bias, probs_ref)[-1]
        for h in range(GROUP):
            cols = slice(j * GW + h * HEAD_DIM, j * GW + (h + 1) * HEAD_DIM)
            out_ref[:, cols] = attn[h * TILE : (h + 1) * TILE]
        low = low + dot(out_ref[:, j * GW : (j + 1) * GW], down_ref[j * GW : (j + 1) * GW, :], NN)
    low = low.astype(BF16)
    for c in range(0, QW, 512):
        lift = dot(low, up_ref[:, c : c + 512], NN)
        out_ref[:, c : c + 512] = (out_ref[:, c : c + 512].astype(F32) + rate * lift).astype(BF16)


def slot_rate(k, rank, tiles, langs_ref, dest_ref, table_ref):
    tile = rank + (k - 1)
    near = jnp.clip(tile, 0, tiles - 1)
    live = (tile == near) & (dest_ref[1, near] == rank)
    return jnp.where(live, table_ref[langs_ref[1, near]], 0.0)


def prepare_kernel(
    place_ref, lens_ref, langs_ref, dest_ref, table_ref, qkv_ref, slots_ref, down_ref, up_ref,
    probs_ref, attn_ref, low_ref, left_ref, own_ref, right_ref,
):
    rank = place_ref[0]
    tiles = lens_ref.shape[1]
    bias = mask_bias(lens_ref, 1, rank)
    low = jnp.zeros((TILE, RANK), F32)
    for j in range(KV):
        block = slice(j * GW, (j + 1) * GW)
        attn = attend_group(j, qkv_ref, bias, probs_ref.at[block, :])[-1]
        for h in range(GROUP):
            cols = slice(j * GW + h * HEAD_DIM, j * GW + (h + 1) * HEAD_DIM)
            attn_ref[:, cols] = attn[h * TILE : (h + 1) * TILE]
        low = low + dot(attn_ref[:, block], down_ref[block, :], NN)
    low_ref[...] = low.astype(BF16)

    @pl.when(place_ref[1] == 0)
    def _():
        for k, out_ref in enumerate((left_ref, own_ref, right_ref)):
            rate = slot_rate(k, rank, tiles, langs_ref, dest_ref, table_ref)
            back = jnp.zeros((TILE, RANK), F32)
            for c in range(0, QW, 512):
                cols = slice(c, c + 512)
                grad = slots_ref[k * TILE : (k + 1) * TILE, cols]
                scaled = (rate * grad.astype(F32)).astype(BF16)
                back = back + dot(scaled, up_ref[:, cols], NT)
            out_ref[...] = jnp.concatenate([low, back], axis=1).astype(BF16)

    @pl.when(place_ref[1] != 0)
    def _():
        for out_ref in (left_ref, own_ref, right_ref):
            out_ref[...] = jnp.zeros(out_ref.shape, BF16)


def terms_kernel(
    place_ref, langs_ref, dest_ref, table_ref, attn_ref, slots_ref, left_ref, own_ref, right_ref,
    scaled_ref, back_ref, low_ref, terms_ref, slot_scaled_ref,
):
    rank = place_ref[0]
    tiles = dest_ref.shape[1]

    @pl.when(place_ref[1] == 0)
    def _():
        went = dest_ref[1, rank] - rank
        back = jnp.where(went < 0, left_ref[...], jnp.where(went > 0, right_ref[...], own_ref[...]))
        lows = jnp.concatenate([left_ref[...], own_ref[...], right_ref[...]], axis=0)
        for c in range(0, QW, 512):
            cols = slice(c, c + 512)
            for k in range(3):
                rows = slice(k * TILE, (k + 1) * TILE)
                rate = slot_rate(k, rank, tiles, langs_ref, dest_ref, table_ref)
                slot_scaled_ref[rows, :] = (rate * slots_ref[rows, cols].astype(F32)).astype(BF16)
            one = dot(attn_ref[:, cols], back, TN)
            two = dot(slot_scaled_ref[...], lows, TN)
            terms = jnp.concatenate([one[:, RANK:], two[:, :RANK]], axis=1)
            terms_ref[cols, :] = terms.astype(terms_ref.dtype)

    @pl.when(place_ref[1] != 0)
    def _():
        for c in range(0, QW, 512):
            cols = slice(c, c + 512)
            one = dot(attn_ref[:, cols], back_ref[...], TN)
            two = dot(scaled_ref[:, cols], low_ref[...], TN)
            terms_ref[cols, :] = jnp.concatenate([one, two], axis=1).astype(terms_ref.dtype)


def backward_kernel(
    place_ref, langs_ref, dest_ref, table_ref, qkv_ref, left_ref, right_ref, last_left_ref,
    last_right_ref, slots_ref, probs_ref, down_ref, up_ref, grad_ref, scaled_ref, back_ref,
    gattn_ref,
):
    rank = place_ref[0]
    rate = table_ref[langs_ref[1, rank]]
    went = dest_ref[1, rank] - rank
    last = place_ref[1] == place_ref[2] - 1

    def chosen():
        back = jnp.zeros((TILE, RANK), F32)
        for c in range(0, QW, 512):
            cols = slice(c, c + 512)
            left = jnp.where(last, last_left_ref[:, cols], left_ref[:, cols])
            right = jnp.where(last, last_right_ref[:, cols], right_ref[:, cols])
            mid = slots_ref[TILE : 2 * TILE, cols]
            grad = jnp.where(went < 0, left, jnp.where(went > 0, right, mid))
            gattn_ref[:, cols] = grad
            scaled = (rate * grad.astype(F32)).astype(BF16)
            scaled_ref[:, cols] = scaled
            back = back + dot(scaled, up_ref[:, cols], NT)
        return back.astype(BF16)

    @pl.when(place_ref[1] != 0)
    def _():
        back = chosen()
        back_ref[...] = back
        for j in range(KV):
            block = slice(j * GW, (j + 1) * GW)
            gattn = gattn_ref[:, block].astype(F32) + dot(back, down_ref[block, :], NT)
            gattn_ref[:, block] = gattn.astype(BF16)
            queries = stacked(qkv_ref, j * GW)
            keys = qkv_ref[:, QW + j * HEAD_DIM : QW + (j + 1) * HEAD_DIM]
            values = qkv_ref[:, QW + KW + j * HEAD_DIM : QW + KW + (j + 1) * HEAD_DIM]
            grads = stacked(gattn_ref, j * GW)
            grad_probs = dot(grads, values, NT)
            lows, scores = [], []
            for h in range(GROUP):
                probs = probs_ref[j * GW + h * TILE : j * GW + (h + 1) * TILE, :]
                lows.append(probs.astype(BF16))
                weighed = probs * grad_probs[h * TILE : (h + 1) * TILE]
                delta = jnp.sum(weighed, axis=-1, keepdims=True)
                scores.append(((weighed - probs * delta) * SCALE).astype(BF16))
            probs_low = jnp.concatenate(lows, axis=0)
            grad_scores = jnp.concatenate(scores, axis=0)
            grad_queries = dot(grad_scores, keys, NN).astype(BF16)
            for h in range(GROUP):
                cols = slice(j * GW + h * HEAD_DIM, j * GW + (h + 1) * HEAD_DIM)
                grad_ref[:, cols] = grad_queries[h * TILE : (h + 1) * TILE]
            cols = slice(QW + j * HEAD_DIM, QW + (j + 1) * HEAD_DIM)
            grad_ref[:, cols] = dot(grad_scores, queries, TN).astype(BF16)
            cols = slice(QW + KW + j * HEAD_DIM, QW + KW + (j + 1) * HEAD_DIM)
            grad_ref[:, cols] = dot(probs_low, grads, TN).astype(BF16)

    @pl.when(place_ref[1] == 0)
    def _():
        grad_ref[...] = jnp.zeros(grad_ref.shape, BF16)
        scaled_ref[...] = jnp.zeros(scaled_ref.shape, BF16)
        back_ref[...] = jnp.zeros(back_ref.shape, BF16)


COST = pl.CostEstimate(flops=2**20, bytes_accessed=2**20, transcendentals=0)
SMEM = pl.BlockSpec(memory_space=pltpu.SMEM)
VMEM = pl.BlockSpec(memory_space=pltpu.VMEM)


def run_forward(rank, lengths, languages, table, qkv, down, up):
    return pl.pallas_call(
        forward_kernel,
        out_shape=jax.ShapeDtypeStruct((TILE, QW), BF16),
        in_specs=[SMEM] * 4 + [VMEM] * 3,
        out_specs=VMEM,
        scratch_shapes=[pltpu.VMEM((GROUP * TILE, TILE), F32)],
        compiler_params=pltpu.CompilerParams(vmem_limit_bytes=24 * 2**20),
        cost_estimate=COST,
        name="forward_tile",
    )(rank, lengths, languages, table, qkv, down, up)


def run_prepare(place, lengths, languages, dest, table, qkv, slots, down, up):
    message = jax.ShapeDtypeStruct((TILE, 2 * RANK), BF16)
    return pl.pallas_call(
        prepare_kernel,
        out_shape=(
            jax.ShapeDtypeStruct((QW, TILE), F32),
            jax.ShapeDtypeStruct((TILE, QW), BF16),
            jax.ShapeDtypeStruct((TILE, RANK), BF16),
            message,
            message,
            message,
        ),
        in_specs=[SMEM] * 5 + [VMEM] * 4,
        out_specs=(VMEM,) * 6,
        compiler_params=pltpu.CompilerParams(vmem_limit_bytes=40 * 2**20),
        cost_estimate=COST,
        name="prepare_tile",
    )(place, lengths, languages, dest, table, qkv, slots, down, up)


def run_terms(place, languages, dest, table, attn, slots, left, own, right, scaled, back, low):
    return pl.pallas_call(
        terms_kernel,
        out_shape=jax.ShapeDtypeStruct((QW, 2 * RANK), BF16),
        in_specs=[SMEM] * 4 + [VMEM] * 8,
        out_specs=VMEM,
        scratch_shapes=[pltpu.VMEM((3 * TILE, 512), BF16)],
        compiler_params=pltpu.CompilerParams(vmem_limit_bytes=40 * 2**20),
        cost_estimate=COST,
        name="adapter_terms",
    )(place, languages, dest, table, attn, slots, left, own, right, scaled, back, low)


def run_backward(place, languages, dest, table, qkv, moved, slots, probs, down, up):
    return pl.pallas_call(
        backward_kernel,
        out_shape=(
            jax.ShapeDtypeStruct((TILE, QW + 2 * KW), BF16),
            jax.ShapeDtypeStruct((TILE, QW), BF16),
            jax.ShapeDtypeStruct((TILE, RANK), BF16),
        ),
        in_specs=[SMEM] * 4 + [VMEM] * 9,
        out_specs=(VMEM,) * 3,
        scratch_shapes=[pltpu.VMEM((TILE, QW), BF16)],
        compiler_params=pltpu.CompilerParams(vmem_limit_bytes=48 * 2**20),
        cost_estimate=COST,
        name="backward_tile",
    )(place, languages, dest, table, qkv, *moved, slots, probs, down, up)


def sections():
    return lax.axis_size("section")


def shift(x, moves):
    size = lax.axis_size("dp")
    route = []
    for s_list, up, step, keep in moves:
        for s in s_list:
            for t in range(size):
                if 0 <= s + up < sections() and 0 <= t + step < size and keep(t):
                    route.append((s * size + t, (s + up) * size + t + step))
    return lax.ppermute(x, AXES, route)


def anywhere(t):
    return True


def run_start(t):
    return t % RUN == 0


def run_end(t):
    return t % RUN == RUN - 1


def not_run_start(t):
    return t % RUN != 0


def not_run_end(t):
    return t % RUN != RUN - 1


def scatter(x, groups):
    return lax.all_to_all(x, "dp", 0, 0, axis_index_groups=groups, tiled=True)


def shards(
    qkv_a, qkv_b, slot_grad_b, adapter_down, adapter_up, lang_scale, languages, lengths, destination
):
    rank, size = lax.axis_index("dp"), lax.axis_size("dp")
    section, last = lax.axis_index("section"), sections() - 1
    place = jnp.stack([rank, section, jnp.int32(sections())]).astype(jnp.int32)
    down, up = adapter_down[0], adapter_up[0]
    slots = slot_grad_b[0]
    every, early = range(sections()), range(1, last)
    to_up, to_down = slots[2 * TILE :], slots[:TILE]
    from_left = shift(to_up, [(early, 0, 1, anywhere)])
    from_right = shift(to_down, [(early, 0, -1, anywhere)])
    out = run_forward(place, lengths, languages, lang_scale, qkv_a[0], down, up)
    out, place = lax.optimization_barrier((out, place))
    near = shift(out, [([0, 2], 1, 0, anywhere)])
    far = shift(out, [([1], 1, 0, anywhere)])
    probs, attn, low, to_left, own, to_right = run_prepare(
        place, lengths, languages, destination, lang_scale, qkv_b[0], slots, down, up
    )
    from_left, from_right, low = lax.optimization_barrier((from_left, from_right, low))
    to_up, to_down, near, low = lax.optimization_barrier((to_up, to_down, near, low))
    last_left = shift(to_up, [([last], 0, 1, anywhere)])
    last_right = shift(to_down, [([last], 0, -1, anywhere)])
    grad_qkv, scaled, back = run_backward(
        place, languages, destination, lang_scale, qkv_b[0],
        (from_left, from_right, last_left, last_right), slots, probs, down, up,
    )
    grad_qkv, near, to_left, to_right = lax.optimization_barrier(
        (grad_qkv, near, to_left, to_right)
    )
    handed_back = shift(grad_qkv, [(every, -1, 0, anywhere)])[None]
    before = shift(near, [([1, 3], 0, 1, anywhere)])
    after = shift(near, [([1, 3], 0, -1, anywhere)])
    left = shift(to_right, [([0], 0, 1, anywhere)])
    right = shift(to_left, [([0], 0, -1, anywhere)])
    terms = run_terms(
        place, languages, destination, lang_scale, attn, slots, left, own, right, scaled, back, low
    )
    planes = [[RUN * k + z for k in range(size // RUN)] for z in range(RUN)]
    columns = [[RUN * k + z for z in range(RUN)] for k in range(size // RUN)]
    far, terms = lax.optimization_barrier((far, terms))
    pieces = scatter(terms.reshape(size // RUN, -1, 2 * RANK), planes)
    crossed = section == 2
    sent = jnp.where(crossed, far, out)
    far_before = shift(sent, [([1], 1, 1, run_end), ([2], 0, 1, not_run_end)])
    far_after = shift(sent, [([1], 1, -1, run_start), ([2], 0, -1, not_run_start)])
    pieces, handed_back, before, after = lax.optimization_barrier(
        (pieces, handed_back, before, after)
    )
    terms = jnp.sum(pieces.astype(F32), axis=0)
    terms = jnp.sum(scatter(terms.reshape(RUN, -1, 2 * RANK), columns), axis=0)
    hop = jnp.where(crossed, far, near)
    slot0 = jnp.where(crossed, far_before, before)
    slot2 = jnp.where(crossed, far_after, after)
    dest = destination[0]
    zero = jnp.zeros((), BF16)
    slot0 = jnp.where((dest[jnp.maximum(rank - 1, 0)] == rank) & (rank > 0), slot0, zero)
    slot1 = jnp.where(dest[rank] == rank, hop, zero)
    slot2 = jnp.where(
        (dest[jnp.minimum(rank + 1, size - 1)] == rank) & (rank < size - 1), slot2, zero
    )
    handed_forward = jnp.concatenate([slot0, slot1, slot2], axis=0)[None]
    return (handed_forward, handed_back, terms[None])


def solution(mesh):
    return jax.shard_map(
        shards,
        mesh=mesh,
        in_specs=(
            P("section", "dp", None),
            P("section", "dp", None),
            P("section", "dp", None),
            P("section", None, None),
            P("section", None, None),
            P(),
            P(),
            P(),
            P(),
        ),
        out_specs=(P("section", "dp", None), P("section", "dp", None), P("section", "dp", None)),
        check_vma=False,
    )
```

```python
import functools
import math

import jax
import jax.numpy as jnp
from jax import lax
from jax.experimental import pallas as pl
from jax.experimental.pallas import tpu as pltpu
from jax.sharding import PartitionSpec as P

HEADS = 32
KV = 4
GROUP = HEADS // KV
HEAD_DIM = 128
TILE = 128
SEGS = 8
RANK = 64
QW = HEADS * HEAD_DIM
KW = KV * HEAD_DIM
GW = GROUP * HEAD_DIM
SCALE = 1.0 / math.sqrt(HEAD_DIM)
HALF = QW // 2
RUN = 4
AXES = ("section", "dp")
BF16 = jnp.bfloat16
F32 = jnp.float32


def dot(a, b, dims):
    return lax.dot_general(a, b, (dims, ((), ())), preferred_element_type=F32)


NN = ((1,), (0,))
NT = ((1,), (1,))
TN = ((0,), (0,))


def mask_bias(lens_ref, m, rank):
    shape = (TILE, TILE)
    row = lax.broadcasted_iota(jnp.int32, shape, 0)
    col = lax.broadcasted_iota(jnp.int32, shape, 1)
    seg_row = jnp.zeros(shape, jnp.int32)
    seg_col = jnp.zeros(shape, jnp.int32)
    end = jnp.int32(0)
    for k in range(SEGS):
        end = end + lens_ref[m, rank, k]
        seg_row = seg_row + (row >= end).astype(jnp.int32)
        seg_col = seg_col + (col >= end).astype(jnp.int32)
    allowed = (seg_row == seg_col) & (row >= col)
    return jnp.where(allowed, 0.0, -1e30).astype(F32)


def stacked(ref, base):
    return jnp.concatenate(
        [ref[:, base + h * HEAD_DIM : base + (h + 1) * HEAD_DIM] for h in range(GROUP)], axis=0
    )


def softmax(scores, bias):
    masked = scores + bias
    top = jnp.max(masked, axis=-1, keepdims=True)
    weights = jnp.exp2((masked - top) * (SCALE * math.log2(math.e)))
    return weights * (1.0 / jnp.sum(weights, axis=-1, keepdims=True))


def attend_group(j, qkv_ref, bias, probs_ref):
    keys = qkv_ref[:, QW + j * HEAD_DIM : QW + (j + 1) * HEAD_DIM]
    values = qkv_ref[:, QW + KW + j * HEAD_DIM : QW + KW + (j + 1) * HEAD_DIM]
    queries = stacked(qkv_ref, j * GW)
    probs_ref[...] = dot(queries, keys, NT)
    lows = []
    for h in range(GROUP):
        rows = slice(h * TILE, (h + 1) * TILE)
        probs = softmax(probs_ref[rows, :], bias)
        probs_ref[rows, :] = probs
        lows.append(probs.astype(BF16))
    probs_low = jnp.concatenate(lows, axis=0)
    attn = dot(probs_low, values, NN).astype(BF16)
    return queries, keys, values, probs_low, attn


def forward_kernel(rank_ref, lens_ref, langs_ref, table_ref, qkv_ref, down_ref, up_ref, out_ref, probs_ref):
    rank = rank_ref[0]
    rate = table_ref[langs_ref[0, rank]]
    bias = mask_bias(lens_ref, 0, rank)
    low = jnp.zeros((TILE, RANK), F32)
    for j in range(KV):
        attn = attend_group(j, qkv_ref, bias, probs_ref)[-1]
        for h in range(GROUP):
            cols = slice(j * GW + h * HEAD_DIM, j * GW + (h + 1) * HEAD_DIM)
            out_ref[:, cols] = attn[h * TILE : (h + 1) * TILE]
        low = low + dot(out_ref[:, j * GW : (j + 1) * GW], down_ref[j * GW : (j + 1) * GW, :], NN)
    low = low.astype(BF16)
    for c in range(0, QW, 512):
        lift = dot(low, up_ref[:, c : c + 512], NN)
        out_ref[:, c : c + 512] = (out_ref[:, c : c + 512].astype(F32) + rate * lift).astype(BF16)


def slot_rate(k, rank, tiles, langs_ref, dest_ref, table_ref):
    tile = rank + (k - 1)
    near = jnp.clip(tile, 0, tiles - 1)
    live = (tile == near) & (dest_ref[1, near] == rank)
    return jnp.where(live, table_ref[langs_ref[1, near]], 0.0)


def prepare_kernel(
    place_ref, lens_ref, langs_ref, dest_ref, table_ref, qkv_ref, slots_ref, down_ref, up_ref,
    probs_ref, attn_ref, low_ref, left_ref, own_ref, right_ref,
):
    rank = place_ref[0]
    tiles = lens_ref.shape[1]
    bias = mask_bias(lens_ref, 1, rank)
    low = jnp.zeros((TILE, RANK), F32)
    for j in range(KV):
        block = slice(j * GW, (j + 1) * GW)
        attn = attend_group(j, qkv_ref, bias, probs_ref.at[block, :])[-1]
        for h in range(GROUP):
            cols = slice(j * GW + h * HEAD_DIM, j * GW + (h + 1) * HEAD_DIM)
            attn_ref[:, cols] = attn[h * TILE : (h + 1) * TILE]
        low = low + dot(attn_ref[:, block], down_ref[block, :], NN)
    low_ref[...] = low.astype(BF16)

    @pl.when(place_ref[1] == 0)
    def _():
        for k, out_ref in enumerate((left_ref, own_ref, right_ref)):
            rate = slot_rate(k, rank, tiles, langs_ref, dest_ref, table_ref)
            back = jnp.zeros((TILE, RANK), F32)
            for c in range(0, QW, 512):
                cols = slice(c, c + 512)
                grad = slots_ref[k * TILE : (k + 1) * TILE, cols]
                scaled = (rate * grad.astype(F32)).astype(BF16)
                back = back + dot(scaled, up_ref[:, cols], NT)
            out_ref[...] = jnp.concatenate([low, back], axis=1).astype(BF16)

    @pl.when(place_ref[1] != 0)
    def _():
        for out_ref in (left_ref, own_ref, right_ref):
            out_ref[...] = jnp.zeros(out_ref.shape, BF16)


def terms_kernel(
    place_ref, langs_ref, dest_ref, table_ref, attn_ref, slots_ref, left_ref, own_ref, right_ref,
    scaled_ref, back_ref, low_ref, terms_ref, slot_scaled_ref,
):
    rank = place_ref[0]
    tiles = dest_ref.shape[1]

    @pl.when(place_ref[1] == 0)
    def _():
        went = dest_ref[1, rank] - rank
        back = jnp.where(went < 0, left_ref[...], jnp.where(went > 0, right_ref[...], own_ref[...]))
        lows = jnp.concatenate([left_ref[...], own_ref[...], right_ref[...]], axis=0)
        for c in range(0, QW, 512):
            cols = slice(c, c + 512)
            for k in range(3):
                rows = slice(k * TILE, (k + 1) * TILE)
                rate = slot_rate(k, rank, tiles, langs_ref, dest_ref, table_ref)
                slot_scaled_ref[rows, :] = (rate * slots_ref[rows, cols].astype(F32)).astype(BF16)
            one = dot(attn_ref[:, cols], back, TN)
            two = dot(slot_scaled_ref[...], lows, TN)
            terms = jnp.concatenate([one[:, RANK:], two[:, :RANK]], axis=1)
            terms_ref[cols, :] = terms.astype(terms_ref.dtype)

    @pl.when(place_ref[1] != 0)
    def _():
        for c in range(0, QW, 512):
            cols = slice(c, c + 512)
            one = dot(attn_ref[:, cols], back_ref[...], TN)
            two = dot(scaled_ref[:, cols], low_ref[...], TN)
            terms_ref[cols, :] = jnp.concatenate([one, two], axis=1).astype(terms_ref.dtype)


def backward_kernel(
    place_ref, langs_ref, dest_ref, table_ref, qkv_ref, left_ref, right_ref, last_left_ref,
    last_right_ref, turned_ref, slots_ref, probs_ref, down_ref, up_ref, grad_ref, scaled_ref, back_ref,
    gattn_ref,
):
    rank = place_ref[0]
    rate = table_ref[langs_ref[1, rank]]
    went = dest_ref[1, rank] - rank
    last = place_ref[1] == place_ref[2] - 1

    def chosen():
        back = jnp.zeros((TILE, RANK), F32)
        for c in range(0, QW, 512):
            cols = slice(c, c + 512)
            turned = turned_ref[:, cols]
            left = jnp.where(run_start(rank), turned, last_left_ref[:, cols])
            left = jnp.where(last, left, left_ref[:, cols])
            right = jnp.where(run_end(rank), turned, last_right_ref[:, cols])
            right = jnp.where(last, right, right_ref[:, cols])
            mid = slots_ref[TILE : 2 * TILE, cols]
            grad = jnp.where(went < 0, left, jnp.where(went > 0, right, mid))
            gattn_ref[:, cols] = grad
            scaled = (rate * grad.astype(F32)).astype(BF16)
            scaled_ref[:, cols] = scaled
            back = back + dot(scaled, up_ref[:, cols], NT)
        return back.astype(BF16)

    @pl.when(place_ref[1] != 0)
    def _():
        back = chosen()
        back_ref[...] = back
        for j in range(KV):
            block = slice(j * GW, (j + 1) * GW)
            gattn = gattn_ref[:, block].astype(F32) + dot(back, down_ref[block, :], NT)
            gattn_ref[:, block] = gattn.astype(BF16)
            queries = stacked(qkv_ref, j * GW)
            keys = qkv_ref[:, QW + j * HEAD_DIM : QW + (j + 1) * HEAD_DIM]
            values = qkv_ref[:, QW + KW + j * HEAD_DIM : QW + KW + (j + 1) * HEAD_DIM]
            grads = stacked(gattn_ref, j * GW)
            grad_probs = dot(grads, values, NT)
            lows, scores = [], []
            for h in range(GROUP):
                probs = probs_ref[j * GW + h * TILE : j * GW + (h + 1) * TILE, :]
                lows.append(probs.astype(BF16))
                weighed = probs * grad_probs[h * TILE : (h + 1) * TILE]
                delta = jnp.sum(weighed, axis=-1, keepdims=True)
                scores.append(((weighed - probs * delta) * SCALE).astype(BF16))
            probs_low = jnp.concatenate(lows, axis=0)
            grad_scores = jnp.concatenate(scores, axis=0)
            grad_queries = dot(grad_scores, keys, NN).astype(BF16)
            for h in range(GROUP):
                cols = slice(j * GW + h * HEAD_DIM, j * GW + (h + 1) * HEAD_DIM)
                grad_ref[:, cols] = grad_queries[h * TILE : (h + 1) * TILE]
            cols = slice(QW + j * HEAD_DIM, QW + (j + 1) * HEAD_DIM)
            grad_ref[:, cols] = dot(grad_scores, queries, TN).astype(BF16)
            cols = slice(QW + KW + j * HEAD_DIM, QW + KW + (j + 1) * HEAD_DIM)
            grad_ref[:, cols] = dot(probs_low, grads, TN).astype(BF16)

    @pl.when(place_ref[1] == 0)
    def _():
        grad_ref[...] = jnp.zeros(grad_ref.shape, BF16)
        scaled_ref[...] = jnp.zeros(scaled_ref.shape, BF16)
        back_ref[...] = jnp.zeros(back_ref.shape, BF16)


COST = pl.CostEstimate(flops=2**20, bytes_accessed=2**20, transcendentals=0)
SMEM = pl.BlockSpec(memory_space=pltpu.SMEM)
VMEM = pl.BlockSpec(memory_space=pltpu.VMEM)


def run_forward(rank, lengths, languages, table, qkv, down, up):
    return pl.pallas_call(
        forward_kernel,
        out_shape=jax.ShapeDtypeStruct((TILE, QW), BF16),
        in_specs=[SMEM] * 4 + [VMEM] * 3,
        out_specs=VMEM,
        scratch_shapes=[pltpu.VMEM((GROUP * TILE, TILE), F32)],
        compiler_params=pltpu.CompilerParams(vmem_limit_bytes=24 * 2**20),
        cost_estimate=COST,
        name="forward_tile",
    )(rank, lengths, languages, table, qkv, down, up)


def run_prepare(place, lengths, languages, dest, table, qkv, slots, down, up):
    message = jax.ShapeDtypeStruct((TILE, 2 * RANK), BF16)
    return pl.pallas_call(
        prepare_kernel,
        out_shape=(
            jax.ShapeDtypeStruct((QW, TILE), F32),
            jax.ShapeDtypeStruct((TILE, QW), BF16),
            jax.ShapeDtypeStruct((TILE, RANK), BF16),
            message,
            message,
            message,
        ),
        in_specs=[SMEM] * 5 + [VMEM] * 4,
        out_specs=(VMEM,) * 6,
        compiler_params=pltpu.CompilerParams(vmem_limit_bytes=40 * 2**20),
        cost_estimate=COST,
        name="prepare_tile",
    )(place, lengths, languages, dest, table, qkv, slots, down, up)


def run_terms(place, languages, dest, table, attn, slots, left, own, right, scaled, back, low):
    return pl.pallas_call(
        terms_kernel,
        out_shape=jax.ShapeDtypeStruct((QW, 2 * RANK), BF16),
        in_specs=[SMEM] * 4 + [VMEM] * 8,
        out_specs=VMEM,
        scratch_shapes=[pltpu.VMEM((3 * TILE, 512), BF16)],
        compiler_params=pltpu.CompilerParams(vmem_limit_bytes=40 * 2**20),
        cost_estimate=COST,
        name="adapter_terms",
    )(place, languages, dest, table, attn, slots, left, own, right, scaled, back, low)


def run_backward(place, languages, dest, table, qkv, moved, slots, probs, down, up):
    return pl.pallas_call(
        backward_kernel,
        out_shape=(
            jax.ShapeDtypeStruct((TILE, QW + 2 * KW), BF16),
            jax.ShapeDtypeStruct((TILE, QW), BF16),
            jax.ShapeDtypeStruct((TILE, RANK), BF16),
        ),
        in_specs=[SMEM] * 4 + [VMEM] * 10,
        out_specs=(VMEM,) * 3,
        scratch_shapes=[pltpu.VMEM((TILE, QW), BF16)],
        compiler_params=pltpu.CompilerParams(vmem_limit_bytes=48 * 2**20),
        cost_estimate=COST,
        name="backward_tile",
    )(place, languages, dest, table, qkv, *moved, slots, probs, down, up)


def sections():
    return lax.axis_size("section")


def shift(x, moves):
    size = lax.axis_size("dp")
    route = []
    for s_list, up, step, keep in moves:
        for s in s_list:
            for t in range(size):
                if 0 <= s + up < sections() and 0 <= t + step < size and keep(t):
                    route.append((s * size + t, (s + up) * size + t + step))
    return lax.ppermute(x, AXES, route)


def anywhere(t):
    return True


def run_start(t):
    return t % RUN == 0


def run_end(t):
    return t % RUN == RUN - 1


def after_run_start(t):
    return t % RUN == 1


def before_run_end(t):
    return t % RUN == RUN - 2


def not_run_start(t):
    return t % RUN != 0


def not_run_end(t):
    return t % RUN != RUN - 1


def scatter(x, groups):
    return lax.all_to_all(x, "dp", 0, 0, axis_index_groups=groups, tiled=True)


def shards(
    qkv_a, qkv_b, slot_grad_b, adapter_down, adapter_up, lang_scale, languages, lengths, destination
):
    rank, size = lax.axis_index("dp"), lax.axis_size("dp")
    section, last = lax.axis_index("section"), sections() - 1
    place = jnp.stack([rank, section, jnp.int32(sections())]).astype(jnp.int32)
    down, up = adapter_down[0], adapter_up[0]
    slots = slot_grad_b[0]
    every, early = range(sections()), range(1, last)
    to_up, to_down = slots[2 * TILE :], slots[:TILE]
    from_left = shift(to_up, [(early, 0, 1, anywhere)])
    from_right = shift(to_down, [(early, 0, -1, anywhere)])
    turning = jnp.where(run_end(rank), to_up, to_down)
    turned = shift(turning, [([last], -last, -1, run_end), ([last], -last, 1, run_start)])
    out = run_forward(place, lengths, languages, lang_scale, qkv_a[0], down, up)
    out, place = lax.optimization_barrier((out, place))
    near = shift(
        out, [([0, 2], 1, 0, anywhere), ([1], 1, 1, run_end), ([1], 1, -1, run_start)]
    )
    far_first = shift(out[:, :HALF], [([1], 1, 0, anywhere)])
    probs, attn, low, to_left, own, to_right = run_prepare(
        place, lengths, languages, destination, lang_scale, qkv_b[0], slots, down, up
    )
    from_left, from_right, low = lax.optimization_barrier((from_left, from_right, low))
    to_up, to_down, turned, near, far_first, low = lax.optimization_barrier(
        (to_up, to_down, turned, near, far_first, low)
    )
    last_left = shift(to_up, [([last], 0, 1, not_run_end)])
    last_right = shift(to_down, [([last], 0, -1, not_run_start)])
    turned = shift(turned, [([0], last, 2, before_run_end), ([0], last, -2, after_run_start)])
    grad_qkv, scaled, back = run_backward(
        place, languages, destination, lang_scale, qkv_b[0],
        (from_left, from_right, last_left, last_right, turned), slots, probs, down, up,
    )
    grad_qkv, near, to_left, to_right, out = lax.optimization_barrier(
        (grad_qkv, near, to_left, to_right, out)
    )
    handed_back = shift(grad_qkv, [(every, -1, 0, anywhere)])[None]
    far_second = shift(out[:, HALF:], [([1], 1, 0, anywhere)])
    left = shift(to_right, [([0], 0, 1, anywhere)])
    right = shift(to_left, [([0], 0, -1, anywhere)])
    terms = run_terms(
        place, languages, destination, lang_scale, attn, slots, left, own, right, scaled, back, low
    )
    planes = [[RUN * k + z for k in range(size // RUN)] for z in range(RUN)]
    columns = [[RUN * k + z for z in range(RUN)] for k in range(size // RUN)]
    far_second, terms = lax.optimization_barrier((far_second, terms))
    pieces = scatter(terms.reshape(size // RUN, -1, 2 * RANK), planes)
    crossed = section == 2
    hop = jnp.where(crossed, jnp.concatenate([far_first, far_second], axis=1), near)
    before = shift(hop, [([1, 3], 0, 1, anywhere), ([2], 0, 1, not_run_end)])
    after = shift(hop, [([1, 3], 0, -1, anywhere), ([2], 0, -1, not_run_start)])
    gate = lax.optimization_barrier((pieces, handed_back))
    terms = jnp.sum(gate[0].astype(F32), axis=0)
    terms = jnp.sum(scatter(terms.reshape(RUN, -1, 2 * RANK), columns), axis=0)
    slot0 = jnp.where(crossed & run_start(rank), near, before)
    slot2 = jnp.where(crossed & run_end(rank), near, after)
    dest = destination[0]
    zero = jnp.zeros((), BF16)
    slot0 = jnp.where((dest[jnp.maximum(rank - 1, 0)] == rank) & (rank > 0), slot0, zero)
    slot1 = jnp.where(dest[rank] == rank, hop, zero)
    slot2 = jnp.where(
        (dest[jnp.minimum(rank + 1, size - 1)] == rank) & (rank < size - 1), slot2, zero
    )
    handed_forward = jnp.concatenate([slot0, slot1, slot2], axis=0)[None]
    return (handed_forward, handed_back, terms[None])


def solution(mesh):
    return jax.shard_map(
        shards,
        mesh=mesh,
        in_specs=(
            P("section", "dp", None),
            P("section", "dp", None),
            P("section", "dp", None),
            P("section", None, None),
            P("section", None, None),
            P(),
            P(),
            P(),
            P(),
        ),
        out_specs=(P("section", "dp", None), P("section", "dp", None), P("section", "dp", None)),
        check_vma=False,
    )
```

```python
import functools
import math

import jax
import jax.numpy as jnp
from jax import lax
from jax.experimental import pallas as pl
from jax.experimental.pallas import tpu as pltpu
from jax.sharding import PartitionSpec as P

HEADS = 32
KV = 4
GROUP = HEADS // KV
HEAD_DIM = 128
TILE = 128
SEGS = 8
RANK = 64
QW = HEADS * HEAD_DIM
KW = KV * HEAD_DIM
GW = GROUP * HEAD_DIM
SCALE = 1.0 / math.sqrt(HEAD_DIM)
RUN = 4
AXES = ("section", "dp")
BF16 = jnp.bfloat16
F32 = jnp.float32


def dot(a, b, dims):
    return lax.dot_general(a, b, (dims, ((), ())), preferred_element_type=F32)


NN = ((1,), (0,))
NT = ((1,), (1,))
TN = ((0,), (0,))


def mask_bias(lens_ref, m, rank):
    shape = (TILE, TILE)
    row = lax.broadcasted_iota(jnp.int32, shape, 0)
    col = lax.broadcasted_iota(jnp.int32, shape, 1)
    seg_row = jnp.zeros(shape, jnp.int32)
    seg_col = jnp.zeros(shape, jnp.int32)
    end = jnp.int32(0)
    for k in range(SEGS):
        end = end + lens_ref[m, rank, k]
        seg_row = seg_row + (row >= end).astype(jnp.int32)
        seg_col = seg_col + (col >= end).astype(jnp.int32)
    allowed = (seg_row == seg_col) & (row >= col)
    return jnp.where(allowed, 0.0, -1e30).astype(F32)


def stacked(ref, base):
    return jnp.concatenate(
        [ref[:, base + h * HEAD_DIM : base + (h + 1) * HEAD_DIM] for h in range(GROUP)], axis=0
    )


def softmax(scores, bias):
    masked = scores + bias
    top = jnp.max(masked, axis=-1, keepdims=True)
    weights = jnp.exp2((masked - top) * (SCALE * math.log2(math.e)))
    return weights * (1.0 / jnp.sum(weights, axis=-1, keepdims=True))


def attend_group(j, qkv_ref, bias, probs_ref):
    keys = qkv_ref[:, QW + j * HEAD_DIM : QW + (j + 1) * HEAD_DIM]
    values = qkv_ref[:, QW + KW + j * HEAD_DIM : QW + KW + (j + 1) * HEAD_DIM]
    queries = stacked(qkv_ref, j * GW)
    probs_ref[...] = dot(queries, keys, NT)
    lows = []
    for h in range(GROUP):
        rows = slice(h * TILE, (h + 1) * TILE)
        probs = softmax(probs_ref[rows, :], bias)
        probs_ref[rows, :] = probs
        lows.append(probs.astype(BF16))
    probs_low = jnp.concatenate(lows, axis=0)
    attn = dot(probs_low, values, NN).astype(BF16)
    return queries, keys, values, probs_low, attn


def forward_kernel(rank_ref, lens_ref, langs_ref, table_ref, qkv_ref, down_ref, up_ref, out_ref, probs_ref):
    rank = rank_ref[0]
    rate = table_ref[langs_ref[0, rank]]
    bias = mask_bias(lens_ref, 0, rank)
    low = jnp.zeros((TILE, RANK), F32)
    for j in range(KV):
        attn = attend_group(j, qkv_ref, bias, probs_ref)[-1]
        for h in range(GROUP):
            cols = slice(j * GW + h * HEAD_DIM, j * GW + (h + 1) * HEAD_DIM)
            out_ref[:, cols] = attn[h * TILE : (h + 1) * TILE]
        low = low + dot(out_ref[:, j * GW : (j + 1) * GW], down_ref[j * GW : (j + 1) * GW, :], NN)
    low = low.astype(BF16)
    for c in range(0, QW, 512):
        lift = dot(low, up_ref[:, c : c + 512], NN)
        out_ref[:, c : c + 512] = (out_ref[:, c : c + 512].astype(F32) + rate * lift).astype(BF16)


def slot_rate(k, rank, tiles, langs_ref, dest_ref, table_ref):
    tile = rank + (k - 1)
    near = jnp.clip(tile, 0, tiles - 1)
    live = (tile == near) & (dest_ref[1, near] == rank)
    return jnp.where(live, table_ref[langs_ref[1, near]], 0.0)


def prepare_kernel(
    place_ref, lens_ref, langs_ref, dest_ref, table_ref, qkv_ref, slots_ref, down_ref, up_ref,
    probs_ref, attn_ref, low_ref, left_ref, own_ref, right_ref,
):
    rank = place_ref[0]
    tiles = lens_ref.shape[1]
    bias = mask_bias(lens_ref, 1, rank)
    low = jnp.zeros((TILE, RANK), F32)
    for j in range(KV):
        block = slice(j * GW, (j + 1) * GW)
        attn = attend_group(j, qkv_ref, bias, probs_ref.at[block, :])[-1]
        for h in range(GROUP):
            cols = slice(j * GW + h * HEAD_DIM, j * GW + (h + 1) * HEAD_DIM)
            attn_ref[:, cols] = attn[h * TILE : (h + 1) * TILE]
        low = low + dot(attn_ref[:, block], down_ref[block, :], NN)
    low_ref[...] = low.astype(BF16)

    @pl.when(place_ref[1] == 0)
    def _():
        for k, out_ref in enumerate((left_ref, own_ref, right_ref)):
            rate = slot_rate(k, rank, tiles, langs_ref, dest_ref, table_ref)
            back = jnp.zeros((TILE, RANK), F32)
            for c in range(0, QW, 512):
                cols = slice(c, c + 512)
                grad = slots_ref[k * TILE : (k + 1) * TILE, cols]
                scaled = (rate * grad.astype(F32)).astype(BF16)
                back = back + dot(scaled, up_ref[:, cols], NT)
            out_ref[...] = jnp.concatenate([low, back], axis=1).astype(BF16)

    @pl.when(place_ref[1] != 0)
    def _():
        for out_ref in (left_ref, own_ref, right_ref):
            out_ref[...] = jnp.zeros(out_ref.shape, BF16)


def terms_kernel(
    place_ref, langs_ref, dest_ref, table_ref, attn_ref, slots_ref, left_ref, own_ref, right_ref,
    scaled_ref, back_ref, low_ref, terms_ref, slot_scaled_ref,
):
    rank = place_ref[0]
    tiles = dest_ref.shape[1]

    @pl.when(place_ref[1] == 0)
    def _():
        went = dest_ref[1, rank] - rank
        back = jnp.where(went < 0, left_ref[...], jnp.where(went > 0, right_ref[...], own_ref[...]))
        lows = jnp.concatenate([left_ref[...], own_ref[...], right_ref[...]], axis=0)
        for c in range(0, QW, 512):
            cols = slice(c, c + 512)
            for k in range(3):
                rows = slice(k * TILE, (k + 1) * TILE)
                rate = slot_rate(k, rank, tiles, langs_ref, dest_ref, table_ref)
                slot_scaled_ref[rows, :] = (rate * slots_ref[rows, cols].astype(F32)).astype(BF16)
            one = dot(attn_ref[:, cols], back, TN)
            two = dot(slot_scaled_ref[...], lows, TN)
            terms = jnp.concatenate([one[:, RANK:], two[:, :RANK]], axis=1)
            terms_ref[cols, :] = terms.astype(terms_ref.dtype)

    @pl.when(place_ref[1] != 0)
    def _():
        for c in range(0, QW, 512):
            cols = slice(c, c + 512)
            one = dot(attn_ref[:, cols], back_ref[...], TN)
            two = dot(scaled_ref[:, cols], low_ref[...], TN)
            terms_ref[cols, :] = jnp.concatenate([one, two], axis=1).astype(terms_ref.dtype)


def backward_kernel(
    place_ref, langs_ref, dest_ref, table_ref, qkv_ref, left_ref, right_ref, last_left_ref,
    last_right_ref, slots_ref, probs_ref, down_ref, up_ref, grad_ref, scaled_ref, back_ref,
    gattn_ref,
):
    rank = place_ref[0]
    rate = table_ref[langs_ref[1, rank]]
    went = dest_ref[1, rank] - rank
    last = place_ref[1] == place_ref[2] - 1

    def chosen():
        back = jnp.zeros((TILE, RANK), F32)
        for c in range(0, QW, 512):
            cols = slice(c, c + 512)
            left = jnp.where(last, last_left_ref[:, cols], left_ref[:, cols])
            right = jnp.where(last, last_right_ref[:, cols], right_ref[:, cols])
            mid = slots_ref[TILE : 2 * TILE, cols]
            grad = jnp.where(went < 0, left, jnp.where(went > 0, right, mid))
            gattn_ref[:, cols] = grad
            scaled = (rate * grad.astype(F32)).astype(BF16)
            scaled_ref[:, cols] = scaled
            back = back + dot(scaled, up_ref[:, cols], NT)
        return back.astype(BF16)

    @pl.when(place_ref[1] != 0)
    def _():
        back = chosen()
        back_ref[...] = back
        for j in range(KV):
            block = slice(j * GW, (j + 1) * GW)
            gattn = gattn_ref[:, block].astype(F32) + dot(back, down_ref[block, :], NT)
            gattn_ref[:, block] = gattn.astype(BF16)
            queries = stacked(qkv_ref, j * GW)
            keys = qkv_ref[:, QW + j * HEAD_DIM : QW + (j + 1) * HEAD_DIM]
            values = qkv_ref[:, QW + KW + j * HEAD_DIM : QW + KW + (j + 1) * HEAD_DIM]
            grads = stacked(gattn_ref, j * GW)
            grad_probs = dot(grads, values, NT)
            lows, scores = [], []
            for h in range(GROUP):
                probs = probs_ref[j * GW + h * TILE : j * GW + (h + 1) * TILE, :]
                lows.append(probs.astype(BF16))
                weighed = probs * grad_probs[h * TILE : (h + 1) * TILE]
                delta = jnp.sum(weighed, axis=-1, keepdims=True)
                scores.append(((weighed - probs * delta) * SCALE).astype(BF16))
            probs_low = jnp.concatenate(lows, axis=0)
            grad_scores = jnp.concatenate(scores, axis=0)
            grad_queries = dot(grad_scores, keys, NN).astype(BF16)
            for h in range(GROUP):
                cols = slice(j * GW + h * HEAD_DIM, j * GW + (h + 1) * HEAD_DIM)
                grad_ref[:, cols] = grad_queries[h * TILE : (h + 1) * TILE]
            cols = slice(QW + j * HEAD_DIM, QW + (j + 1) * HEAD_DIM)
            grad_ref[:, cols] = dot(grad_scores, queries, TN).astype(BF16)
            cols = slice(QW + KW + j * HEAD_DIM, QW + KW + (j + 1) * HEAD_DIM)
            grad_ref[:, cols] = dot(probs_low, grads, TN).astype(BF16)

    @pl.when(place_ref[1] == 0)
    def _():
        grad_ref[...] = jnp.zeros(grad_ref.shape, BF16)
        scaled_ref[...] = jnp.zeros(scaled_ref.shape, BF16)
        back_ref[...] = jnp.zeros(back_ref.shape, BF16)


COST = pl.CostEstimate(flops=2**20, bytes_accessed=2**20, transcendentals=0)
SMEM = pl.BlockSpec(memory_space=pltpu.SMEM)
VMEM = pl.BlockSpec(memory_space=pltpu.VMEM)


def run_forward(rank, lengths, languages, table, qkv, down, up):
    return pl.pallas_call(
        forward_kernel,
        out_shape=jax.ShapeDtypeStruct((TILE, QW), BF16),
        in_specs=[SMEM] * 4 + [VMEM] * 3,
        out_specs=VMEM,
        scratch_shapes=[pltpu.VMEM((GROUP * TILE, TILE), F32)],
        compiler_params=pltpu.CompilerParams(vmem_limit_bytes=24 * 2**20),
        cost_estimate=COST,
        name="forward_tile",
    )(rank, lengths, languages, table, qkv, down, up)


def run_prepare(place, lengths, languages, dest, table, qkv, slots, down, up):
    message = jax.ShapeDtypeStruct((TILE, 2 * RANK), BF16)
    return pl.pallas_call(
        prepare_kernel,
        out_shape=(
            jax.ShapeDtypeStruct((QW, TILE), F32),
            jax.ShapeDtypeStruct((TILE, QW), BF16),
            jax.ShapeDtypeStruct((TILE, RANK), BF16),
            message,
            message,
            message,
        ),
        in_specs=[SMEM] * 5 + [VMEM] * 4,
        out_specs=(VMEM,) * 6,
        compiler_params=pltpu.CompilerParams(vmem_limit_bytes=40 * 2**20),
        cost_estimate=COST,
        name="prepare_tile",
    )(place, lengths, languages, dest, table, qkv, slots, down, up)


def run_terms(place, languages, dest, table, attn, slots, left, own, right, scaled, back, low):
    return pl.pallas_call(
        terms_kernel,
        out_shape=jax.ShapeDtypeStruct((QW, 2 * RANK), BF16),
        in_specs=[SMEM] * 4 + [VMEM] * 8,
        out_specs=VMEM,
        scratch_shapes=[pltpu.VMEM((3 * TILE, 512), BF16)],
        compiler_params=pltpu.CompilerParams(vmem_limit_bytes=40 * 2**20),
        cost_estimate=COST,
        name="adapter_terms",
    )(place, languages, dest, table, attn, slots, left, own, right, scaled, back, low)


def run_backward(place, languages, dest, table, qkv, moved, slots, probs, down, up):
    return pl.pallas_call(
        backward_kernel,
        out_shape=(
            jax.ShapeDtypeStruct((TILE, QW + 2 * KW), BF16),
            jax.ShapeDtypeStruct((TILE, QW), BF16),
            jax.ShapeDtypeStruct((TILE, RANK), BF16),
        ),
        in_specs=[SMEM] * 4 + [VMEM] * 9,
        out_specs=(VMEM,) * 3,
        scratch_shapes=[pltpu.VMEM((TILE, QW), BF16)],
        compiler_params=pltpu.CompilerParams(vmem_limit_bytes=48 * 2**20),
        cost_estimate=COST,
        name="backward_tile",
    )(place, languages, dest, table, qkv, *moved, slots, probs, down, up)


def place_kernel(
    place_ref, dest_ref, before_ref, hop_ref, after_ref, ends_ref, back_ref,
    placed_ref, handed_ref, zero_ref, sems,
):
    rank, section = place_ref[0], place_ref[1]
    tiles = dest_ref.shape[1]
    zero_ref[...] = jnp.zeros(zero_ref.shape, BF16)
    handed = pltpu.make_async_copy(back_ref, handed_ref, sems.at[0])
    handed.start()
    copies = []
    for k, (near_ref, edge) in enumerate(
        ((before_ref, run_start(rank)), (hop_ref, False), (after_ref, run_end(rank)))
    ):
        tile = rank + (k - 1)
        held = jnp.clip(tile, 0, tiles - 1)
        live = (tile == held) & (dest_ref[0, held] == rank) & (section > 0)
        crossed = (section == 2) & edge
        slot = placed_ref.at[pl.ds(k * TILE, TILE), :]
        for source, chosen in (
            (near_ref, live & jnp.logical_not(crossed)),
            (ends_ref, live & crossed),
            (zero_ref, jnp.logical_not(live)),
        ):
            copy = pltpu.make_async_copy(source, slot, sems.at[k + 1])
            copies.append((copy, chosen))
    for copy, chosen in copies:
        pl.when(chosen)(copy.start)
    for copy, chosen in copies:
        pl.when(chosen)(copy.wait)
    handed.wait()


def run_place(place, dest, before, hop, after, ends, back):
    hbm = pl.BlockSpec(memory_space=pl.ANY)
    return pl.pallas_call(
        place_kernel,
        out_shape=(
            jax.ShapeDtypeStruct((3 * TILE, QW), BF16),
            jax.ShapeDtypeStruct(back.shape, BF16),
        ),
        in_specs=[SMEM] * 2 + [VMEM] * 5,
        out_specs=(hbm, hbm),
        scratch_shapes=[pltpu.VMEM((TILE, QW), BF16), pltpu.SemaphoreType.DMA((4,))],
        compiler_params=pltpu.CompilerParams(vmem_limit_bytes=24 * 2**20),
        cost_estimate=COST,
        name="place_outputs",
    )(place, dest, before, hop, after, ends, back)


def sections():
    return lax.axis_size("section")


def shift(x, moves):
    size = lax.axis_size("dp")
    route = []
    for s_list, up, step, keep in moves:
        for s in s_list:
            for t in range(size):
                if 0 <= s + up < sections() and 0 <= t + step < size and keep(t):
                    route.append((s * size + t, (s + up) * size + t + step))
    return lax.ppermute(x, AXES, route)


def anywhere(t):
    return True


def run_start(t):
    return t % RUN == 0


def run_end(t):
    return t % RUN == RUN - 1


def not_run_start(t):
    return t % RUN != 0


def not_run_end(t):
    return t % RUN != RUN - 1


def scatter(x, groups):
    return lax.all_to_all(x, "dp", 0, 0, axis_index_groups=groups, tiled=True)


def shards(
    qkv_a, qkv_b, slot_grad_b, adapter_down, adapter_up, lang_scale, languages, lengths, destination
):
    rank, size = lax.axis_index("dp"), lax.axis_size("dp")
    section, last = lax.axis_index("section"), sections() - 1
    place = jnp.stack([rank, section, jnp.int32(sections())]).astype(jnp.int32)
    down, up = adapter_down[0], adapter_up[0]
    slots = slot_grad_b[0]
    every, early = range(sections()), range(1, last)
    to_up, to_down = slots[2 * TILE :], slots[:TILE]
    from_left = shift(to_up, [(early, 0, 1, anywhere)])
    from_right = shift(to_down, [(early, 0, -1, anywhere)])
    out = run_forward(place, lengths, languages, lang_scale, qkv_a[0], down, up)
    out, place = lax.optimization_barrier((out, place))
    hop = shift(out, [(every, 1, 0, anywhere)])
    probs, attn, low, to_left, own, to_right = run_prepare(
        place, lengths, languages, destination, lang_scale, qkv_b[0], slots, down, up
    )
    from_left, from_right, low = lax.optimization_barrier((from_left, from_right, low))
    to_up, to_down, hop, low = lax.optimization_barrier((to_up, to_down, hop, low))
    last_left = shift(to_up, [([last], 0, 1, anywhere)])
    last_right = shift(to_down, [([last], 0, -1, anywhere)])
    grad_qkv, scaled, back = run_backward(
        place, languages, destination, lang_scale, qkv_b[0],
        (from_left, from_right, last_left, last_right), slots, probs, down, up,
    )
    grad_qkv, hop, to_left, to_right, out = lax.optimization_barrier(
        (grad_qkv, hop, to_left, to_right, out)
    )
    handed_back = shift(grad_qkv, [(every, -1, 0, anywhere)])
    ends = shift(out, [([1], 1, 1, run_end), ([1], 1, -1, run_start)])
    before = shift(hop, [([1, 3], 0, 1, anywhere), ([2], 0, 1, not_run_end)])
    after = shift(hop, [([1, 3], 0, -1, anywhere), ([2], 0, -1, not_run_start)])
    left = shift(to_right, [([0], 0, 1, anywhere)])
    right = shift(to_left, [([0], 0, -1, anywhere)])
    terms = run_terms(
        place, languages, destination, lang_scale, attn, slots, left, own, right, scaled, back, low
    )
    planes = [[RUN * k + z for k in range(size // RUN)] for z in range(RUN)]
    columns = [[RUN * k + z for z in range(RUN)] for k in range(size // RUN)]
    pieces = scatter(terms.reshape(size // RUN, -1, 2 * RANK), planes)
    pieces, gated, before = lax.optimization_barrier((pieces, handed_back, before))
    terms = jnp.sum(pieces.astype(F32), axis=0)
    terms = jnp.sum(scatter(terms.reshape(RUN, -1, 2 * RANK), columns), axis=0)
    handed_forward, handed_back = run_place(
        place, destination, before, hop, after, ends, handed_back
    )
    return (handed_forward[None], handed_back[None], terms[None])


def solution(mesh):
    return jax.shard_map(
        shards,
        mesh=mesh,
        in_specs=(
            P("section", "dp", None),
            P("section", "dp", None),
            P("section", "dp", None),
            P("section", None, None),
            P("section", None, None),
            P(),
            P(),
            P(),
            P(),
        ),
        out_specs=(P("section", "dp", None), P("section", "dp", None), P("section", "dp", None)),
        check_vma=False,
    )
```

```python
import functools
import math

import jax
import jax.numpy as jnp
from jax import lax
from jax.experimental import pallas as pl
from jax.experimental.pallas import tpu as pltpu
from jax.sharding import PartitionSpec as P

HEADS = 32
KV = 4
GROUP = HEADS // KV
HEAD_DIM = 128
TILE = 128
SEGS = 8
RANK = 64
QW = HEADS * HEAD_DIM
KW = KV * HEAD_DIM
GW = GROUP * HEAD_DIM
SCALE = 1.0 / math.sqrt(HEAD_DIM)
RUN = 4
AXES = ("section", "dp")
BF16 = jnp.bfloat16
F32 = jnp.float32


def dot(a, b, dims):
    return lax.dot_general(a, b, (dims, ((), ())), preferred_element_type=F32)


NN = ((1,), (0,))
NT = ((1,), (1,))
TN = ((0,), (0,))


def mask_bias(lens_ref, m, rank):
    shape = (TILE, TILE)
    row = lax.broadcasted_iota(jnp.int32, shape, 0)
    col = lax.broadcasted_iota(jnp.int32, shape, 1)
    seg_row = jnp.zeros(shape, jnp.int32)
    seg_col = jnp.zeros(shape, jnp.int32)
    end = jnp.int32(0)
    for k in range(SEGS):
        end = end + lens_ref[m, rank, k]
        seg_row = seg_row + (row >= end).astype(jnp.int32)
        seg_col = seg_col + (col >= end).astype(jnp.int32)
    allowed = (seg_row == seg_col) & (row >= col)
    return jnp.where(allowed, 0.0, -1e30).astype(F32)


def stacked(ref, base):
    return jnp.concatenate(
        [ref[:, base + h * HEAD_DIM : base + (h + 1) * HEAD_DIM] for h in range(GROUP)], axis=0
    )


def softmax(scores, bias):
    masked = scores + bias
    top = jnp.max(masked, axis=-1, keepdims=True)
    weights = jnp.exp2((masked - top) * (SCALE * math.log2(math.e)))
    return weights * (1.0 / jnp.sum(weights, axis=-1, keepdims=True))


def attend_group(j, qkv_ref, bias, probs_ref):
    keys = qkv_ref[:, QW + j * HEAD_DIM : QW + (j + 1) * HEAD_DIM]
    values = qkv_ref[:, QW + KW + j * HEAD_DIM : QW + KW + (j + 1) * HEAD_DIM]
    queries = stacked(qkv_ref, j * GW)
    probs_ref[...] = dot(queries, keys, NT)
    lows = []
    for h in range(GROUP):
        rows = slice(h * TILE, (h + 1) * TILE)
        probs = softmax(probs_ref[rows, :], bias)
        probs_ref[rows, :] = probs
        lows.append(probs.astype(BF16))
    probs_low = jnp.concatenate(lows, axis=0)
    attn = dot(probs_low, values, NN).astype(BF16)
    return queries, keys, values, probs_low, attn


def forward_kernel(rank_ref, lens_ref, langs_ref, table_ref, qkv_ref, down_ref, up_ref, out_ref, probs_ref):
    rank = rank_ref[0]
    rate = table_ref[langs_ref[0, rank]]
    bias = mask_bias(lens_ref, 0, rank)
    low = jnp.zeros((TILE, RANK), F32)
    for j in range(KV):
        attn = attend_group(j, qkv_ref, bias, probs_ref)[-1]
        for h in range(GROUP):
            cols = slice(j * GW + h * HEAD_DIM, j * GW + (h + 1) * HEAD_DIM)
            out_ref[:, cols] = attn[h * TILE : (h + 1) * TILE]
        low = low + dot(out_ref[:, j * GW : (j + 1) * GW], down_ref[j * GW : (j + 1) * GW, :], NN)
    low = low.astype(BF16)
    for c in range(0, QW, 512):
        lift = dot(low, up_ref[:, c : c + 512], NN)
        out_ref[:, c : c + 512] = (out_ref[:, c : c + 512].astype(F32) + rate * lift).astype(BF16)


def slot_rate(k, rank, tiles, langs_ref, dest_ref, table_ref):
    tile = rank + (k - 1)
    near = jnp.clip(tile, 0, tiles - 1)
    live = (tile == near) & (dest_ref[1, near] == rank)
    return jnp.where(live, table_ref[langs_ref[1, near]], 0.0)


def prepare_kernel(
    place_ref, lens_ref, langs_ref, dest_ref, table_ref, qkv_ref, slots_ref, down_ref, up_ref,
    probs_ref, attn_ref, low_ref, left_ref, own_ref, right_ref,
):
    rank = place_ref[0]
    tiles = lens_ref.shape[1]
    bias = mask_bias(lens_ref, 1, rank)
    low = jnp.zeros((TILE, RANK), F32)
    for j in range(KV):
        block = slice(j * GW, (j + 1) * GW)
        attn = attend_group(j, qkv_ref, bias, probs_ref.at[block, :])[-1]
        for h in range(GROUP):
            cols = slice(j * GW + h * HEAD_DIM, j * GW + (h + 1) * HEAD_DIM)
            attn_ref[:, cols] = attn[h * TILE : (h + 1) * TILE]
        low = low + dot(attn_ref[:, block], down_ref[block, :], NN)
    low_ref[...] = low.astype(BF16)

    @pl.when(place_ref[1] == 0)
    def _():
        for k, out_ref in enumerate((left_ref, own_ref, right_ref)):
            rate = slot_rate(k, rank, tiles, langs_ref, dest_ref, table_ref)
            back = jnp.zeros((TILE, RANK), F32)
            for c in range(0, QW, 512):
                cols = slice(c, c + 512)
                grad = slots_ref[k * TILE : (k + 1) * TILE, cols]
                scaled = (rate * grad.astype(F32)).astype(BF16)
                back = back + dot(scaled, up_ref[:, cols], NT)
            out_ref[...] = jnp.concatenate([low, back], axis=1).astype(BF16)

    @pl.when(place_ref[1] != 0)
    def _():
        for out_ref in (left_ref, own_ref, right_ref):
            out_ref[...] = jnp.zeros(out_ref.shape, BF16)


def terms_kernel(
    place_ref, langs_ref, dest_ref, table_ref, attn_ref, slots_ref, left_ref, own_ref, right_ref,
    one_scaled_ref, one_back_ref, more_scaled_ref, more_back_ref, low_ref, terms_ref,
    slot_scaled_ref,
):
    rank = place_ref[0]
    tiles = dest_ref.shape[1]

    @pl.when(place_ref[1] == 0)
    def _():
        went = dest_ref[1, rank] - rank
        back = jnp.where(went < 0, left_ref[...], jnp.where(went > 0, right_ref[...], own_ref[...]))
        lows = jnp.concatenate([left_ref[...], own_ref[...], right_ref[...]], axis=0)
        for c in range(0, QW, 512):
            cols = slice(c, c + 512)
            for k in range(3):
                rows = slice(k * TILE, (k + 1) * TILE)
                rate = slot_rate(k, rank, tiles, langs_ref, dest_ref, table_ref)
                slot_scaled_ref[rows, :] = (rate * slots_ref[rows, cols].astype(F32)).astype(BF16)
            one = dot(attn_ref[:, cols], back, TN)
            two = dot(slot_scaled_ref[...], lows, TN)
            terms = jnp.concatenate([one[:, RANK:], two[:, :RANK]], axis=1)
            terms_ref[cols, :] = terms.astype(terms_ref.dtype)

    def at_home(scaled_ref, back_ref):
        for c in range(0, QW, 512):
            cols = slice(c, c + 512)
            one = dot(attn_ref[:, cols], back_ref[...], TN)
            two = dot(scaled_ref[:, cols], low_ref[...], TN)
            terms_ref[cols, :] = jnp.concatenate([one, two], axis=1).astype(terms_ref.dtype)

    @pl.when(place_ref[1] == 2)
    def _():
        at_home(one_scaled_ref, one_back_ref)

    @pl.when((place_ref[1] != 0) & (place_ref[1] != 2))
    def _():
        at_home(more_scaled_ref, more_back_ref)


def backward_kernel(
    wanted, place_ref, langs_ref, dest_ref, table_ref, qkv_ref, left_ref, right_ref, more_left_ref,
    more_right_ref, slots_ref, probs_ref, down_ref, up_ref, grad_ref, scaled_ref, back_ref,
    gattn_ref,
):
    rank = place_ref[0]
    rate = table_ref[langs_ref[1, rank]]
    went = dest_ref[1, rank] - rank
    more = place_ref[1] == place_ref[2] - 1
    active = functools.reduce(jnp.logical_or, [place_ref[1] == s for s in wanted])

    def chosen():
        back = jnp.zeros((TILE, RANK), F32)
        for c in range(0, QW, 512):
            cols = slice(c, c + 512)
            left, right = left_ref[:, cols], right_ref[:, cols]
            if more_left_ref is not None:
                left = jnp.where(more, more_left_ref[:, cols], left)
                right = jnp.where(more, more_right_ref[:, cols], right)
            mid = slots_ref[TILE : 2 * TILE, cols]
            grad = jnp.where(went < 0, left, jnp.where(went > 0, right, mid))
            gattn_ref[:, cols] = grad
            scaled = (rate * grad.astype(F32)).astype(BF16)
            scaled_ref[:, cols] = scaled
            back = back + dot(scaled, up_ref[:, cols], NT)
        return back.astype(BF16)

    @pl.when(active)
    def _():
        back = chosen()
        back_ref[...] = back
        for j in range(KV):
            block = slice(j * GW, (j + 1) * GW)
            gattn = gattn_ref[:, block].astype(F32) + dot(back, down_ref[block, :], NT)
            gattn_ref[:, block] = gattn.astype(BF16)
            queries = stacked(qkv_ref, j * GW)
            keys = qkv_ref[:, QW + j * HEAD_DIM : QW + (j + 1) * HEAD_DIM]
            values = qkv_ref[:, QW + KW + j * HEAD_DIM : QW + KW + (j + 1) * HEAD_DIM]
            grads = stacked(gattn_ref, j * GW)
            grad_probs = dot(grads, values, NT)
            lows, scores = [], []
            for h in range(GROUP):
                probs = probs_ref[j * GW + h * TILE : j * GW + (h + 1) * TILE, :]
                lows.append(probs.astype(BF16))
                weighed = probs * grad_probs[h * TILE : (h + 1) * TILE]
                delta = jnp.sum(weighed, axis=-1, keepdims=True)
                scores.append(((weighed - probs * delta) * SCALE).astype(BF16))
            probs_low = jnp.concatenate(lows, axis=0)
            grad_scores = jnp.concatenate(scores, axis=0)
            grad_queries = dot(grad_scores, keys, NN).astype(BF16)
            for h in range(GROUP):
                cols = slice(j * GW + h * HEAD_DIM, j * GW + (h + 1) * HEAD_DIM)
                grad_ref[:, cols] = grad_queries[h * TILE : (h + 1) * TILE]
            cols = slice(QW + j * HEAD_DIM, QW + (j + 1) * HEAD_DIM)
            grad_ref[:, cols] = dot(grad_scores, queries, TN).astype(BF16)
            cols = slice(QW + KW + j * HEAD_DIM, QW + KW + (j + 1) * HEAD_DIM)
            grad_ref[:, cols] = dot(probs_low, grads, TN).astype(BF16)

    @pl.when(jnp.logical_not(active))
    def _():
        scaled_ref[...] = jnp.zeros(scaled_ref.shape, BF16)
        back_ref[...] = jnp.zeros(back_ref.shape, BF16)


def backward_one_kernel(wanted, *refs):
    backward_kernel(wanted, *refs[:7], None, None, *refs[7:])


COST = pl.CostEstimate(flops=2**20, bytes_accessed=2**20, transcendentals=0)
SMEM = pl.BlockSpec(memory_space=pltpu.SMEM)
VMEM = pl.BlockSpec(memory_space=pltpu.VMEM)


def run_forward(rank, lengths, languages, table, qkv, down, up):
    return pl.pallas_call(
        forward_kernel,
        out_shape=jax.ShapeDtypeStruct((TILE, QW), BF16),
        in_specs=[SMEM] * 4 + [VMEM] * 3,
        out_specs=VMEM,
        scratch_shapes=[pltpu.VMEM((GROUP * TILE, TILE), F32)],
        compiler_params=pltpu.CompilerParams(vmem_limit_bytes=24 * 2**20),
        cost_estimate=COST,
        name="forward_tile",
    )(rank, lengths, languages, table, qkv, down, up)


def run_prepare(place, lengths, languages, dest, table, qkv, slots, down, up):
    message = jax.ShapeDtypeStruct((TILE, 2 * RANK), BF16)
    return pl.pallas_call(
        prepare_kernel,
        out_shape=(
            jax.ShapeDtypeStruct((QW, TILE), F32),
            jax.ShapeDtypeStruct((TILE, QW), BF16),
            jax.ShapeDtypeStruct((TILE, RANK), BF16),
            message,
            message,
            message,
        ),
        in_specs=[SMEM] * 5 + [VMEM] * 4,
        out_specs=(VMEM,) * 6,
        compiler_params=pltpu.CompilerParams(vmem_limit_bytes=40 * 2**20),
        cost_estimate=COST,
        name="prepare_tile",
    )(place, lengths, languages, dest, table, qkv, slots, down, up)


def run_terms(place, languages, dest, table, attn, slots, left, own, right, one, more, low):
    return pl.pallas_call(
        terms_kernel,
        out_shape=jax.ShapeDtypeStruct((QW, 2 * RANK), BF16),
        in_specs=[SMEM] * 4 + [VMEM] * 10,
        out_specs=VMEM,
        scratch_shapes=[pltpu.VMEM((3 * TILE, 512), BF16)],
        compiler_params=pltpu.CompilerParams(vmem_limit_bytes=40 * 2**20),
        cost_estimate=COST,
        name="adapter_terms",
    )(place, languages, dest, table, attn, slots, left, own, right, *one, *more, low)


def run_backward(wanted, place, languages, dest, table, qkv, moved, slots, probs, down, up):
    kernel = backward_one_kernel if len(moved) == 2 else backward_kernel
    return pl.pallas_call(
        functools.partial(kernel, wanted),
        out_shape=(
            jax.ShapeDtypeStruct((TILE, QW + 2 * KW), BF16),
            jax.ShapeDtypeStruct((TILE, QW), BF16),
            jax.ShapeDtypeStruct((TILE, RANK), BF16),
        ),
        in_specs=[SMEM] * 4 + [VMEM] * (5 + len(moved)),
        out_specs=(VMEM,) * 3,
        scratch_shapes=[pltpu.VMEM((TILE, QW), BF16)],
        compiler_params=pltpu.CompilerParams(vmem_limit_bytes=48 * 2**20),
        cost_estimate=COST,
        name="backward_tile",
    )(place, languages, dest, table, qkv, *moved, slots, probs, down, up)


def place_kernel(
    place_ref, dest_ref, before_ref, near_ref, after_ref, far_before_ref, far_ref, far_after_ref,
    back_one_ref, back_more_ref, placed_ref, handed_ref, zero_ref, sems,
):
    rank, section = place_ref[0], place_ref[1]
    tiles = dest_ref.shape[1]
    zero_ref[...] = jnp.zeros(zero_ref.shape, BF16)
    copies = [
        (pltpu.make_async_copy(back_one_ref, handed_ref, sems.at[0]), section == 1),
        (pltpu.make_async_copy(back_more_ref, handed_ref, sems.at[0]), section != 1),
    ]
    for k, (near, far) in enumerate(
        ((before_ref, far_before_ref), (near_ref, far_ref), (after_ref, far_after_ref))
    ):
        tile = rank + (k - 1)
        held = jnp.clip(tile, 0, tiles - 1)
        live = (tile == held) & (dest_ref[0, held] == rank) & (section > 0)
        slot = placed_ref.at[pl.ds(k * TILE, TILE), :]
        for source, chosen in (
            (near, live & (section != 2)),
            (far, live & (section == 2)),
            (zero_ref, jnp.logical_not(live)),
        ):
            copies.append((pltpu.make_async_copy(source, slot, sems.at[k + 1]), chosen))
    for copy, chosen in copies:
        pl.when(chosen)(copy.start)
    for copy, chosen in copies:
        pl.when(chosen)(copy.wait)


def run_place(place, dest, *tiles):
    hbm = pl.BlockSpec(memory_space=pl.ANY)
    return pl.pallas_call(
        place_kernel,
        out_shape=(
            jax.ShapeDtypeStruct((3 * TILE, QW), BF16),
            jax.ShapeDtypeStruct(tiles[-1].shape, BF16),
        ),
        in_specs=[SMEM] * 2 + [VMEM] * len(tiles),
        out_specs=(hbm, hbm),
        scratch_shapes=[pltpu.VMEM((TILE, QW), BF16), pltpu.SemaphoreType.DMA((4,))],
        compiler_params=pltpu.CompilerParams(vmem_limit_bytes=24 * 2**20),
        cost_estimate=COST,
        name="place_outputs",
    )(place, dest, *tiles)


def sections():
    return lax.axis_size("section")


def shift(x, moves):
    size = lax.axis_size("dp")
    route = []
    for s_list, up, step, keep in moves:
        for s in s_list:
            for t in range(size):
                if 0 <= s + up < sections() and 0 <= t + step < size and keep(t):
                    route.append((s * size + t, (s + up) * size + t + step))
    return lax.ppermute(x, AXES, route)


def anywhere(t):
    return True


def run_start(t):
    return t % RUN == 0


def run_end(t):
    return t % RUN == RUN - 1


def not_run_start(t):
    return t % RUN != 0


def not_run_end(t):
    return t % RUN != RUN - 1


def scatter(x, groups):
    return lax.all_to_all(x, "dp", 0, 0, axis_index_groups=groups, tiled=True)


def shards(
    qkv_a, qkv_b, slot_grad_b, adapter_down, adapter_up, lang_scale, languages, lengths, destination
):
    rank, size = lax.axis_index("dp"), lax.axis_size("dp")
    section, last = lax.axis_index("section"), sections() - 1
    place = jnp.stack([rank, section, jnp.int32(sections())]).astype(jnp.int32)
    down, up = adapter_down[0], adapter_up[0]
    slots = slot_grad_b[0]
    every, early = range(sections()), range(1, last)
    to_up, to_down = slots[2 * TILE :], slots[:TILE]
    from_left = shift(to_up, [(early, 0, 1, anywhere)])
    from_right = shift(to_down, [(early, 0, -1, anywhere)])
    out = run_forward(place, lengths, languages, lang_scale, qkv_a[0], down, up)
    out, place = lax.optimization_barrier((out, place))
    near = shift(out, [([0, 2], 1, 0, anywhere)])
    far = shift(out, [([1], 1, 0, anywhere)])
    probs, attn, low, to_left, own, to_right = run_prepare(
        place, lengths, languages, destination, lang_scale, qkv_b[0], slots, down, up
    )
    from_left, from_right, low = lax.optimization_barrier((from_left, from_right, low))
    to_up, to_down, near, low = lax.optimization_barrier((to_up, to_down, near, low))
    last_left = shift(to_up, [([last], 0, 1, anywhere)])
    last_right = shift(to_down, [([last], 0, -1, anywhere)])
    shared = (place, languages, destination, lang_scale, qkv_b[0])
    grad_one, *one = run_backward((2,), *shared, (from_left, from_right), slots, probs, down, up)
    back_one = shift(grad_one, [([2], -1, 0, anywhere)])
    grad_more, *more = run_backward(
        (1, 3), *shared, (from_left, from_right, last_left, last_right), slots, probs, down, up
    )
    grad_more, near, to_left, to_right = lax.optimization_barrier(
        (grad_more, near, to_left, to_right)
    )
    back_more = shift(grad_more, [([1, 3], -1, 0, anywhere)])
    before = shift(near, [([1, 3], 0, 1, anywhere)])
    after = shift(near, [([1, 3], 0, -1, anywhere)])
    left = shift(to_right, [([0], 0, 1, anywhere)])
    right = shift(to_left, [([0], 0, -1, anywhere)])
    terms = run_terms(
        place, languages, destination, lang_scale, attn, slots, left, own, right, one, more, low
    )
    planes = [[RUN * k + z for k in range(size // RUN)] for z in range(RUN)]
    columns = [[RUN * k + z for z in range(RUN)] for k in range(size // RUN)]
    far, terms = lax.optimization_barrier((far, terms))
    pieces = scatter(terms.reshape(size // RUN, -1, 2 * RANK), planes)
    sent = jnp.where(section == 2, far, out)
    far_before = shift(sent, [([1], 1, 1, run_end), ([2], 0, 1, not_run_end)])
    far_after = shift(sent, [([1], 1, -1, run_start), ([2], 0, -1, not_run_start)])
    pieces, _, before, after = lax.optimization_barrier((pieces, back_one, before, after))
    terms = jnp.sum(pieces.astype(F32), axis=0)
    terms = jnp.sum(scatter(terms.reshape(RUN, -1, 2 * RANK), columns), axis=0)
    handed_forward, handed_back = run_place(
        place, destination, before, near, after, far_before, far, far_after, back_one, back_more
    )
    return (handed_forward[None], handed_back[None], terms[None])


def solution(mesh):
    return jax.shard_map(
        shards,
        mesh=mesh,
        in_specs=(
            P("section", "dp", None),
            P("section", "dp", None),
            P("section", "dp", None),
            P("section", None, None),
            P("section", None, None),
            P(),
            P(),
            P(),
            P(),
        ),
        out_specs=(P("section", "dp", None), P("section", "dp", None), P("section", "dp", None)),
        check_vma=False,
    )
```

```python
import functools
import math

import jax
import jax.numpy as jnp
from jax import lax
from jax.experimental import pallas as pl
from jax.experimental.pallas import tpu as pltpu
from jax.sharding import PartitionSpec as P

HEADS = 32
KV = 4
GROUP = HEADS // KV
HEAD_DIM = 128
TILE = 128
SEGS = 8
RANK = 64
QW = HEADS * HEAD_DIM
KW = KV * HEAD_DIM
GW = GROUP * HEAD_DIM
SCALE = 1.0 / math.sqrt(HEAD_DIM)
RUN = 4
AXES = ("section", "dp")
BF16 = jnp.bfloat16
F32 = jnp.float32


def dot(a, b, dims):
    return lax.dot_general(a, b, (dims, ((), ())), preferred_element_type=F32)


NN = ((1,), (0,))
NT = ((1,), (1,))
TN = ((0,), (0,))


def mask_bias(lens_ref, m, rank):
    shape = (TILE, TILE)
    row = lax.broadcasted_iota(jnp.int32, shape, 0)
    col = lax.broadcasted_iota(jnp.int32, shape, 1)
    seg_row = jnp.zeros(shape, jnp.int32)
    seg_col = jnp.zeros(shape, jnp.int32)
    end = jnp.int32(0)
    for k in range(SEGS):
        end = end + lens_ref[m, rank, k]
        seg_row = seg_row + (row >= end).astype(jnp.int32)
        seg_col = seg_col + (col >= end).astype(jnp.int32)
    allowed = (seg_row == seg_col) & (row >= col)
    return jnp.where(allowed, 0.0, -1e30).astype(F32)


def stacked(ref, base):
    return jnp.concatenate(
        [ref[:, base + h * HEAD_DIM : base + (h + 1) * HEAD_DIM] for h in range(GROUP)], axis=0
    )


def softmax(scores, bias):
    masked = scores + bias
    top = jnp.max(masked, axis=-1, keepdims=True)
    weights = jnp.exp2((masked - top) * (SCALE * math.log2(math.e)))
    return weights * (1.0 / jnp.sum(weights, axis=-1, keepdims=True))


def attend_group(j, qkv_ref, bias, probs_ref):
    keys = qkv_ref[:, QW + j * HEAD_DIM : QW + (j + 1) * HEAD_DIM]
    values = qkv_ref[:, QW + KW + j * HEAD_DIM : QW + KW + (j + 1) * HEAD_DIM]
    queries = stacked(qkv_ref, j * GW)
    probs_ref[...] = dot(queries, keys, NT)
    lows = []
    for h in range(GROUP):
        rows = slice(h * TILE, (h + 1) * TILE)
        probs = softmax(probs_ref[rows, :], bias)
        probs_ref[rows, :] = probs
        lows.append(probs.astype(BF16))
    probs_low = jnp.concatenate(lows, axis=0)
    attn = dot(probs_low, values, NN).astype(BF16)
    return queries, keys, values, probs_low, attn


def forward_kernel(rank_ref, lens_ref, langs_ref, table_ref, qkv_ref, down_ref, up_ref, out_ref, probs_ref):
    rank = rank_ref[0]
    rate = table_ref[langs_ref[0, rank]]
    bias = mask_bias(lens_ref, 0, rank)
    low = jnp.zeros((TILE, RANK), F32)
    for j in range(KV):
        attn = attend_group(j, qkv_ref, bias, probs_ref)[-1]
        for h in range(GROUP):
            cols = slice(j * GW + h * HEAD_DIM, j * GW + (h + 1) * HEAD_DIM)
            out_ref[:, cols] = attn[h * TILE : (h + 1) * TILE]
        low = low + dot(out_ref[:, j * GW : (j + 1) * GW], down_ref[j * GW : (j + 1) * GW, :], NN)
    low = low.astype(BF16)
    for c in range(0, QW, 512):
        lift = dot(low, up_ref[:, c : c + 512], NN)
        out_ref[:, c : c + 512] = (out_ref[:, c : c + 512].astype(F32) + rate * lift).astype(BF16)


def slot_rate(k, rank, tiles, langs_ref, dest_ref, table_ref):
    tile = rank + (k - 1)
    near = jnp.clip(tile, 0, tiles - 1)
    live = (tile == near) & (dest_ref[1, near] == rank)
    return jnp.where(live, table_ref[langs_ref[1, near]], 0.0)


def prepare_kernel(
    place_ref, lens_ref, langs_ref, dest_ref, table_ref, qkv_ref, slots_ref, down_ref, up_ref,
    probs_ref, attn_ref, low_ref, left_ref, own_ref, right_ref, held_ref, sem,
):
    rank = place_ref[0]
    tiles = lens_ref.shape[1]
    fetch = pltpu.make_async_copy(slots_ref, held_ref, sem)
    pl.when(place_ref[1] == 0)(fetch.start)
    bias = mask_bias(lens_ref, 1, rank)
    low = jnp.zeros((TILE, RANK), F32)
    for j in range(KV):
        block = slice(j * GW, (j + 1) * GW)
        attn = attend_group(j, qkv_ref, bias, probs_ref.at[block, :])[-1]
        for h in range(GROUP):
            cols = slice(j * GW + h * HEAD_DIM, j * GW + (h + 1) * HEAD_DIM)
            attn_ref[:, cols] = attn[h * TILE : (h + 1) * TILE]
        low = low + dot(attn_ref[:, block], down_ref[block, :], NN)
    low_ref[...] = low.astype(BF16)

    @pl.when(place_ref[1] == 0)
    def _():
        fetch.wait()
        for k, out_ref in enumerate((left_ref, own_ref, right_ref)):
            rate = slot_rate(k, rank, tiles, langs_ref, dest_ref, table_ref)
            back = jnp.zeros((TILE, RANK), F32)
            for c in range(0, QW, 512):
                cols = slice(c, c + 512)
                grad = held_ref[k * TILE : (k + 1) * TILE, cols]
                scaled = (rate * grad.astype(F32)).astype(BF16)
                back = back + dot(scaled, up_ref[:, cols], NT)
            out_ref[...] = jnp.concatenate([low, back], axis=1).astype(BF16)

    @pl.when(place_ref[1] != 0)
    def _():
        for out_ref in (left_ref, own_ref, right_ref):
            out_ref[...] = jnp.zeros(out_ref.shape, BF16)


def terms_kernel(
    place_ref, langs_ref, dest_ref, table_ref, attn_ref, slots_ref, left_ref, own_ref, right_ref,
    scaled_ref, back_ref, low_ref, terms_ref, slot_scaled_ref, held_ref, sem,
):
    rank = place_ref[0]
    tiles = dest_ref.shape[1]
    fetch = pltpu.make_async_copy(slots_ref, held_ref, sem)

    @pl.when(place_ref[1] == 0)
    def _():
        fetch.start()
        fetch.wait()
        went = dest_ref[1, rank] - rank
        back = jnp.where(went < 0, left_ref[...], jnp.where(went > 0, right_ref[...], own_ref[...]))
        lows = jnp.concatenate([left_ref[...], own_ref[...], right_ref[...]], axis=0)
        for c in range(0, QW, 512):
            cols = slice(c, c + 512)
            for k in range(3):
                rows = slice(k * TILE, (k + 1) * TILE)
                rate = slot_rate(k, rank, tiles, langs_ref, dest_ref, table_ref)
                slot_scaled_ref[rows, :] = (rate * held_ref[rows, cols].astype(F32)).astype(BF16)
            one = dot(attn_ref[:, cols], back, TN)
            two = dot(slot_scaled_ref[...], lows, TN)
            terms = jnp.concatenate([one[:, RANK:], two[:, :RANK]], axis=1)
            terms_ref[cols, :] = terms.astype(terms_ref.dtype)

    @pl.when(place_ref[1] != 0)
    def _():
        for c in range(0, QW, 512):
            cols = slice(c, c + 512)
            one = dot(attn_ref[:, cols], back_ref[...], TN)
            two = dot(scaled_ref[:, cols], low_ref[...], TN)
            terms_ref[cols, :] = jnp.concatenate([one, two], axis=1).astype(terms_ref.dtype)


def backward_kernel(
    place_ref, langs_ref, dest_ref, table_ref, qkv_ref, left_ref, right_ref, last_left_ref,
    last_right_ref, slots_ref, probs_ref, down_ref, up_ref, grad_ref, scaled_ref, back_ref,
    gattn_ref, mid_ref, sem,
):
    rank = place_ref[0]
    rate = table_ref[langs_ref[1, rank]]
    went = dest_ref[1, rank] - rank
    last = place_ref[1] == place_ref[2] - 1
    active = place_ref[1] != 0
    fetch = pltpu.make_async_copy(slots_ref.at[pl.ds(TILE, TILE), :], mid_ref, sem)

    def chosen():
        fetch.start()
        fetch.wait()
        back = jnp.zeros((TILE, RANK), F32)
        for c in range(0, QW, 512):
            cols = slice(c, c + 512)
            left = jnp.where(last, last_left_ref[:, cols], left_ref[:, cols])
            right = jnp.where(last, last_right_ref[:, cols], right_ref[:, cols])
            mid = mid_ref[:, cols]
            grad = jnp.where(went < 0, left, jnp.where(went > 0, right, mid))
            gattn_ref[:, cols] = grad
            scaled = (rate * grad.astype(F32)).astype(BF16)
            scaled_ref[:, cols] = scaled
            back = back + dot(scaled, up_ref[:, cols], NT)
        return back.astype(BF16)

    @pl.when(active)
    def _():
        back = chosen()
        back_ref[...] = back
        for j in range(KV):
            block = slice(j * GW, (j + 1) * GW)
            gattn = gattn_ref[:, block].astype(F32) + dot(back, down_ref[block, :], NT)
            gattn_ref[:, block] = gattn.astype(BF16)
            queries = stacked(qkv_ref, j * GW)
            keys = qkv_ref[:, QW + j * HEAD_DIM : QW + (j + 1) * HEAD_DIM]
            values = qkv_ref[:, QW + KW + j * HEAD_DIM : QW + KW + (j + 1) * HEAD_DIM]
            grads = stacked(gattn_ref, j * GW)
            grad_probs = dot(grads, values, NT)
            lows, scores = [], []
            for h in range(GROUP):
                probs = probs_ref[j * GW + h * TILE : j * GW + (h + 1) * TILE, :]
                lows.append(probs.astype(BF16))
                weighed = probs * grad_probs[h * TILE : (h + 1) * TILE]
                delta = jnp.sum(weighed, axis=-1, keepdims=True)
                scores.append(((weighed - probs * delta) * SCALE).astype(BF16))
            probs_low = jnp.concatenate(lows, axis=0)
            grad_scores = jnp.concatenate(scores, axis=0)
            grad_queries = dot(grad_scores, keys, NN).astype(BF16)
            for h in range(GROUP):
                cols = slice(j * GW + h * HEAD_DIM, j * GW + (h + 1) * HEAD_DIM)
                grad_ref[:, cols] = grad_queries[h * TILE : (h + 1) * TILE]
            cols = slice(QW + j * HEAD_DIM, QW + (j + 1) * HEAD_DIM)
            grad_ref[:, cols] = dot(grad_scores, queries, TN).astype(BF16)
            cols = slice(QW + KW + j * HEAD_DIM, QW + KW + (j + 1) * HEAD_DIM)
            grad_ref[:, cols] = dot(probs_low, grads, TN).astype(BF16)


COST = pl.CostEstimate(flops=2**20, bytes_accessed=2**20, transcendentals=0)
SMEM = pl.BlockSpec(memory_space=pltpu.SMEM)
VMEM = pl.BlockSpec(memory_space=pltpu.VMEM)
ANY = pl.BlockSpec(memory_space=pl.ANY)


def run_forward(rank, lengths, languages, table, qkv, down, up):
    return pl.pallas_call(
        forward_kernel,
        out_shape=jax.ShapeDtypeStruct((TILE, QW), BF16),
        in_specs=[SMEM] * 4 + [VMEM] * 3,
        out_specs=VMEM,
        scratch_shapes=[pltpu.VMEM((GROUP * TILE, TILE), F32)],
        compiler_params=pltpu.CompilerParams(vmem_limit_bytes=16 * 2**20),
        cost_estimate=COST,
        name="forward_tile",
    )(rank, lengths, languages, table, qkv, down, up)


def run_prepare(place, lengths, languages, dest, table, qkv, slots, down, up):
    message = jax.ShapeDtypeStruct((TILE, 2 * RANK), BF16)
    return pl.pallas_call(
        prepare_kernel,
        out_shape=(
            jax.ShapeDtypeStruct((QW, TILE), F32),
            jax.ShapeDtypeStruct((TILE, QW), BF16),
            jax.ShapeDtypeStruct((TILE, RANK), BF16),
            message,
            message,
            message,
        ),
        in_specs=[SMEM] * 5 + [VMEM, ANY, VMEM, VMEM],
        out_specs=(VMEM,) * 6,
        scratch_shapes=[pltpu.VMEM((3 * TILE, QW), BF16), pltpu.SemaphoreType.DMA],
        compiler_params=pltpu.CompilerParams(vmem_limit_bytes=22 * 2**20),
        cost_estimate=COST,
        name="prepare_tile",
    )(place, lengths, languages, dest, table, qkv, slots, down, up)


def run_terms(place, languages, dest, table, attn, slots, left, own, right, scaled, back, low):
    return pl.pallas_call(
        terms_kernel,
        out_shape=jax.ShapeDtypeStruct((QW, 2 * RANK), BF16),
        in_specs=[SMEM] * 4 + [VMEM, ANY] + [VMEM] * 6,
        out_specs=VMEM,
        scratch_shapes=[
            pltpu.VMEM((3 * TILE, 512), BF16),
            pltpu.VMEM((3 * TILE, QW), BF16),
            pltpu.SemaphoreType.DMA,
        ],
        compiler_params=pltpu.CompilerParams(vmem_limit_bytes=22 * 2**20),
        cost_estimate=COST,
        name="adapter_terms",
    )(place, languages, dest, table, attn, slots, left, own, right, scaled, back, low)


def run_backward(place, languages, dest, table, qkv, moved, slots, probs, down, up):
    return pl.pallas_call(
        backward_kernel,
        out_shape=(
            jax.ShapeDtypeStruct((TILE, QW + 2 * KW), BF16),
            jax.ShapeDtypeStruct((TILE, QW), BF16),
            jax.ShapeDtypeStruct((TILE, RANK), BF16),
        ),
        in_specs=[SMEM] * 4 + [VMEM] * (1 + len(moved)) + [ANY] + [VMEM] * 3,
        out_specs=(VMEM,) * 3,
        scratch_shapes=[
            pltpu.VMEM((TILE, QW), BF16),
            pltpu.VMEM((TILE, QW), BF16),
            pltpu.SemaphoreType.DMA,
        ],
        compiler_params=pltpu.CompilerParams(vmem_limit_bytes=24 * 2**20),
        cost_estimate=COST,
        name="backward_tile",
    )(place, languages, dest, table, qkv, *moved, slots, probs, down, up)


def place_kernel(
    place_ref, dest_ref, before_ref, hop_ref, after_ref, ends_ref, back_ref,
    placed_ref, handed_ref, zero_ref, sems,
):
    rank, section = place_ref[0], place_ref[1]
    tiles = dest_ref.shape[1]
    zero_ref[...] = jnp.zeros(zero_ref.shape, BF16)
    handed = pltpu.make_async_copy(back_ref, handed_ref, sems.at[0])
    handed.start()
    copies = []
    for k, (near, edge) in enumerate(
        ((before_ref, run_start(rank)), (hop_ref, False), (after_ref, run_end(rank)))
    ):
        tile = rank + (k - 1)
        held = jnp.clip(tile, 0, tiles - 1)
        live = (tile == held) & (dest_ref[0, held] == rank) & (section > 0)
        crossed = (section == 2) & edge
        slot = placed_ref.at[pl.ds(k * TILE, TILE), :]
        for source, chosen in (
            (near, live & jnp.logical_not(crossed)),
            (ends_ref, live & crossed),
            (zero_ref, jnp.logical_not(live)),
        ):
            copies.append((pltpu.make_async_copy(source, slot, sems.at[k + 1]), chosen))
    for copy, chosen in copies:
        pl.when(chosen)(copy.start)
    for copy, chosen in copies:
        pl.when(chosen)(copy.wait)
    handed.wait()


def run_place(place, dest, *tiles):
    return pl.pallas_call(
        place_kernel,
        out_shape=(
            jax.ShapeDtypeStruct((3 * TILE, QW), BF16),
            jax.ShapeDtypeStruct(tiles[-1].shape, BF16),
        ),
        in_specs=[SMEM] * 2 + [VMEM] * len(tiles),
        out_specs=(ANY, ANY),
        scratch_shapes=[pltpu.VMEM((TILE, QW), BF16), pltpu.SemaphoreType.DMA((4,))],
        compiler_params=pltpu.CompilerParams(vmem_limit_bytes=24 * 2**20),
        cost_estimate=COST,
        name="place_outputs",
    )(place, dest, *tiles)


def sections():
    return lax.axis_size("section")


def shift(x, moves):
    size = lax.axis_size("dp")
    route = []
    for s_list, up, step, keep in moves:
        for s in s_list:
            for t in range(size):
                if 0 <= s + up < sections() and 0 <= t + step < size and keep(t):
                    route.append((s * size + t, (s + up) * size + t + step))
    return lax.ppermute(x, AXES, route)


def anywhere(t):
    return True


def run_start(t):
    return t % RUN == 0


def run_end(t):
    return t % RUN == RUN - 1


def after_run_start(t):
    return t % RUN == 1


def before_run_end(t):
    return t % RUN == RUN - 2


def not_run_start(t):
    return t % RUN != 0


def not_run_end(t):
    return t % RUN != RUN - 1


def scatter(x, groups):
    return lax.all_to_all(x, "dp", 0, 0, axis_index_groups=groups, tiled=True)


def shards(
    qkv_a, qkv_b, slot_grad_b, adapter_down, adapter_up, lang_scale, languages, lengths, destination
):
    rank, size = lax.axis_index("dp"), lax.axis_size("dp")
    section, last = lax.axis_index("section"), sections() - 1
    place = jnp.stack([rank, section, jnp.int32(sections())]).astype(jnp.int32)
    down, up = adapter_down[0], adapter_up[0]
    slots = slot_grad_b[0]
    every, early = range(sections()), range(1, last)
    to_up, to_down = slots[2 * TILE :], slots[:TILE]
    from_left = shift(to_up, [(early, 0, 1, anywhere)])
    from_right = shift(to_down, [(early, 0, -1, anywhere)])
    out = run_forward(place, lengths, languages, lang_scale, qkv_a[0], down, up)
    out, place = lax.optimization_barrier((out, place))
    near = shift(out, [([0, 2], 1, 0, anywhere)])
    probs, attn, low, to_left, own, to_right = run_prepare(
        place, lengths, languages, destination, lang_scale, qkv_b[0], slots, down, up
    )
    from_left, from_right, low = lax.optimization_barrier((from_left, from_right, low))
    to_up, to_down, near, low = lax.optimization_barrier((to_up, to_down, near, low))
    last_left = shift(to_up, [([last], 0, 1, anywhere)])
    last_right = shift(to_down, [([last], 0, -1, anywhere)])
    far = shift(
        jnp.where(section == last, near, out),
        [([1], 1, 0, anywhere), ([last], -last, -1, run_end), ([last], -last, 1, run_start)],
    )
    grad_qkv, scaled, back = run_backward(
        place, languages, destination, lang_scale, qkv_b[0],
        (from_left, from_right, last_left, last_right), slots, probs, down, up,
    )
    grad_qkv, near, to_left, to_right = lax.optimization_barrier(
        (grad_qkv, near, to_left, to_right)
    )
    handed_back = shift(grad_qkv, [(every, -1, 0, anywhere)])
    left = shift(to_right, [([0], 0, 1, anywhere)])
    right = shift(to_left, [([0], 0, -1, anywhere)])
    terms = run_terms(
        place, languages, destination, lang_scale, attn, slots, left, own, right, scaled, back, low
    )
    planes = [[RUN * k + z for k in range(size // RUN)] for z in range(RUN)]
    columns = [[RUN * k + z for z in range(RUN)] for k in range(size // RUN)]
    far, terms, out = lax.optimization_barrier((far, terms, out))
    pieces = scatter(terms.reshape(size // RUN, -1, 2 * RANK), planes)
    hop = jnp.where((section == 1) | (section == last), near, far)
    before = shift(
        hop,
        [([1], 0, 1, anywhere), ([2, last], 0, 1, not_run_end), ([0], last, 2, before_run_end)],
    )
    after = shift(
        hop,
        [([1], 0, -1, anywhere), ([2, last], 0, -1, not_run_start), ([0], last, -2, after_run_start)],
    )
    ends = shift(out, [([1], 1, 1, run_end), ([1], 1, -1, run_start)])
    pieces, _ = lax.optimization_barrier((pieces, handed_back))
    terms = jnp.sum(pieces.astype(F32), axis=0)
    terms = jnp.sum(scatter(terms.reshape(RUN, -1, 2 * RANK), columns), axis=0)
    handed_forward, handed_back = run_place(
        place, destination, before, hop, after, ends, handed_back
    )
    return (handed_forward[None], handed_back[None], terms[None])


def solution(mesh):
    return jax.shard_map(
        shards,
        mesh=mesh,
        in_specs=(
            P("section", "dp", None),
            P("section", "dp", None),
            P("section", "dp", None),
            P("section", None, None),
            P("section", None, None),
            P(),
            P(),
            P(),
            P(),
        ),
        out_specs=(P("section", "dp", None), P("section", "dp", None), P("section", "dp", None)),
        check_vma=False,
    )
```

```python
import functools
import math

import jax
import jax.numpy as jnp
from jax import lax
from jax.experimental import pallas as pl
from jax.experimental.pallas import tpu as pltpu
from jax.sharding import PartitionSpec as P

HEADS = 32
KV = 4
GROUP = HEADS // KV
HEAD_DIM = 128
TILE = 128
SEGS = 8
RANK = 64
QW = HEADS * HEAD_DIM
KW = KV * HEAD_DIM
GW = GROUP * HEAD_DIM
SCALE = 1.0 / math.sqrt(HEAD_DIM)
RUN = 4
AXES = ("section", "dp")
BF16 = jnp.bfloat16
F32 = jnp.float32


def dot(a, b, dims):
    return lax.dot_general(a, b, (dims, ((), ())), preferred_element_type=F32)


NN = ((1,), (0,))
NT = ((1,), (1,))
TN = ((0,), (0,))


def mask_bias(lens_ref, m, rank):
    shape = (TILE, TILE)
    row = lax.broadcasted_iota(jnp.int32, shape, 0)
    col = lax.broadcasted_iota(jnp.int32, shape, 1)
    seg_row = jnp.zeros(shape, jnp.int32)
    seg_col = jnp.zeros(shape, jnp.int32)
    end = jnp.int32(0)
    for k in range(SEGS):
        end = end + lens_ref[m, rank, k]
        seg_row = seg_row + (row >= end).astype(jnp.int32)
        seg_col = seg_col + (col >= end).astype(jnp.int32)
    allowed = (seg_row == seg_col) & (row >= col)
    return jnp.where(allowed, 0.0, -1e30).astype(F32)


def stacked(ref, base):
    return jnp.concatenate(
        [ref[:, base + h * HEAD_DIM : base + (h + 1) * HEAD_DIM] for h in range(GROUP)], axis=0
    )


def softmax(scores, bias):
    masked = scores + bias
    top = jnp.max(masked, axis=-1, keepdims=True)
    weights = jnp.exp2((masked - top) * (SCALE * math.log2(math.e)))
    return weights * (1.0 / jnp.sum(weights, axis=-1, keepdims=True))


def attend_group(j, qkv_ref, bias, probs_ref):
    keys = qkv_ref[:, QW + j * HEAD_DIM : QW + (j + 1) * HEAD_DIM]
    values = qkv_ref[:, QW + KW + j * HEAD_DIM : QW + KW + (j + 1) * HEAD_DIM]
    queries = stacked(qkv_ref, j * GW)
    probs_ref[...] = dot(queries, keys, NT)
    lows = []
    for h in range(GROUP):
        rows = slice(h * TILE, (h + 1) * TILE)
        probs = softmax(probs_ref[rows, :], bias)
        probs_ref[rows, :] = probs
        lows.append(probs.astype(BF16))
    probs_low = jnp.concatenate(lows, axis=0)
    attn = dot(probs_low, values, NN).astype(BF16)
    return queries, keys, values, probs_low, attn


def forward_kernel(rank_ref, lens_ref, langs_ref, table_ref, qkv_ref, down_ref, up_ref, out_ref, probs_ref):
    rank = rank_ref[0]
    rate = table_ref[langs_ref[0, rank]]
    bias = mask_bias(lens_ref, 0, rank)
    low = jnp.zeros((TILE, RANK), F32)
    for j in range(KV):
        attn = attend_group(j, qkv_ref, bias, probs_ref)[-1]
        for h in range(GROUP):
            cols = slice(j * GW + h * HEAD_DIM, j * GW + (h + 1) * HEAD_DIM)
            out_ref[:, cols] = attn[h * TILE : (h + 1) * TILE]
        block = slice(j * GW, (j + 1) * GW)
        low = low + dot(out_ref[:, block], down_ref[:, block], NT)
    low = low.astype(BF16)
    for c in range(0, QW, 512):
        lift = dot(low, up_ref[:, c : c + 512], NN)
        out_ref[:, c : c + 512] = (out_ref[:, c : c + 512].astype(F32) + rate * lift).astype(BF16)


def slot_rate(k, rank, tiles, langs_ref, dest_ref, table_ref):
    tile = rank + (k - 1)
    near = jnp.clip(tile, 0, tiles - 1)
    live = (tile == near) & (dest_ref[1, near] == rank)
    return jnp.where(live, table_ref[langs_ref[1, near]], 0.0)


def prepare_kernel(
    place_ref, lens_ref, langs_ref, dest_ref, table_ref, qkv_ref, slots_ref, down_ref, up_ref,
    probs_ref, attn_ref, low_ref, left_ref, own_ref, right_ref, held_ref, sem,
):
    rank = place_ref[0]
    tiles = lens_ref.shape[1]
    fetch = pltpu.make_async_copy(slots_ref, held_ref, sem)
    pl.when(place_ref[1] == 0)(fetch.start)
    bias = mask_bias(lens_ref, 1, rank)
    low = jnp.zeros((TILE, RANK), F32)
    for j in range(KV):
        block = slice(j * GW, (j + 1) * GW)
        attn = attend_group(j, qkv_ref, bias, probs_ref.at[block, :])[-1]
        for h in range(GROUP):
            cols = slice(j * GW + h * HEAD_DIM, j * GW + (h + 1) * HEAD_DIM)
            attn_ref[:, cols] = attn[h * TILE : (h + 1) * TILE]
        low = low + dot(attn_ref[:, block], down_ref[:, block], NT)
    low_ref[...] = low.astype(BF16)

    @pl.when(place_ref[1] == 0)
    def _():
        fetch.wait()
        for k, out_ref in enumerate((left_ref, own_ref, right_ref)):
            rate = slot_rate(k, rank, tiles, langs_ref, dest_ref, table_ref)
            back = jnp.zeros((TILE, RANK), F32)
            for c in range(0, QW, 512):
                cols = slice(c, c + 512)
                grad = held_ref[k * TILE : (k + 1) * TILE, cols]
                scaled = (rate * grad.astype(F32)).astype(BF16)
                back = back + dot(scaled, up_ref[:, cols], NT)
            out_ref[...] = jnp.concatenate([low, back], axis=1).astype(BF16)

    @pl.when(place_ref[1] != 0)
    def _():
        for out_ref in (left_ref, own_ref, right_ref):
            out_ref[...] = jnp.zeros(out_ref.shape, BF16)


def terms_kernel(
    place_ref, langs_ref, dest_ref, table_ref, attn_ref, slots_ref, left_ref, own_ref, right_ref,
    home_ref, terms_ref, slot_scaled_ref, held_ref, summed_ref, sem,
):
    rank = place_ref[0]
    tiles = dest_ref.shape[1]
    fetch = pltpu.make_async_copy(slots_ref, held_ref, sem)

    @pl.when(place_ref[1] == 0)
    def _():
        fetch.start()
        fetch.wait()
        went = dest_ref[1, rank] - rank
        back = jnp.where(went < 0, left_ref[...], jnp.where(went > 0, right_ref[...], own_ref[...]))
        lows = jnp.concatenate([left_ref[...], own_ref[...], right_ref[...]], axis=0)
        for c in range(0, QW, 512):
            cols = slice(c, c + 512)
            for k in range(3):
                rows = slice(k * TILE, (k + 1) * TILE)
                rate = slot_rate(k, rank, tiles, langs_ref, dest_ref, table_ref)
                slot_scaled_ref[rows, :] = (rate * held_ref[rows, cols].astype(F32)).astype(BF16)
            one = dot(attn_ref[:, cols], back, TN)
            two = dot(slot_scaled_ref[...], lows, TN)
            terms = jnp.concatenate([one[:, RANK:], two[:, :RANK]], axis=1)
            summed_ref[cols, :] = terms.astype(BF16)
        store = pltpu.make_async_copy(summed_ref, terms_ref, sem)
        store.start()
        store.wait()


def backward_kernel(
    place_ref, langs_ref, dest_ref, table_ref, qkv_ref, left_ref, right_ref, last_left_ref,
    last_right_ref, slots_ref, probs_ref, attn_ref, low_ref, down_ref, up_ref, grad_ref, terms_ref,
    gattn_ref, scaled_ref, mid_ref, sem,
):
    rank = place_ref[0]
    rate = table_ref[langs_ref[1, rank]]
    went = dest_ref[1, rank] - rank
    last = place_ref[1] == place_ref[2] - 1
    active = place_ref[1] != 0
    fetch = pltpu.make_async_copy(slots_ref.at[pl.ds(TILE, TILE), :], mid_ref, sem)

    def chosen():
        fetch.start()
        fetch.wait()
        back = jnp.zeros((TILE, RANK), F32)
        for c in range(0, QW, 512):
            cols = slice(c, c + 512)
            left = jnp.where(last, last_left_ref[:, cols], left_ref[:, cols])
            right = jnp.where(last, last_right_ref[:, cols], right_ref[:, cols])
            mid = mid_ref[:, cols]
            grad = jnp.where(went < 0, left, jnp.where(went > 0, right, mid))
            gattn_ref[:, cols] = grad
            scaled = (rate * grad.astype(F32)).astype(BF16)
            scaled_ref[:, cols] = scaled
            back = back + dot(scaled, up_ref[:, cols], NT)
        return back.astype(BF16)

    @pl.when(active)
    def _():
        back = chosen()
        for j in range(KV):
            block = slice(j * GW, (j + 1) * GW)
            gattn = gattn_ref[:, block].astype(F32) + dot(back, down_ref[:, block], NN)
            gattn_ref[:, block] = gattn.astype(BF16)
            queries = stacked(qkv_ref, j * GW)
            keys = qkv_ref[:, QW + j * HEAD_DIM : QW + (j + 1) * HEAD_DIM]
            values = qkv_ref[:, QW + KW + j * HEAD_DIM : QW + KW + (j + 1) * HEAD_DIM]
            grads = stacked(gattn_ref, j * GW)
            grad_probs = dot(grads, values, NT)
            lows, scores = [], []
            for h in range(GROUP):
                probs = probs_ref[j * GW + h * TILE : j * GW + (h + 1) * TILE, :]
                lows.append(probs.astype(BF16))
                weighed = probs * grad_probs[h * TILE : (h + 1) * TILE]
                delta = jnp.sum(weighed, axis=-1, keepdims=True)
                scores.append(((weighed - probs * delta) * SCALE).astype(BF16))
            probs_low = jnp.concatenate(lows, axis=0)
            grad_scores = jnp.concatenate(scores, axis=0)
            grad_queries = dot(grad_scores, keys, NN).astype(BF16)
            for h in range(GROUP):
                cols = slice(j * GW + h * HEAD_DIM, j * GW + (h + 1) * HEAD_DIM)
                grad_ref[:, cols] = grad_queries[h * TILE : (h + 1) * TILE]
            cols = slice(QW + j * HEAD_DIM, QW + (j + 1) * HEAD_DIM)
            grad_ref[:, cols] = dot(grad_scores, queries, TN).astype(BF16)
            cols = slice(QW + KW + j * HEAD_DIM, QW + KW + (j + 1) * HEAD_DIM)
            grad_ref[:, cols] = dot(probs_low, grads, TN).astype(BF16)
        for c in range(0, QW, 512):
            cols = slice(c, c + 512)
            one = dot(attn_ref[:, cols], back, TN)
            two = dot(scaled_ref[:, cols], low_ref[...], TN)
            terms_ref[cols, :] = jnp.concatenate([one, two], axis=1).astype(terms_ref.dtype)


COST = pl.CostEstimate(flops=2**20, bytes_accessed=2**20, transcendentals=0)
SMEM = pl.BlockSpec(memory_space=pltpu.SMEM)
VMEM = pl.BlockSpec(memory_space=pltpu.VMEM)
ANY = pl.BlockSpec(memory_space=pl.ANY)


def run_forward(rank, lengths, languages, table, qkv, down, up):
    return pl.pallas_call(
        forward_kernel,
        out_shape=jax.ShapeDtypeStruct((TILE, QW), BF16),
        in_specs=[SMEM] * 4 + [VMEM] * 3,
        out_specs=VMEM,
        scratch_shapes=[pltpu.VMEM((GROUP * TILE, TILE), F32)],
        compiler_params=pltpu.CompilerParams(vmem_limit_bytes=16 * 2**20),
        cost_estimate=COST,
        name="forward_tile",
    )(rank, lengths, languages, table, qkv, down, up)


def run_prepare(place, lengths, languages, dest, table, qkv, slots, down, up):
    message = jax.ShapeDtypeStruct((TILE, 2 * RANK), BF16)
    return pl.pallas_call(
        prepare_kernel,
        out_shape=(
            jax.ShapeDtypeStruct((QW, TILE), F32),
            jax.ShapeDtypeStruct((TILE, QW), BF16),
            jax.ShapeDtypeStruct((TILE, RANK), BF16),
            message,
            message,
            message,
        ),
        in_specs=[SMEM] * 5 + [VMEM, ANY, VMEM, VMEM],
        out_specs=(VMEM,) * 6,
        scratch_shapes=[pltpu.VMEM((3 * TILE, QW), BF16), pltpu.SemaphoreType.DMA],
        compiler_params=pltpu.CompilerParams(vmem_limit_bytes=22 * 2**20),
        cost_estimate=COST,
        name="prepare_tile",
    )(place, lengths, languages, dest, table, qkv, slots, down, up)


def run_terms(place, languages, dest, table, attn, slots, left, own, right, home):
    return pl.pallas_call(
        terms_kernel,
        out_shape=jax.ShapeDtypeStruct((QW, 2 * RANK), BF16),
        in_specs=[SMEM] * 4 + [VMEM, ANY] + [VMEM] * 3 + [ANY],
        input_output_aliases={9: 0},
        out_specs=ANY,
        scratch_shapes=[
            pltpu.VMEM((3 * TILE, 512), BF16),
            pltpu.VMEM((3 * TILE, QW), BF16),
            pltpu.VMEM((QW, 2 * RANK), BF16),
            pltpu.SemaphoreType.DMA,
        ],
        compiler_params=pltpu.CompilerParams(vmem_limit_bytes=22 * 2**20),
        cost_estimate=COST,
        name="adapter_terms",
    )(place, languages, dest, table, attn, slots, left, own, right, home)


def run_backward(place, languages, dest, table, qkv, moved, slots, probs, attn, low, down, up):
    return pl.pallas_call(
        backward_kernel,
        out_shape=(
            jax.ShapeDtypeStruct((TILE, QW + 2 * KW), BF16),
            jax.ShapeDtypeStruct((QW, 2 * RANK), BF16),
        ),
        in_specs=[SMEM] * 4 + [VMEM] * 5 + [ANY] + [VMEM] * 5,
        out_specs=(VMEM, VMEM),
        scratch_shapes=[
            pltpu.VMEM((TILE, QW), BF16),
            pltpu.VMEM((TILE, QW), BF16),
            pltpu.VMEM((TILE, QW), BF16),
            pltpu.SemaphoreType.DMA,
        ],
        compiler_params=pltpu.CompilerParams(vmem_limit_bytes=24 * 2**20),
        cost_estimate=COST,
        name="backward_tile",
    )(place, languages, dest, table, qkv, *moved, slots, probs, attn, low, down, up)


def place_kernel(
    place_ref, dest_ref, before_ref, hop_ref, after_ref, ends_ref, back_ref,
    placed_ref, handed_ref, zero_ref, sems,
):
    rank, section = place_ref[0], place_ref[1]
    tiles = dest_ref.shape[1]
    zero_ref[...] = jnp.zeros(zero_ref.shape, BF16)
    handed = pltpu.make_async_copy(back_ref, handed_ref, sems.at[0])
    handed.start()
    copies = []
    for k, (near, edge) in enumerate(
        ((before_ref, run_start(rank)), (hop_ref, False), (after_ref, run_end(rank)))
    ):
        tile = rank + (k - 1)
        held = jnp.clip(tile, 0, tiles - 1)
        live = (tile == held) & (dest_ref[0, held] == rank) & (section > 0)
        crossed = (section == 2) & edge
        slot = placed_ref.at[pl.ds(k * TILE, TILE), :]
        for source, chosen in (
            (near, live & jnp.logical_not(crossed)),
            (ends_ref, live & crossed),
            (zero_ref, jnp.logical_not(live)),
        ):
            copies.append((pltpu.make_async_copy(source, slot, sems.at[k + 1]), chosen))
    for copy, chosen in copies:
        pl.when(chosen)(copy.start)
    for copy, chosen in copies:
        pl.when(chosen)(copy.wait)
    handed.wait()


def run_place(place, dest, *tiles):
    return pl.pallas_call(
        place_kernel,
        out_shape=(
            jax.ShapeDtypeStruct((3 * TILE, QW), BF16),
            jax.ShapeDtypeStruct(tiles[-1].shape, BF16),
        ),
        in_specs=[SMEM] * 2 + [ANY] * len(tiles),
        out_specs=(ANY, ANY),
        scratch_shapes=[pltpu.VMEM((TILE, QW), BF16), pltpu.SemaphoreType.DMA((4,))],
        compiler_params=pltpu.CompilerParams(vmem_limit_bytes=24 * 2**20),
        cost_estimate=COST,
        name="place_outputs",
    )(place, dest, *tiles)


def sections():
    return lax.axis_size("section")


def shift(x, moves):
    size = lax.axis_size("dp")
    route = []
    for s_list, up, step, keep in moves:
        for s in s_list:
            for t in range(size):
                if 0 <= s + up < sections() and 0 <= t + step < size and keep(t):
                    route.append((s * size + t, (s + up) * size + t + step))
    return lax.ppermute(x, AXES, route)


def anywhere(t):
    return True


def run_start(t):
    return t % RUN == 0


def run_end(t):
    return t % RUN == RUN - 1


def not_run_start(t):
    return t % RUN != 0


def not_run_end(t):
    return t % RUN != RUN - 1


def scatter(x, groups):
    return lax.all_to_all(x, "dp", 0, 0, axis_index_groups=groups, tiled=True)


def shards(
    qkv_a, qkv_b, slot_grad_b, adapter_down, adapter_up, lang_scale, languages, lengths, destination
):
    rank, size = lax.axis_index("dp"), lax.axis_size("dp")
    section, last = lax.axis_index("section"), sections() - 1
    place = jnp.stack([rank, section, jnp.int32(sections())]).astype(jnp.int32)
    down, up = adapter_down[0].T, adapter_up[0]
    slots = slot_grad_b[0]
    every, early = range(sections()), range(1, last)
    to_up, to_down = slots[2 * TILE :], slots[:TILE]
    from_left = shift(to_up, [(early, 0, 1, anywhere)])
    from_right = shift(to_down, [(early, 0, -1, anywhere)])
    out = run_forward(place, lengths, languages, lang_scale, qkv_a[0], down, up)
    out, place = lax.optimization_barrier((out, place))
    near = shift(out, [([0, 2], 1, 0, anywhere)])
    probs, attn, low, to_left, own, to_right = run_prepare(
        place, lengths, languages, destination, lang_scale, qkv_b[0], slots, down, up
    )
    from_left, from_right, low = lax.optimization_barrier((from_left, from_right, low))
    to_up, to_down, near, low = lax.optimization_barrier((to_up, to_down, near, low))
    last_left = shift(to_up, [([last], 0, 1, anywhere)])
    last_right = shift(to_down, [([last], 0, -1, anywhere)])
    far = shift(out, [([1], 1, 0, anywhere)])
    grad_qkv, terms = run_backward(
        place, languages, destination, lang_scale, qkv_b[0],
        (from_left, from_right, last_left, last_right), slots, probs, attn, low, down, up,
    )
    grad_qkv, near, to_left, to_right = lax.optimization_barrier(
        (grad_qkv, near, to_left, to_right)
    )
    handed_back = shift(grad_qkv, [(every, -1, 0, anywhere)])
    left = shift(to_right, [([0], 0, 1, anywhere)])
    right = shift(to_left, [([0], 0, -1, anywhere)])
    terms = run_terms(
        place, languages, destination, lang_scale, attn, slots, left, own, right, terms
    )
    planes = [[RUN * k + z for k in range(size // RUN)] for z in range(RUN)]
    columns = [[RUN * k + z for z in range(RUN)] for k in range(size // RUN)]
    far, terms, out = lax.optimization_barrier((far, terms, out))
    pieces = scatter(terms.reshape(size // RUN, -1, 2 * RANK), planes)
    hop = jnp.where(section == 2, far, near)
    before = shift(hop, [([1, last], 0, 1, anywhere), ([2], 0, 1, not_run_end)])
    after = shift(hop, [([1, last], 0, -1, anywhere), ([2], 0, -1, not_run_start)])
    ends = shift(out, [([1], 1, 1, run_end), ([1], 1, -1, run_start)])
    pieces, _ = lax.optimization_barrier((pieces, handed_back))
    terms = jnp.sum(pieces.astype(F32), axis=0)
    terms = jnp.sum(scatter(terms.reshape(RUN, -1, 2 * RANK), columns), axis=0)
    handed_forward, handed_back = run_place(
        place, destination, before, hop, after, ends, handed_back
    )
    return (handed_forward[None], handed_back[None], terms[None])


def solution(mesh):
    return jax.shard_map(
        shards,
        mesh=mesh,
        in_specs=(
            P("section", "dp", None),
            P("section", "dp", None),
            P("section", "dp", None),
            P("section", None, None),
            P("section", None, None),
            P(),
            P(),
            P(),
            P(),
        ),
        out_specs=(P("section", "dp", None), P("section", "dp", None), P("section", "dp", None)),
        check_vma=False,
    )
```

```python
import functools
import math

import jax
import jax.numpy as jnp
from jax import lax
from jax.experimental import pallas as pl
from jax.experimental.pallas import tpu as pltpu
from jax.sharding import PartitionSpec as P

HEADS = 32
KV = 4
GROUP = HEADS // KV
HEAD_DIM = 128
TILE = 128
SEGS = 8
RANK = 64
QW = HEADS * HEAD_DIM
KW = KV * HEAD_DIM
GW = GROUP * HEAD_DIM
SCALE = 1.0 / math.sqrt(HEAD_DIM)
RUN = 4
AXES = ("section", "dp")
BF16 = jnp.bfloat16
F32 = jnp.float32


def dot(a, b, dims):
    return lax.dot_general(a, b, (dims, ((), ())), preferred_element_type=F32)


NN = ((1,), (0,))
NT = ((1,), (1,))
TN = ((0,), (0,))


def mask_bias(lens_ref, m, rank):
    shape = (TILE, TILE)
    row = lax.broadcasted_iota(jnp.int32, shape, 0)
    col = lax.broadcasted_iota(jnp.int32, shape, 1)
    seg_row = jnp.zeros(shape, jnp.int32)
    seg_col = jnp.zeros(shape, jnp.int32)
    end = jnp.int32(0)
    for k in range(SEGS):
        end = end + lens_ref[m, rank, k]
        seg_row = seg_row + (row >= end).astype(jnp.int32)
        seg_col = seg_col + (col >= end).astype(jnp.int32)
    allowed = (seg_row == seg_col) & (row >= col)
    return jnp.where(allowed, 0.0, -1e30).astype(F32)


def stacked(ref, base):
    return jnp.concatenate(
        [ref[:, base + h * HEAD_DIM : base + (h + 1) * HEAD_DIM] for h in range(GROUP)], axis=0
    )


def softmax(scores, bias):
    masked = scores + bias
    top = jnp.max(masked, axis=-1, keepdims=True)
    weights = jnp.exp2((masked - top) * (SCALE * math.log2(math.e)))
    return weights * (1.0 / jnp.sum(weights, axis=-1, keepdims=True))


def attend_group(j, qkv_ref, bias, probs_ref):
    keys = qkv_ref[:, QW + j * HEAD_DIM : QW + (j + 1) * HEAD_DIM]
    values = qkv_ref[:, QW + KW + j * HEAD_DIM : QW + KW + (j + 1) * HEAD_DIM]
    queries = stacked(qkv_ref, j * GW)
    probs_ref[...] = dot(queries, keys, NT)
    lows = []
    for h in range(GROUP):
        rows = slice(h * TILE, (h + 1) * TILE)
        probs = softmax(probs_ref[rows, :], bias)
        probs_ref[rows, :] = probs
        lows.append(probs.astype(BF16))
    probs_low = jnp.concatenate(lows, axis=0)
    attn = dot(probs_low, values, NN).astype(BF16)
    return queries, keys, values, probs_low, attn


def forward_kernel(rank_ref, lens_ref, langs_ref, table_ref, qkv_ref, down_ref, up_ref, out_ref, probs_ref):
    rank = rank_ref[0]
    rate = table_ref[langs_ref[0, rank]]
    bias = mask_bias(lens_ref, 0, rank)
    low = jnp.zeros((TILE, RANK), F32)
    for j in range(KV):
        attn = attend_group(j, qkv_ref, bias, probs_ref)[-1]
        for h in range(GROUP):
            cols = slice(j * GW + h * HEAD_DIM, j * GW + (h + 1) * HEAD_DIM)
            out_ref[:, cols] = attn[h * TILE : (h + 1) * TILE]
        block = slice(j * GW, (j + 1) * GW)
        low = low + dot(out_ref[:, block], down_ref[:, block], NT)
    low = low.astype(BF16)
    for c in range(0, QW, 512):
        lift = dot(low, up_ref[:, c : c + 512], NN)
        out_ref[:, c : c + 512] = (out_ref[:, c : c + 512].astype(F32) + rate * lift).astype(BF16)


def slot_rate(k, rank, tiles, langs_ref, dest_ref, table_ref):
    tile = rank + (k - 1)
    near = jnp.clip(tile, 0, tiles - 1)
    live = (tile == near) & (dest_ref[1, near] == rank)
    return jnp.where(live, table_ref[langs_ref[1, near]], 0.0)


def prepare_kernel(
    place_ref, lens_ref, langs_ref, dest_ref, table_ref, qkv_ref, slots_ref, down_ref, up_ref,
    probs_ref, attn_ref, low_ref, left_ref, own_ref, right_ref, held_ref, sem,
):
    rank = place_ref[0]
    tiles = lens_ref.shape[1]
    fetch = pltpu.make_async_copy(slots_ref, held_ref, sem)
    pl.when(place_ref[1] == 0)(fetch.start)
    bias = mask_bias(lens_ref, 1, rank)
    low = jnp.zeros((TILE, RANK), F32)
    for j in range(KV):
        block = slice(j * GW, (j + 1) * GW)
        attn = attend_group(j, qkv_ref, bias, probs_ref.at[block, :])[-1]
        for h in range(GROUP):
            cols = slice(j * GW + h * HEAD_DIM, j * GW + (h + 1) * HEAD_DIM)
            attn_ref[:, cols] = attn[h * TILE : (h + 1) * TILE]
        low = low + dot(attn_ref[:, block], down_ref[:, block], NT)
    low_ref[...] = low.astype(BF16)

    @pl.when(place_ref[1] == 0)
    def _():
        fetch.wait()
        for k, out_ref in enumerate((left_ref, own_ref, right_ref)):
            rate = slot_rate(k, rank, tiles, langs_ref, dest_ref, table_ref)
            back = jnp.zeros((TILE, RANK), F32)
            for c in range(0, QW, 512):
                cols = slice(c, c + 512)
                grad = held_ref[k * TILE : (k + 1) * TILE, cols]
                scaled = (rate * grad.astype(F32)).astype(BF16)
                back = back + dot(scaled, up_ref[:, cols], NT)
            out_ref[...] = jnp.concatenate([low, back], axis=1).astype(BF16)

    @pl.when(place_ref[1] != 0)
    def _():
        for out_ref in (left_ref, own_ref, right_ref):
            out_ref[...] = jnp.zeros(out_ref.shape, BF16)


def terms_kernel(
    place_ref, langs_ref, dest_ref, table_ref, attn_ref, slots_ref, left_ref, own_ref, right_ref,
    home_ref, terms_ref, slot_scaled_ref, held_ref, summed_ref, sem,
):
    rank = place_ref[0]
    tiles = dest_ref.shape[1]
    fetch = pltpu.make_async_copy(slots_ref, held_ref, sem)

    @pl.when(place_ref[1] == 0)
    def _():
        fetch.start()
        fetch.wait()
        went = dest_ref[1, rank] - rank
        back = jnp.where(went < 0, left_ref[...], jnp.where(went > 0, right_ref[...], own_ref[...]))
        lows = jnp.concatenate([left_ref[...], own_ref[...], right_ref[...]], axis=0)
        for c in range(0, QW, 512):
            cols = slice(c, c + 512)
            for k in range(3):
                rows = slice(k * TILE, (k + 1) * TILE)
                rate = slot_rate(k, rank, tiles, langs_ref, dest_ref, table_ref)
                slot_scaled_ref[rows, :] = (rate * held_ref[rows, cols].astype(F32)).astype(BF16)
            one = dot(attn_ref[:, cols], back, TN)
            two = dot(slot_scaled_ref[...], lows, TN)
            terms = jnp.concatenate([one[:, RANK:], two[:, :RANK]], axis=1)
            summed_ref[cols, :] = terms.astype(BF16)
        store = pltpu.make_async_copy(summed_ref, terms_ref, sem)
        store.start()
        store.wait()


def backward_kernel(
    place_ref, langs_ref, dest_ref, table_ref, qkv_ref, left_ref, right_ref, last_left_ref,
    last_right_ref, slots_ref, probs_ref, attn_ref, low_ref, down_ref, up_ref, grad_ref, terms_ref,
    gattn_ref, scaled_ref, mid_ref, sem,
):
    rank = place_ref[0]
    rate = table_ref[langs_ref[1, rank]]
    went = dest_ref[1, rank] - rank
    last = place_ref[1] == place_ref[2] - 1
    active = place_ref[1] != 0
    fetch = pltpu.make_async_copy(slots_ref.at[pl.ds(TILE, TILE), :], mid_ref, sem)

    def chosen():
        fetch.start()
        fetch.wait()
        back = jnp.zeros((TILE, RANK), F32)
        for c in range(0, QW, 512):
            cols = slice(c, c + 512)
            left = jnp.where(last, last_left_ref[:, cols], left_ref[:, cols])
            right = jnp.where(last, last_right_ref[:, cols], right_ref[:, cols])
            mid = mid_ref[:, cols]
            grad = jnp.where(went < 0, left, jnp.where(went > 0, right, mid))
            gattn_ref[:, cols] = grad
            scaled = (rate * grad.astype(F32)).astype(BF16)
            scaled_ref[:, cols] = scaled
            back = back + dot(scaled, up_ref[:, cols], NT)
        return back.astype(BF16)

    @pl.when(active)
    def _():
        back = chosen()
        for j in range(KV):
            block = slice(j * GW, (j + 1) * GW)
            gattn = gattn_ref[:, block].astype(F32) + dot(back, down_ref[:, block], NN)
            gattn_ref[:, block] = gattn.astype(BF16)
            queries = stacked(qkv_ref, j * GW)
            keys = qkv_ref[:, QW + j * HEAD_DIM : QW + (j + 1) * HEAD_DIM]
            values = qkv_ref[:, QW + KW + j * HEAD_DIM : QW + KW + (j + 1) * HEAD_DIM]
            grads = stacked(gattn_ref, j * GW)
            grad_probs = dot(grads, values, NT)
            lows, scores = [], []
            for h in range(GROUP):
                probs = probs_ref[j * GW + h * TILE : j * GW + (h + 1) * TILE, :]
                lows.append(probs.astype(BF16))
                weighed = probs * grad_probs[h * TILE : (h + 1) * TILE]
                delta = jnp.sum(weighed, axis=-1, keepdims=True)
                scores.append(((weighed - probs * delta) * SCALE).astype(BF16))
            probs_low = jnp.concatenate(lows, axis=0)
            grad_scores = jnp.concatenate(scores, axis=0)
            grad_queries = dot(grad_scores, keys, NN).astype(BF16)
            for h in range(GROUP):
                cols = slice(j * GW + h * HEAD_DIM, j * GW + (h + 1) * HEAD_DIM)
                grad_ref[:, cols] = grad_queries[h * TILE : (h + 1) * TILE]
            cols = slice(QW + j * HEAD_DIM, QW + (j + 1) * HEAD_DIM)
            grad_ref[:, cols] = dot(grad_scores, queries, TN).astype(BF16)
            cols = slice(QW + KW + j * HEAD_DIM, QW + KW + (j + 1) * HEAD_DIM)
            grad_ref[:, cols] = dot(probs_low, grads, TN).astype(BF16)
        for c in range(0, QW, 512):
            cols = slice(c, c + 512)
            one = dot(attn_ref[:, cols], back, TN)
            two = dot(scaled_ref[:, cols], low_ref[...], TN)
            terms_ref[cols, :] = jnp.concatenate([one, two], axis=1).astype(terms_ref.dtype)


COST = pl.CostEstimate(flops=2**20, bytes_accessed=2**20, transcendentals=0)
SMEM = pl.BlockSpec(memory_space=pltpu.SMEM)
VMEM = pl.BlockSpec(memory_space=pltpu.VMEM)
ANY = pl.BlockSpec(memory_space=pl.ANY)


def run_forward(rank, lengths, languages, table, qkv, down, up):
    return pl.pallas_call(
        forward_kernel,
        out_shape=jax.ShapeDtypeStruct((TILE, QW), BF16),
        in_specs=[SMEM] * 4 + [VMEM] * 3,
        out_specs=VMEM,
        scratch_shapes=[pltpu.VMEM((GROUP * TILE, TILE), F32)],
        compiler_params=pltpu.CompilerParams(vmem_limit_bytes=16 * 2**20),
        cost_estimate=COST,
        name="forward_tile",
    )(rank, lengths, languages, table, qkv, down, up)


def run_prepare(place, lengths, languages, dest, table, qkv, slots, down, up):
    message = jax.ShapeDtypeStruct((TILE, 2 * RANK), BF16)
    return pl.pallas_call(
        prepare_kernel,
        out_shape=(
            jax.ShapeDtypeStruct((QW, TILE), F32),
            jax.ShapeDtypeStruct((TILE, QW), BF16),
            jax.ShapeDtypeStruct((TILE, RANK), BF16),
            message,
            message,
            message,
        ),
        in_specs=[SMEM] * 5 + [VMEM, ANY, VMEM, VMEM],
        out_specs=(VMEM,) * 6,
        scratch_shapes=[pltpu.VMEM((3 * TILE, QW), BF16), pltpu.SemaphoreType.DMA],
        compiler_params=pltpu.CompilerParams(vmem_limit_bytes=22 * 2**20),
        cost_estimate=COST,
        name="prepare_tile",
    )(place, lengths, languages, dest, table, qkv, slots, down, up)


def run_terms(place, languages, dest, table, attn, slots, left, own, right, home):
    return pl.pallas_call(
        terms_kernel,
        out_shape=jax.ShapeDtypeStruct((QW, 2 * RANK), BF16),
        in_specs=[SMEM] * 4 + [VMEM, ANY] + [VMEM] * 3 + [ANY],
        input_output_aliases={9: 0},
        out_specs=ANY,
        scratch_shapes=[
            pltpu.VMEM((3 * TILE, 512), BF16),
            pltpu.VMEM((3 * TILE, QW), BF16),
            pltpu.VMEM((QW, 2 * RANK), BF16),
            pltpu.SemaphoreType.DMA,
        ],
        compiler_params=pltpu.CompilerParams(vmem_limit_bytes=22 * 2**20),
        cost_estimate=COST,
        name="adapter_terms",
    )(place, languages, dest, table, attn, slots, left, own, right, home)


def run_backward(place, languages, dest, table, qkv, moved, slots, probs, attn, low, down, up):
    return pl.pallas_call(
        backward_kernel,
        out_shape=(
            jax.ShapeDtypeStruct((TILE, QW + 2 * KW), BF16),
            jax.ShapeDtypeStruct((QW, 2 * RANK), BF16),
        ),
        in_specs=[SMEM] * 4 + [VMEM] * 5 + [ANY] + [VMEM] * 5,
        out_specs=(VMEM, VMEM),
        scratch_shapes=[
            pltpu.VMEM((TILE, QW), BF16),
            pltpu.VMEM((TILE, QW), BF16),
            pltpu.VMEM((TILE, QW), BF16),
            pltpu.SemaphoreType.DMA,
        ],
        compiler_params=pltpu.CompilerParams(vmem_limit_bytes=24 * 2**20),
        cost_estimate=COST,
        name="backward_tile",
    )(place, languages, dest, table, qkv, *moved, slots, probs, attn, low, down, up)


def place_kernel(
    place_ref, dest_ref, before_ref, hop_ref, after_ref, ends_ref, back_ref,
    placed_ref, handed_ref, zero_ref, sems,
):
    rank, section = place_ref[0], place_ref[1]
    tiles = dest_ref.shape[1]
    zero_ref[...] = jnp.zeros(zero_ref.shape, BF16)
    handed = pltpu.make_async_copy(back_ref, handed_ref, sems.at[0])
    handed.start()
    copies = []
    for k, (near, edge) in enumerate(
        ((before_ref, run_start(rank)), (hop_ref, False), (after_ref, run_end(rank)))
    ):
        tile = rank + (k - 1)
        held = jnp.clip(tile, 0, tiles - 1)
        live = (tile == held) & (dest_ref[0, held] == rank) & (section > 0)
        crossed = (section == 2) & edge
        slot = placed_ref.at[pl.ds(k * TILE, TILE), :]
        for source, chosen in (
            (near, live & jnp.logical_not(crossed)),
            (ends_ref, live & crossed),
            (zero_ref, jnp.logical_not(live)),
        ):
            copies.append((pltpu.make_async_copy(source, slot, sems.at[k + 1]), chosen))
    for copy, chosen in copies:
        pl.when(chosen)(copy.start)
    for copy, chosen in copies:
        pl.when(chosen)(copy.wait)
    handed.wait()


def run_place(place, dest, *tiles):
    return pl.pallas_call(
        place_kernel,
        out_shape=(
            jax.ShapeDtypeStruct((3 * TILE, QW), BF16),
            jax.ShapeDtypeStruct(tiles[-1].shape, BF16),
        ),
        in_specs=[SMEM] * 2 + [VMEM] * len(tiles),
        out_specs=(ANY, ANY),
        scratch_shapes=[pltpu.VMEM((TILE, QW), BF16), pltpu.SemaphoreType.DMA((4,))],
        compiler_params=pltpu.CompilerParams(vmem_limit_bytes=24 * 2**20),
        cost_estimate=COST,
        name="place_outputs",
    )(place, dest, *tiles)


def sections():
    return lax.axis_size("section")


def shift(x, moves):
    size = lax.axis_size("dp")
    route = []
    for s_list, up, step, keep in moves:
        for s in s_list:
            for t in range(size):
                if 0 <= s + up < sections() and 0 <= t + step < size and keep(t):
                    route.append((s * size + t, (s + up) * size + t + step))
    return lax.ppermute(x, AXES, route)


def anywhere(t):
    return True


def run_start(t):
    return t % RUN == 0


def run_end(t):
    return t % RUN == RUN - 1


def after_run_start(t):
    return t % RUN == 1


def before_run_end(t):
    return t % RUN == RUN - 2


def not_run_start(t):
    return t % RUN != 0


def not_run_end(t):
    return t % RUN != RUN - 1


def scatter(x, groups):
    return lax.all_to_all(x, "dp", 0, 0, axis_index_groups=groups, tiled=True)


def shards(
    qkv_a, qkv_b, slot_grad_b, adapter_down, adapter_up, lang_scale, languages, lengths, destination
):
    rank, size = lax.axis_index("dp"), lax.axis_size("dp")
    section, last = lax.axis_index("section"), sections() - 1
    place = jnp.stack([rank, section, jnp.int32(sections())]).astype(jnp.int32)
    down, up = adapter_down[0].T, adapter_up[0]
    slots = slot_grad_b[0]
    every, early = range(sections()), range(1, last)
    to_up, to_down = slots[2 * TILE :], slots[:TILE]
    from_left = shift(to_up, [(early, 0, 1, anywhere)])
    from_right = shift(to_down, [(early, 0, -1, anywhere)])
    out = run_forward(place, lengths, languages, lang_scale, qkv_a[0], down, up)
    out, place = lax.optimization_barrier((out, place))
    near = shift(out, [([0, 2], 1, 0, anywhere)])
    probs, attn, low, to_left, own, to_right = run_prepare(
        place, lengths, languages, destination, lang_scale, qkv_b[0], slots, down, up
    )
    from_left, from_right, low = lax.optimization_barrier((from_left, from_right, low))
    to_up, to_down, near, low = lax.optimization_barrier((to_up, to_down, near, low))
    last_left = shift(to_up, [([last], 0, 1, anywhere)])
    last_right = shift(to_down, [([last], 0, -1, anywhere)])
    far = shift(
        jnp.where(section == last, near, out),
        [([1], 1, 0, anywhere), ([last], -last, -1, run_end), ([last], -last, 1, run_start)],
    )
    grad_qkv, terms = run_backward(
        place, languages, destination, lang_scale, qkv_b[0],
        (from_left, from_right, last_left, last_right), slots, probs, attn, low, down, up,
    )
    grad_qkv, near, to_left, to_right = lax.optimization_barrier(
        (grad_qkv, near, to_left, to_right)
    )
    handed_back = shift(grad_qkv, [(every, -1, 0, anywhere)])
    left = shift(to_right, [([0], 0, 1, anywhere)])
    right = shift(to_left, [([0], 0, -1, anywhere)])
    terms = run_terms(
        place, languages, destination, lang_scale, attn, slots, left, own, right, terms
    )
    planes = [[RUN * k + z for k in range(size // RUN)] for z in range(RUN)]
    columns = [[RUN * k + z for z in range(RUN)] for k in range(size // RUN)]
    far, terms, out = lax.optimization_barrier((far, terms, out))
    pieces = scatter(terms.reshape(size // RUN, -1, 2 * RANK), planes)
    hop = jnp.where((section == 1) | (section == last), near, far)
    before = shift(
        hop,
        [([1], 0, 1, anywhere), ([2, last], 0, 1, not_run_end), ([0], last, 2, before_run_end)],
    )
    after = shift(
        hop,
        [([1], 0, -1, anywhere), ([2, last], 0, -1, not_run_start), ([0], last, -2, after_run_start)],
    )
    ends = shift(out, [([1], 1, 1, run_end), ([1], 1, -1, run_start)])
    pieces, _ = lax.optimization_barrier((pieces, handed_back))
    terms = jnp.sum(pieces.astype(F32), axis=0)
    terms = jnp.sum(scatter(terms.reshape(RUN, -1, 2 * RANK), columns), axis=0)
    handed_forward, handed_back = run_place(
        place, destination, before, hop, after, ends, handed_back
    )
    return (handed_forward[None], handed_back[None], terms[None])


def solution(mesh):
    return jax.shard_map(
        shards,
        mesh=mesh,
        in_specs=(
            P("section", "dp", None),
            P("section", "dp", None),
            P("section", "dp", None),
            P("section", None, None),
            P("section", None, None),
            P(),
            P(),
            P(),
            P(),
        ),
        out_specs=(P("section", "dp", None), P("section", "dp", None), P("section", "dp", None)),
        check_vma=False,
    )
```

```python
import functools
import math

import jax
import jax.numpy as jnp
from jax import lax
from jax.experimental import pallas as pl
from jax.experimental.pallas import tpu as pltpu
from jax.sharding import PartitionSpec as P

HEADS = 32
KV = 4
GROUP = HEADS // KV
HEAD_DIM = 128
TILE = 128
SEGS = 8
RANK = 64
QW = HEADS * HEAD_DIM
KW = KV * HEAD_DIM
GW = GROUP * HEAD_DIM
SCALE = 1.0 / math.sqrt(HEAD_DIM)
RUN = 4
AXES = ("section", "dp")
BF16 = jnp.bfloat16
F32 = jnp.float32


def dot(a, b, dims):
    return lax.dot_general(a, b, (dims, ((), ())), preferred_element_type=F32)


NN = ((1,), (0,))
NT = ((1,), (1,))
TN = ((0,), (0,))


def mask_bias(lens_ref, m, rank):
    shape = (TILE, TILE)
    row = lax.broadcasted_iota(jnp.int32, shape, 0)
    col = lax.broadcasted_iota(jnp.int32, shape, 1)
    seg_row = jnp.zeros(shape, jnp.int32)
    seg_col = jnp.zeros(shape, jnp.int32)
    end = jnp.int32(0)
    for k in range(SEGS):
        end = end + lens_ref[m, rank, k]
        seg_row = seg_row + (row >= end).astype(jnp.int32)
        seg_col = seg_col + (col >= end).astype(jnp.int32)
    allowed = (seg_row == seg_col) & (row >= col)
    return jnp.where(allowed, 0.0, -1e30).astype(F32)


def stacked(ref, base):
    return jnp.concatenate(
        [ref[:, base + h * HEAD_DIM : base + (h + 1) * HEAD_DIM] for h in range(GROUP)], axis=0
    )


def softmax(scores, bias):
    masked = scores + bias
    top = jnp.max(masked, axis=-1, keepdims=True)
    weights = jnp.exp2((masked - top) * (SCALE * math.log2(math.e)))
    return weights * (1.0 / jnp.sum(weights, axis=-1, keepdims=True))


def attend_group(j, qkv_ref, bias, probs_ref):
    keys = qkv_ref[:, QW + j * HEAD_DIM : QW + (j + 1) * HEAD_DIM]
    values = qkv_ref[:, QW + KW + j * HEAD_DIM : QW + KW + (j + 1) * HEAD_DIM]
    queries = stacked(qkv_ref, j * GW)
    probs_ref[...] = dot(queries, keys, NT)
    lows = []
    for h in range(GROUP):
        rows = slice(h * TILE, (h + 1) * TILE)
        probs = softmax(probs_ref[rows, :], bias)
        probs_ref[rows, :] = probs
        lows.append(probs.astype(BF16))
    probs_low = jnp.concatenate(lows, axis=0)
    attn = dot(probs_low, values, NN).astype(BF16)
    return queries, keys, values, probs_low, attn


def forward_kernel(rank_ref, lens_ref, langs_ref, table_ref, qkv_ref, down_ref, up_ref, out_ref, probs_ref):
    rank = rank_ref[0]
    rate = table_ref[langs_ref[0, rank]]
    bias = mask_bias(lens_ref, 0, rank)
    low = jnp.zeros((TILE, RANK), F32)
    for j in range(KV):
        attn = attend_group(j, qkv_ref, bias, probs_ref)[-1]
        for h in range(GROUP):
            cols = slice(j * GW + h * HEAD_DIM, j * GW + (h + 1) * HEAD_DIM)
            out_ref[:, cols] = attn[h * TILE : (h + 1) * TILE]
        block = slice(j * GW, (j + 1) * GW)
        low = low + dot(out_ref[:, block], down_ref[:, block], NT)
    low = low.astype(BF16)
    for c in range(0, QW, 512):
        lift = dot(low, up_ref[:, c : c + 512], NN)
        out_ref[:, c : c + 512] = (out_ref[:, c : c + 512].astype(F32) + rate * lift).astype(BF16)


def slot_rate(k, rank, tiles, langs_ref, dest_ref, table_ref):
    tile = rank + (k - 1)
    near = jnp.clip(tile, 0, tiles - 1)
    live = (tile == near) & (dest_ref[1, near] == rank)
    return jnp.where(live, table_ref[langs_ref[1, near]], 0.0)


def prepare_kernel(
    place_ref, lens_ref, langs_ref, dest_ref, table_ref, qkv_ref, slots_ref, down_ref, up_ref,
    probs_ref, attn_ref, low_ref, left_ref, own_ref, right_ref, held_ref, sem,
):
    rank = place_ref[0]
    tiles = lens_ref.shape[1]
    fetch = pltpu.make_async_copy(slots_ref, held_ref, sem)
    pl.when(place_ref[1] == 0)(fetch.start)
    bias = mask_bias(lens_ref, 1, rank)
    low = jnp.zeros((TILE, RANK), F32)
    for j in range(KV):
        block = slice(j * GW, (j + 1) * GW)
        attn = attend_group(j, qkv_ref, bias, probs_ref.at[block, :])[-1]
        for h in range(GROUP):
            cols = slice(j * GW + h * HEAD_DIM, j * GW + (h + 1) * HEAD_DIM)
            attn_ref[:, cols] = attn[h * TILE : (h + 1) * TILE]
        low = low + dot(attn_ref[:, block], down_ref[:, block], NT)
    low_ref[...] = low.astype(BF16)

    @pl.when(place_ref[1] == 0)
    def _():
        fetch.wait()
        for k, out_ref in enumerate((left_ref, own_ref, right_ref)):
            rate = slot_rate(k, rank, tiles, langs_ref, dest_ref, table_ref)
            back = jnp.zeros((TILE, RANK), F32)
            for c in range(0, QW, 512):
                cols = slice(c, c + 512)
                grad = held_ref[k * TILE : (k + 1) * TILE, cols]
                scaled = (rate * grad.astype(F32)).astype(BF16)
                back = back + dot(scaled, up_ref[:, cols], NT)
            out_ref[...] = jnp.concatenate([low, back], axis=1).astype(BF16)

    @pl.when(place_ref[1] != 0)
    def _():
        for out_ref in (left_ref, own_ref, right_ref):
            out_ref[...] = jnp.zeros(out_ref.shape, BF16)


def terms_kernel(
    place_ref, langs_ref, dest_ref, table_ref, attn_ref, slots_ref, left_ref, own_ref, right_ref,
    home_ref, terms_ref, slot_scaled_ref, held_ref, summed_ref, sem,
):
    rank = place_ref[0]
    tiles = dest_ref.shape[1]
    fetch = pltpu.make_async_copy(slots_ref, held_ref, sem)

    @pl.when(place_ref[1] == 0)
    def _():
        fetch.start()
        fetch.wait()
        went = dest_ref[1, rank] - rank
        back = jnp.where(went < 0, left_ref[...], jnp.where(went > 0, right_ref[...], own_ref[...]))
        lows = jnp.concatenate([left_ref[...], own_ref[...], right_ref[...]], axis=0)
        for c in range(0, QW, 512):
            cols = slice(c, c + 512)
            for k in range(3):
                rows = slice(k * TILE, (k + 1) * TILE)
                rate = slot_rate(k, rank, tiles, langs_ref, dest_ref, table_ref)
                slot_scaled_ref[rows, :] = (rate * held_ref[rows, cols].astype(F32)).astype(BF16)
            one = dot(attn_ref[:, cols], back, TN)
            two = dot(slot_scaled_ref[...], lows, TN)
            terms = jnp.concatenate([one[:, RANK:], two[:, :RANK]], axis=1)
            summed_ref[cols, :] = terms.astype(BF16)
        store = pltpu.make_async_copy(summed_ref, terms_ref, sem)
        store.start()
        store.wait()


def backward_kernel(
    place_ref, langs_ref, dest_ref, table_ref, qkv_ref, left_ref, right_ref, last_left_ref,
    last_right_ref, slots_ref, probs_ref, attn_ref, low_ref, down_ref, up_ref, grad_ref, terms_ref,
    gattn_ref, scaled_ref, mid_ref, sem,
):
    rank = place_ref[0]
    rate = table_ref[langs_ref[1, rank]]
    went = dest_ref[1, rank] - rank
    last = place_ref[1] == place_ref[2] - 1
    active = place_ref[1] != 0
    fetch = pltpu.make_async_copy(slots_ref.at[pl.ds(TILE, TILE), :], mid_ref, sem)

    def chosen():
        fetch.start()
        fetch.wait()
        back = jnp.zeros((TILE, RANK), F32)
        for c in range(0, QW, 512):
            cols = slice(c, c + 512)
            left = jnp.where(last, last_left_ref[:, cols], left_ref[:, cols])
            right = jnp.where(last, last_right_ref[:, cols], right_ref[:, cols])
            mid = mid_ref[:, cols]
            grad = jnp.where(went < 0, left, jnp.where(went > 0, right, mid))
            gattn_ref[:, cols] = grad
            scaled = (rate * grad.astype(F32)).astype(BF16)
            scaled_ref[:, cols] = scaled
            back = back + dot(scaled, up_ref[:, cols], NT)
        return back.astype(BF16)

    @pl.when(active)
    def _():
        back = chosen()
        for j in range(KV):
            block = slice(j * GW, (j + 1) * GW)
            gattn = gattn_ref[:, block].astype(F32) + dot(back, down_ref[:, block], NN)
            gattn_ref[:, block] = gattn.astype(BF16)
            queries = stacked(qkv_ref, j * GW)
            keys = qkv_ref[:, QW + j * HEAD_DIM : QW + (j + 1) * HEAD_DIM]
            values = qkv_ref[:, QW + KW + j * HEAD_DIM : QW + KW + (j + 1) * HEAD_DIM]
            grads = stacked(gattn_ref, j * GW)
            grad_probs = dot(grads, values, NT)
            lows, scores = [], []
            for h in range(GROUP):
                probs = probs_ref[j * GW + h * TILE : j * GW + (h + 1) * TILE, :]
                lows.append(probs.astype(BF16))
                weighed = probs * grad_probs[h * TILE : (h + 1) * TILE]
                delta = jnp.sum(weighed, axis=-1, keepdims=True)
                scores.append(((weighed - probs * delta) * SCALE).astype(BF16))
            probs_low = jnp.concatenate(lows, axis=0)
            grad_scores = jnp.concatenate(scores, axis=0)
            grad_queries = dot(grad_scores, keys, NN).astype(BF16)
            for h in range(GROUP):
                cols = slice(j * GW + h * HEAD_DIM, j * GW + (h + 1) * HEAD_DIM)
                grad_ref[:, cols] = grad_queries[h * TILE : (h + 1) * TILE]
            cols = slice(QW + j * HEAD_DIM, QW + (j + 1) * HEAD_DIM)
            grad_ref[:, cols] = dot(grad_scores, queries, TN).astype(BF16)
            cols = slice(QW + KW + j * HEAD_DIM, QW + KW + (j + 1) * HEAD_DIM)
            grad_ref[:, cols] = dot(probs_low, grads, TN).astype(BF16)
        for c in range(0, QW, 512):
            cols = slice(c, c + 512)
            one = dot(attn_ref[:, cols], back, TN)
            two = dot(scaled_ref[:, cols], low_ref[...], TN)
            terms_ref[cols, :] = jnp.concatenate([one, two], axis=1).astype(terms_ref.dtype)


COST = pl.CostEstimate(flops=2**20, bytes_accessed=2**20, transcendentals=0)
SMEM = pl.BlockSpec(memory_space=pltpu.SMEM)
VMEM = pl.BlockSpec(memory_space=pltpu.VMEM)
ANY = pl.BlockSpec(memory_space=pl.ANY)


def run_forward(rank, lengths, languages, table, qkv, down, up):
    return pl.pallas_call(
        forward_kernel,
        out_shape=jax.ShapeDtypeStruct((TILE, QW), BF16),
        in_specs=[SMEM] * 4 + [VMEM] * 3,
        out_specs=VMEM,
        scratch_shapes=[pltpu.VMEM((GROUP * TILE, TILE), F32)],
        compiler_params=pltpu.CompilerParams(vmem_limit_bytes=16 * 2**20),
        cost_estimate=COST,
        name="forward_tile",
    )(rank, lengths, languages, table, qkv, down, up)


def run_prepare(place, lengths, languages, dest, table, qkv, slots, down, up):
    message = jax.ShapeDtypeStruct((TILE, 2 * RANK), BF16)
    return pl.pallas_call(
        prepare_kernel,
        out_shape=(
            jax.ShapeDtypeStruct((QW, TILE), F32),
            jax.ShapeDtypeStruct((TILE, QW), BF16),
            jax.ShapeDtypeStruct((TILE, RANK), BF16),
            message,
            message,
            message,
        ),
        in_specs=[SMEM] * 5 + [VMEM, ANY, VMEM, VMEM],
        out_specs=(VMEM,) * 6,
        scratch_shapes=[pltpu.VMEM((3 * TILE, QW), BF16), pltpu.SemaphoreType.DMA],
        compiler_params=pltpu.CompilerParams(vmem_limit_bytes=22 * 2**20),
        cost_estimate=COST,
        name="prepare_tile",
    )(place, lengths, languages, dest, table, qkv, slots, down, up)


def run_terms(place, languages, dest, table, attn, slots, left, own, right, home):
    return pl.pallas_call(
        terms_kernel,
        out_shape=jax.ShapeDtypeStruct((QW, 2 * RANK), BF16),
        in_specs=[SMEM] * 4 + [VMEM, ANY] + [VMEM] * 3 + [ANY],
        input_output_aliases={9: 0},
        out_specs=ANY,
        scratch_shapes=[
            pltpu.VMEM((3 * TILE, 512), BF16),
            pltpu.VMEM((3 * TILE, QW), BF16),
            pltpu.VMEM((QW, 2 * RANK), BF16),
            pltpu.SemaphoreType.DMA,
        ],
        compiler_params=pltpu.CompilerParams(vmem_limit_bytes=22 * 2**20),
        cost_estimate=COST,
        name="adapter_terms",
    )(place, languages, dest, table, attn, slots, left, own, right, home)


def run_backward(place, languages, dest, table, qkv, moved, slots, probs, attn, low, down, up):
    return pl.pallas_call(
        backward_kernel,
        out_shape=(
            jax.ShapeDtypeStruct((TILE, QW + 2 * KW), BF16),
            jax.ShapeDtypeStruct((QW, 2 * RANK), BF16),
        ),
        in_specs=[SMEM] * 4 + [VMEM] * 5 + [ANY] + [VMEM] * 5,
        out_specs=(VMEM, VMEM),
        scratch_shapes=[
            pltpu.VMEM((TILE, QW), BF16),
            pltpu.VMEM((TILE, QW), BF16),
            pltpu.VMEM((TILE, QW), BF16),
            pltpu.SemaphoreType.DMA,
        ],
        compiler_params=pltpu.CompilerParams(vmem_limit_bytes=24 * 2**20),
        cost_estimate=COST,
        name="backward_tile",
    )(place, languages, dest, table, qkv, *moved, slots, probs, attn, low, down, up)


def place_kernel(
    place_ref, dest_ref, before_ref, near_ref, after_ref, far_before_ref, far_ref, far_after_ref,
    back_ref, placed_ref, handed_ref, zero_ref, sems,
):
    rank, section = place_ref[0], place_ref[1]
    tiles = dest_ref.shape[1]
    zero_ref[...] = jnp.zeros(zero_ref.shape, BF16)
    handed = pltpu.make_async_copy(back_ref, handed_ref, sems.at[0])
    handed.start()
    copies = []
    for k, (near, far) in enumerate(
        ((before_ref, far_before_ref), (near_ref, far_ref), (after_ref, far_after_ref))
    ):
        tile = rank + (k - 1)
        held = jnp.clip(tile, 0, tiles - 1)
        live = (tile == held) & (dest_ref[0, held] == rank) & (section > 0)
        slot = placed_ref.at[pl.ds(k * TILE, TILE), :]
        for source, chosen in (
            (near, live & (section != 2)),
            (far, live & (section == 2)),
            (zero_ref, jnp.logical_not(live)),
        ):
            copies.append((pltpu.make_async_copy(source, slot, sems.at[k + 1]), chosen))
    for copy, chosen in copies:
        pl.when(chosen)(copy.start)
    for copy, chosen in copies:
        pl.when(chosen)(copy.wait)
    handed.wait()


def run_place(place, dest, *tiles):
    return pl.pallas_call(
        place_kernel,
        out_shape=(
            jax.ShapeDtypeStruct((3 * TILE, QW), BF16),
            jax.ShapeDtypeStruct(tiles[-1].shape, BF16),
        ),
        in_specs=[SMEM] * 2 + [VMEM] * len(tiles),
        out_specs=(ANY, ANY),
        scratch_shapes=[pltpu.VMEM((TILE, QW), BF16), pltpu.SemaphoreType.DMA((4,))],
        compiler_params=pltpu.CompilerParams(vmem_limit_bytes=24 * 2**20),
        cost_estimate=COST,
        name="place_outputs",
    )(place, dest, *tiles)


def sections():
    return lax.axis_size("section")


def shift(x, moves):
    size = lax.axis_size("dp")
    route = []
    for s_list, up, step, keep in moves:
        for s in s_list:
            for t in range(size):
                if 0 <= s + up < sections() and 0 <= t + step < size and keep(t):
                    route.append((s * size + t, (s + up) * size + t + step))
    return lax.ppermute(x, AXES, route)


def anywhere(t):
    return True


def run_start(t):
    return t % RUN == 0


def run_end(t):
    return t % RUN == RUN - 1


def not_run_start(t):
    return t % RUN != 0


def not_run_end(t):
    return t % RUN != RUN - 1


def scatter(x, groups):
    return lax.all_to_all(x, "dp", 0, 0, axis_index_groups=groups, tiled=True)


def shards(
    qkv_a, qkv_b, slot_grad_b, adapter_down, adapter_up, lang_scale, languages, lengths, destination
):
    rank, size = lax.axis_index("dp"), lax.axis_size("dp")
    section, last = lax.axis_index("section"), sections() - 1
    place = jnp.stack([rank, section, jnp.int32(sections())]).astype(jnp.int32)
    down, up = adapter_down[0].T, adapter_up[0]
    slots = slot_grad_b[0]
    every, early = range(sections()), range(1, last)
    to_up, to_down = slots[2 * TILE :], slots[:TILE]
    from_left = shift(to_up, [(early, 0, 1, anywhere)])
    from_right = shift(to_down, [(early, 0, -1, anywhere)])
    out = run_forward(place, lengths, languages, lang_scale, qkv_a[0], down, up)
    out, place = lax.optimization_barrier((out, place))
    near = shift(out, [([0, 2], 1, 0, anywhere)])
    far = shift(out, [([1], 1, 0, anywhere)])
    probs, attn, low, to_left, own, to_right = run_prepare(
        place, lengths, languages, destination, lang_scale, qkv_b[0], slots, down, up
    )
    from_left, from_right, low = lax.optimization_barrier((from_left, from_right, low))
    to_up, to_down, near, low = lax.optimization_barrier((to_up, to_down, near, low))
    last_left = shift(to_up, [([last], 0, 1, anywhere)])
    last_right = shift(to_down, [([last], 0, -1, anywhere)])
    grad_qkv, terms = run_backward(
        place, languages, destination, lang_scale, qkv_b[0],
        (from_left, from_right, last_left, last_right), slots, probs, attn, low, down, up,
    )
    grad_qkv, near, to_left, to_right = lax.optimization_barrier(
        (grad_qkv, near, to_left, to_right)
    )
    handed_back = shift(grad_qkv, [(every, -1, 0, anywhere)])
    before = shift(near, [([1, last], 0, 1, anywhere)])
    after = shift(near, [([1, last], 0, -1, anywhere)])
    left = shift(to_right, [([0], 0, 1, anywhere)])
    right = shift(to_left, [([0], 0, -1, anywhere)])
    terms = run_terms(
        place, languages, destination, lang_scale, attn, slots, left, own, right, terms
    )
    planes = [[RUN * k + z for k in range(size // RUN)] for z in range(RUN)]
    columns = [[RUN * k + z for z in range(RUN)] for k in range(size // RUN)]
    far, terms = lax.optimization_barrier((far, terms))
    pieces = scatter(terms.reshape(size // RUN, -1, 2 * RANK), planes)
    sent = jnp.where(section == 2, far, out)
    far_before = shift(sent, [([1], 1, 1, run_end), ([2], 0, 1, not_run_end)])
    far_after = shift(sent, [([1], 1, -1, run_start), ([2], 0, -1, not_run_start)])
    pieces, _, before, after = lax.optimization_barrier((pieces, handed_back, before, after))
    terms = jnp.sum(pieces.astype(F32), axis=0)
    terms = jnp.sum(scatter(terms.reshape(RUN, -1, 2 * RANK), columns), axis=0)
    handed_forward, handed_back = run_place(
        place, destination, before, near, after, far_before, far, far_after, handed_back
    )
    return (handed_forward[None], handed_back[None], terms[None])


def solution(mesh):
    return jax.shard_map(
        shards,
        mesh=mesh,
        in_specs=(
            P("section", "dp", None),
            P("section", "dp", None),
            P("section", "dp", None),
            P("section", None, None),
            P("section", None, None),
            P(),
            P(),
            P(),
            P(),
        ),
        out_specs=(P("section", "dp", None), P("section", "dp", None), P("section", "dp", None)),
        check_vma=False,
    )
```

```python
import functools
import math

import jax
import jax.numpy as jnp
from jax import lax
from jax.experimental import pallas as pl
from jax.experimental.pallas import tpu as pltpu
from jax.sharding import PartitionSpec as P

HEADS = 32
KV = 4
GROUP = HEADS // KV
HEAD_DIM = 128
TILE = 128
SEGS = 8
RANK = 64
QW = HEADS * HEAD_DIM
KW = KV * HEAD_DIM
GW = GROUP * HEAD_DIM
SCALE = 1.0 / math.sqrt(HEAD_DIM)
RUN = 4
AXES = ("section", "dp")
BF16 = jnp.bfloat16
F32 = jnp.float32


def dot(a, b, dims):
    return lax.dot_general(a, b, (dims, ((), ())), preferred_element_type=F32)


NN = ((1,), (0,))
NT = ((1,), (1,))
TN = ((0,), (0,))


def mask_bias(lens_ref, m, rank):
    shape = (TILE, TILE)
    row = lax.broadcasted_iota(jnp.int32, shape, 0)
    col = lax.broadcasted_iota(jnp.int32, shape, 1)
    seg_row = jnp.zeros(shape, jnp.int32)
    seg_col = jnp.zeros(shape, jnp.int32)
    end = jnp.int32(0)
    for k in range(SEGS):
        end = end + lens_ref[m, rank, k]
        seg_row = seg_row + (row >= end).astype(jnp.int32)
        seg_col = seg_col + (col >= end).astype(jnp.int32)
    allowed = (seg_row == seg_col) & (row >= col)
    return jnp.where(allowed, 0.0, -1e30).astype(F32)


def stacked(ref, base):
    return jnp.concatenate(
        [ref[:, base + h * HEAD_DIM : base + (h + 1) * HEAD_DIM] for h in range(GROUP)], axis=0
    )


def softmax(scores, bias):
    masked = scores + bias
    top = jnp.max(masked, axis=-1, keepdims=True)
    weights = jnp.exp2((masked - top) * (SCALE * math.log2(math.e)))
    return weights * (1.0 / jnp.sum(weights, axis=-1, keepdims=True))


def attend_group(j, qkv_ref, bias, probs_ref):
    keys = qkv_ref[:, QW + j * HEAD_DIM : QW + (j + 1) * HEAD_DIM]
    values = qkv_ref[:, QW + KW + j * HEAD_DIM : QW + KW + (j + 1) * HEAD_DIM]
    queries = stacked(qkv_ref, j * GW)
    probs_ref[...] = dot(queries, keys, NT)
    lows = []
    for h in range(GROUP):
        rows = slice(h * TILE, (h + 1) * TILE)
        probs = softmax(probs_ref[rows, :], bias)
        probs_ref[rows, :] = probs
        lows.append(probs.astype(BF16))
    probs_low = jnp.concatenate(lows, axis=0)
    attn = dot(probs_low, values, NN).astype(BF16)
    return queries, keys, values, probs_low, attn


def forward_kernel(rank_ref, lens_ref, langs_ref, table_ref, qkv_ref, down_ref, up_ref, out_ref, probs_ref):
    rank = rank_ref[0]
    rate = table_ref[langs_ref[0, rank]]
    bias = mask_bias(lens_ref, 0, rank)
    low = jnp.zeros((TILE, RANK), F32)
    for j in range(KV):
        attn = attend_group(j, qkv_ref, bias, probs_ref)[-1]
        for h in range(GROUP):
            cols = slice(j * GW + h * HEAD_DIM, j * GW + (h + 1) * HEAD_DIM)
            out_ref[:, cols] = attn[h * TILE : (h + 1) * TILE]
        low = low + dot(out_ref[:, j * GW : (j + 1) * GW], down_ref[j * GW : (j + 1) * GW, :], NN)
    low = low.astype(BF16)
    for c in range(0, QW, 512):
        lift = dot(low, up_ref[:, c : c + 512], NN)
        out_ref[:, c : c + 512] = (out_ref[:, c : c + 512].astype(F32) + rate * lift).astype(BF16)


def slot_rate(k, rank, tiles, langs_ref, dest_ref, table_ref):
    tile = rank + (k - 1)
    near = jnp.clip(tile, 0, tiles - 1)
    live = (tile == near) & (dest_ref[1, near] == rank)
    return jnp.where(live, table_ref[langs_ref[1, near]], 0.0)


def prepare_kernel(
    place_ref, lens_ref, langs_ref, dest_ref, table_ref, qkv_ref, slots_ref, down_ref, up_ref,
    probs_ref, attn_ref, low_ref, left_ref, own_ref, right_ref,
):
    rank = place_ref[0]
    tiles = lens_ref.shape[1]
    bias = mask_bias(lens_ref, 1, rank)
    low = jnp.zeros((TILE, RANK), F32)
    for j in range(KV):
        block = slice(j * GW, (j + 1) * GW)
        attn = attend_group(j, qkv_ref, bias, probs_ref.at[block, :])[-1]
        for h in range(GROUP):
            cols = slice(j * GW + h * HEAD_DIM, j * GW + (h + 1) * HEAD_DIM)
            attn_ref[:, cols] = attn[h * TILE : (h + 1) * TILE]
        low = low + dot(attn_ref[:, block], down_ref[block, :], NN)
    low_ref[...] = low.astype(BF16)

    @pl.when(place_ref[1] == 0)
    def _():
        for k, out_ref in enumerate((left_ref, own_ref, right_ref)):
            rate = slot_rate(k, rank, tiles, langs_ref, dest_ref, table_ref)
            back = jnp.zeros((TILE, RANK), F32)
            for c in range(0, QW, 512):
                cols = slice(c, c + 512)
                grad = slots_ref[k * TILE : (k + 1) * TILE, cols]
                scaled = (rate * grad.astype(F32)).astype(BF16)
                back = back + dot(scaled, up_ref[:, cols], NT)
            out_ref[...] = jnp.concatenate([low, back], axis=1).astype(BF16)

    @pl.when(place_ref[1] != 0)
    def _():
        for out_ref in (left_ref, own_ref, right_ref):
            out_ref[...] = jnp.zeros(out_ref.shape, BF16)


def terms_kernel(
    place_ref, langs_ref, dest_ref, table_ref, attn_ref, slots_ref, left_ref, own_ref, right_ref,
    scaled_ref, back_ref, low_ref, terms_ref, slot_scaled_ref,
):
    rank = place_ref[0]
    tiles = dest_ref.shape[1]

    @pl.when(place_ref[1] == 0)
    def _():
        went = dest_ref[1, rank] - rank
        back = jnp.where(went < 0, left_ref[...], jnp.where(went > 0, right_ref[...], own_ref[...]))
        lows = jnp.concatenate([left_ref[...], own_ref[...], right_ref[...]], axis=0)
        for c in range(0, QW, 512):
            cols = slice(c, c + 512)
            for k in range(3):
                rows = slice(k * TILE, (k + 1) * TILE)
                rate = slot_rate(k, rank, tiles, langs_ref, dest_ref, table_ref)
                slot_scaled_ref[rows, :] = (rate * slots_ref[rows, cols].astype(F32)).astype(BF16)
            one = dot(attn_ref[:, cols], back, TN)
            two = dot(slot_scaled_ref[...], lows, TN)
            terms = jnp.concatenate([one[:, RANK:], two[:, :RANK]], axis=1)
            terms_ref[cols, :] = terms.astype(terms_ref.dtype)

    @pl.when(place_ref[1] != 0)
    def _():
        for c in range(0, QW, 512):
            cols = slice(c, c + 512)
            one = dot(attn_ref[:, cols], back_ref[...], TN)
            two = dot(scaled_ref[:, cols], low_ref[...], TN)
            terms_ref[cols, :] = jnp.concatenate([one, two], axis=1).astype(terms_ref.dtype)


def backward_kernel(
    place_ref, langs_ref, dest_ref, table_ref, qkv_ref, left_ref, right_ref, last_left_ref,
    last_right_ref, slots_ref, probs_ref, down_ref, up_ref, grad_ref, scaled_ref, back_ref,
    gattn_ref,
):
    rank = place_ref[0]
    rate = table_ref[langs_ref[1, rank]]
    went = dest_ref[1, rank] - rank
    last = place_ref[1] == place_ref[2] - 1

    def chosen():
        back = jnp.zeros((TILE, RANK), F32)
        for c in range(0, QW, 512):
            cols = slice(c, c + 512)
            left = jnp.where(last, last_left_ref[:, cols], left_ref[:, cols])
            right = jnp.where(last, last_right_ref[:, cols], right_ref[:, cols])
            mid = slots_ref[TILE : 2 * TILE, cols]
            grad = jnp.where(went < 0, left, jnp.where(went > 0, right, mid))
            gattn_ref[:, cols] = grad
            scaled = (rate * grad.astype(F32)).astype(BF16)
            scaled_ref[:, cols] = scaled
            back = back + dot(scaled, up_ref[:, cols], NT)
        return back.astype(BF16)

    @pl.when(place_ref[1] != 0)
    def _():
        back = chosen()
        back_ref[...] = back
        for j in range(KV):
            block = slice(j * GW, (j + 1) * GW)
            gattn = gattn_ref[:, block].astype(F32) + dot(back, down_ref[block, :], NT)
            gattn_ref[:, block] = gattn.astype(BF16)
            queries = stacked(qkv_ref, j * GW)
            keys = qkv_ref[:, QW + j * HEAD_DIM : QW + (j + 1) * HEAD_DIM]
            values = qkv_ref[:, QW + KW + j * HEAD_DIM : QW + KW + (j + 1) * HEAD_DIM]
            grads = stacked(gattn_ref, j * GW)
            grad_probs = dot(grads, values, NT)
            lows, scores = [], []
            for h in range(GROUP):
                probs = probs_ref[j * GW + h * TILE : j * GW + (h + 1) * TILE, :]
                lows.append(probs.astype(BF16))
                weighed = probs * grad_probs[h * TILE : (h + 1) * TILE]
                delta = jnp.sum(weighed, axis=-1, keepdims=True)
                scores.append(((weighed - probs * delta) * SCALE).astype(BF16))
            probs_low = jnp.concatenate(lows, axis=0)
            grad_scores = jnp.concatenate(scores, axis=0)
            grad_queries = dot(grad_scores, keys, NN).astype(BF16)
            for h in range(GROUP):
                cols = slice(j * GW + h * HEAD_DIM, j * GW + (h + 1) * HEAD_DIM)
                grad_ref[:, cols] = grad_queries[h * TILE : (h + 1) * TILE]
            cols = slice(QW + j * HEAD_DIM, QW + (j + 1) * HEAD_DIM)
            grad_ref[:, cols] = dot(grad_scores, queries, TN).astype(BF16)
            cols = slice(QW + KW + j * HEAD_DIM, QW + KW + (j + 1) * HEAD_DIM)
            grad_ref[:, cols] = dot(probs_low, grads, TN).astype(BF16)

    @pl.when(place_ref[1] == 0)
    def _():
        grad_ref[...] = jnp.zeros(grad_ref.shape, BF16)
        scaled_ref[...] = jnp.zeros(scaled_ref.shape, BF16)
        back_ref[...] = jnp.zeros(back_ref.shape, BF16)


COST = pl.CostEstimate(flops=2**20, bytes_accessed=2**20, transcendentals=0)
SMEM = pl.BlockSpec(memory_space=pltpu.SMEM)
VMEM = pl.BlockSpec(memory_space=pltpu.VMEM)


def run_forward(rank, lengths, languages, table, qkv, down, up):
    return pl.pallas_call(
        forward_kernel,
        out_shape=jax.ShapeDtypeStruct((TILE, QW), BF16),
        in_specs=[SMEM] * 4 + [VMEM] * 3,
        out_specs=VMEM,
        scratch_shapes=[pltpu.VMEM((GROUP * TILE, TILE), F32)],
        compiler_params=pltpu.CompilerParams(vmem_limit_bytes=24 * 2**20),
        cost_estimate=COST,
        name="forward_tile",
    )(rank, lengths, languages, table, qkv, down, up)


def run_prepare(place, lengths, languages, dest, table, qkv, slots, down, up):
    message = jax.ShapeDtypeStruct((TILE, 2 * RANK), BF16)
    return pl.pallas_call(
        prepare_kernel,
        out_shape=(
            jax.ShapeDtypeStruct((QW, TILE), F32),
            jax.ShapeDtypeStruct((TILE, QW), BF16),
            jax.ShapeDtypeStruct((TILE, RANK), BF16),
            message,
            message,
            message,
        ),
        in_specs=[SMEM] * 5 + [VMEM] * 4,
        out_specs=(VMEM,) * 6,
        compiler_params=pltpu.CompilerParams(vmem_limit_bytes=40 * 2**20),
        cost_estimate=COST,
        name="prepare_tile",
    )(place, lengths, languages, dest, table, qkv, slots, down, up)


def run_terms(place, languages, dest, table, attn, slots, left, own, right, scaled, back, low):
    return pl.pallas_call(
        terms_kernel,
        out_shape=jax.ShapeDtypeStruct((QW, 2 * RANK), BF16),
        in_specs=[SMEM] * 4 + [VMEM] * 8,
        out_specs=VMEM,
        scratch_shapes=[pltpu.VMEM((3 * TILE, 512), BF16)],
        compiler_params=pltpu.CompilerParams(vmem_limit_bytes=40 * 2**20),
        cost_estimate=COST,
        name="adapter_terms",
    )(place, languages, dest, table, attn, slots, left, own, right, scaled, back, low)


def run_backward(place, languages, dest, table, qkv, moved, slots, probs, down, up):
    return pl.pallas_call(
        backward_kernel,
        out_shape=(
            jax.ShapeDtypeStruct((TILE, QW + 2 * KW), BF16),
            jax.ShapeDtypeStruct((TILE, QW), BF16),
            jax.ShapeDtypeStruct((TILE, RANK), BF16),
        ),
        in_specs=[SMEM] * 4 + [VMEM] * 9,
        out_specs=(VMEM,) * 3,
        scratch_shapes=[pltpu.VMEM((TILE, QW), BF16)],
        compiler_params=pltpu.CompilerParams(vmem_limit_bytes=48 * 2**20),
        cost_estimate=COST,
        name="backward_tile",
    )(place, languages, dest, table, qkv, *moved, slots, probs, down, up)


def place_kernel(
    place_ref, dest_ref, before_ref, near_ref, after_ref, far_before_ref, far_ref, far_after_ref,
    back_ref, placed_ref, handed_ref, zero_ref, sems,
):
    rank, section = place_ref[0], place_ref[1]
    tiles = dest_ref.shape[1]
    zero_ref[...] = jnp.zeros(zero_ref.shape, BF16)
    handed = pltpu.make_async_copy(back_ref, handed_ref, sems.at[0])
    handed.start()
    copies = []
    for k, (near, far) in enumerate(
        ((before_ref, far_before_ref), (near_ref, far_ref), (after_ref, far_after_ref))
    ):
        tile = rank + (k - 1)
        held = jnp.clip(tile, 0, tiles - 1)
        live = (tile == held) & (dest_ref[0, held] == rank) & (section > 0)
        slot = placed_ref.at[pl.ds(k * TILE, TILE), :]
        for source, chosen in (
            (near, live & (section != 2)),
            (far, live & (section == 2)),
            (zero_ref, jnp.logical_not(live)),
        ):
            copies.append((pltpu.make_async_copy(source, slot, sems.at[k + 1]), chosen))
    for copy, chosen in copies:
        pl.when(chosen)(copy.start)
    for copy, chosen in copies:
        pl.when(chosen)(copy.wait)
    handed.wait()


def run_place(place, dest, *tiles):
    return pl.pallas_call(
        place_kernel,
        out_shape=(
            jax.ShapeDtypeStruct((3 * TILE, QW), BF16),
            jax.ShapeDtypeStruct(tiles[-1].shape, BF16),
        ),
        in_specs=[SMEM] * 2 + [VMEM] * len(tiles),
        out_specs=(pl.BlockSpec(memory_space=pl.ANY),) * 2,
        scratch_shapes=[pltpu.VMEM((TILE, QW), BF16), pltpu.SemaphoreType.DMA((4,))],
        compiler_params=pltpu.CompilerParams(vmem_limit_bytes=24 * 2**20),
        cost_estimate=COST,
        name="place_outputs",
    )(place, dest, *tiles)


def sections():
    return lax.axis_size("section")


def shift(x, moves):
    size = lax.axis_size("dp")
    route = []
    for s_list, up, step, keep in moves:
        for s in s_list:
            for t in range(size):
                if 0 <= s + up < sections() and 0 <= t + step < size and keep(t):
                    route.append((s * size + t, (s + up) * size + t + step))
    return lax.ppermute(x, AXES, route)


def anywhere(t):
    return True


def run_start(t):
    return t % RUN == 0


def run_end(t):
    return t % RUN == RUN - 1


def not_run_start(t):
    return t % RUN != 0


def not_run_end(t):
    return t % RUN != RUN - 1


def scatter(x, groups):
    return lax.all_to_all(x, "dp", 0, 0, axis_index_groups=groups, tiled=True)


def shards(
    qkv_a, qkv_b, slot_grad_b, adapter_down, adapter_up, lang_scale, languages, lengths, destination
):
    rank, size = lax.axis_index("dp"), lax.axis_size("dp")
    section, last = lax.axis_index("section"), sections() - 1
    place = jnp.stack([rank, section, jnp.int32(sections())]).astype(jnp.int32)
    down, up = adapter_down[0], adapter_up[0]
    slots = slot_grad_b[0]
    every, early = range(sections()), range(1, last)
    to_up, to_down = slots[2 * TILE :], slots[:TILE]
    from_left = shift(to_up, [(early, 0, 1, anywhere)])
    from_right = shift(to_down, [(early, 0, -1, anywhere)])
    out = run_forward(place, lengths, languages, lang_scale, qkv_a[0], down, up)
    out, place = lax.optimization_barrier((out, place))
    near = shift(out, [([0, 2], 1, 0, anywhere)])
    far = shift(out, [([1], 1, 0, anywhere)])
    probs, attn, low, to_left, own, to_right = run_prepare(
        place, lengths, languages, destination, lang_scale, qkv_b[0], slots, down, up
    )
    from_left, from_right, low = lax.optimization_barrier((from_left, from_right, low))
    to_up, to_down, near, low = lax.optimization_barrier((to_up, to_down, near, low))
    last_left = shift(to_up, [([last], 0, 1, anywhere)])
    last_right = shift(to_down, [([last], 0, -1, anywhere)])
    grad_qkv, scaled, back = run_backward(
        place, languages, destination, lang_scale, qkv_b[0],
        (from_left, from_right, last_left, last_right), slots, probs, down, up,
    )
    grad_qkv, near, to_left, to_right = lax.optimization_barrier(
        (grad_qkv, near, to_left, to_right)
    )
    handed_back = shift(grad_qkv, [(every, -1, 0, anywhere)])[None]
    before = shift(near, [([1, 3], 0, 1, anywhere)])
    after = shift(near, [([1, 3], 0, -1, anywhere)])
    left = shift(to_right, [([0], 0, 1, anywhere)])
    right = shift(to_left, [([0], 0, -1, anywhere)])
    terms = run_terms(
        place, languages, destination, lang_scale, attn, slots, left, own, right, scaled, back, low
    )
    planes = [[RUN * k + z for k in range(size // RUN)] for z in range(RUN)]
    columns = [[RUN * k + z for z in range(RUN)] for k in range(size // RUN)]
    far, terms = lax.optimization_barrier((far, terms))
    pieces = scatter(terms.reshape(size // RUN, -1, 2 * RANK), planes)
    crossed = section == 2
    sent = jnp.where(crossed, far, out)
    far_before = shift(sent, [([1], 1, 1, run_end), ([2], 0, 1, not_run_end)])
    far_after = shift(sent, [([1], 1, -1, run_start), ([2], 0, -1, not_run_start)])
    pieces, handed_back, before, after = lax.optimization_barrier(
        (pieces, handed_back, before, after)
    )
    terms = jnp.sum(pieces.astype(F32), axis=0)
    terms = jnp.sum(scatter(terms.reshape(RUN, -1, 2 * RANK), columns), axis=0)
    handed_forward, handed_back = run_place(
        place, destination, before, near, after, far_before, far, far_after, handed_back[0]
    )
    return (handed_forward[None], handed_back[None], terms[None])


def solution(mesh):
    return jax.shard_map(
        shards,
        mesh=mesh,
        in_specs=(
            P("section", "dp", None),
            P("section", "dp", None),
            P("section", "dp", None),
            P("section", None, None),
            P("section", None, None),
            P(),
            P(),
            P(),
            P(),
        ),
        out_specs=(P("section", "dp", None), P("section", "dp", None), P("section", "dp", None)),
        check_vma=False,
    )
```

```python
import functools
import math

import jax
import jax.numpy as jnp
from jax import lax
from jax.experimental import pallas as pl
from jax.experimental.pallas import tpu as pltpu
from jax.sharding import PartitionSpec as P

HEADS = 32
KV = 4
GROUP = HEADS // KV
HEAD_DIM = 128
TILE = 128
SEGS = 8
RANK = 64
QW = HEADS * HEAD_DIM
KW = KV * HEAD_DIM
GW = GROUP * HEAD_DIM
SCALE = 1.0 / math.sqrt(HEAD_DIM)
RUN = 4
AXES = ("section", "dp")
BF16 = jnp.bfloat16
F32 = jnp.float32


def dot(a, b, dims):
    return lax.dot_general(a, b, (dims, ((), ())), preferred_element_type=F32)


NN = ((1,), (0,))
NT = ((1,), (1,))
TN = ((0,), (0,))


def mask_bias(lens_ref, m, rank):
    shape = (TILE, TILE)
    row = lax.broadcasted_iota(jnp.int32, shape, 0)
    col = lax.broadcasted_iota(jnp.int32, shape, 1)
    seg_row = jnp.zeros(shape, jnp.int32)
    seg_col = jnp.zeros(shape, jnp.int32)
    end = jnp.int32(0)
    for k in range(SEGS):
        end = end + lens_ref[m, rank, k]
        seg_row = seg_row + (row >= end).astype(jnp.int32)
        seg_col = seg_col + (col >= end).astype(jnp.int32)
    allowed = (seg_row == seg_col) & (row >= col)
    return jnp.where(allowed, 0.0, -1e30).astype(F32)


def stacked(ref, base):
    return jnp.concatenate(
        [ref[:, base + h * HEAD_DIM : base + (h + 1) * HEAD_DIM] for h in range(GROUP)], axis=0
    )


def softmax(scores, bias):
    masked = scores + bias
    top = jnp.max(masked, axis=-1, keepdims=True)
    weights = jnp.exp2((masked - top) * (SCALE * math.log2(math.e)))
    return weights * (1.0 / jnp.sum(weights, axis=-1, keepdims=True))


def attend_group(j, qkv_ref, bias, probs_ref):
    keys = qkv_ref[:, QW + j * HEAD_DIM : QW + (j + 1) * HEAD_DIM]
    values = qkv_ref[:, QW + KW + j * HEAD_DIM : QW + KW + (j + 1) * HEAD_DIM]
    queries = stacked(qkv_ref, j * GW)
    probs_ref[...] = dot(queries, keys, NT)
    lows = []
    for h in range(GROUP):
        rows = slice(h * TILE, (h + 1) * TILE)
        probs = softmax(probs_ref[rows, :], bias)
        probs_ref[rows, :] = probs
        lows.append(probs.astype(BF16))
    probs_low = jnp.concatenate(lows, axis=0)
    attn = dot(probs_low, values, NN).astype(BF16)
    return queries, keys, values, probs_low, attn


def forward_kernel(rank_ref, lens_ref, langs_ref, table_ref, qkv_ref, down_ref, up_ref, out_ref, probs_ref):
    rank = rank_ref[0]
    rate = table_ref[langs_ref[0, rank]]
    bias = mask_bias(lens_ref, 0, rank)
    low = jnp.zeros((TILE, RANK), F32)
    for j in range(KV):
        attn = attend_group(j, qkv_ref, bias, probs_ref)[-1]
        for h in range(GROUP):
            cols = slice(j * GW + h * HEAD_DIM, j * GW + (h + 1) * HEAD_DIM)
            out_ref[:, cols] = attn[h * TILE : (h + 1) * TILE]
        low = low + dot(out_ref[:, j * GW : (j + 1) * GW], down_ref[j * GW : (j + 1) * GW, :], NN)
    low = low.astype(BF16)
    for c in range(0, QW, 512):
        lift = dot(low, up_ref[:, c : c + 512], NN)
        out_ref[:, c : c + 512] = (out_ref[:, c : c + 512].astype(F32) + rate * lift).astype(BF16)


def slot_rate(k, rank, tiles, langs_ref, dest_ref, table_ref):
    tile = rank + (k - 1)
    near = jnp.clip(tile, 0, tiles - 1)
    live = (tile == near) & (dest_ref[1, near] == rank)
    return jnp.where(live, table_ref[langs_ref[1, near]], 0.0)


def prepare_kernel(
    place_ref, lens_ref, langs_ref, dest_ref, table_ref, qkv_ref, slots_ref, down_ref, up_ref,
    probs_ref, attn_ref, low_ref, left_ref, own_ref, right_ref,
):
    rank = place_ref[0]
    tiles = lens_ref.shape[1]
    bias = mask_bias(lens_ref, 1, rank)
    low = jnp.zeros((TILE, RANK), F32)
    for j in range(KV):
        block = slice(j * GW, (j + 1) * GW)
        attn = attend_group(j, qkv_ref, bias, probs_ref.at[block, :])[-1]
        for h in range(GROUP):
            cols = slice(j * GW + h * HEAD_DIM, j * GW + (h + 1) * HEAD_DIM)
            attn_ref[:, cols] = attn[h * TILE : (h + 1) * TILE]
        low = low + dot(attn_ref[:, block], down_ref[block, :], NN)
    low_ref[...] = low.astype(BF16)

    @pl.when(place_ref[1] == 0)
    def _():
        for k, out_ref in enumerate((left_ref, own_ref, right_ref)):
            rate = slot_rate(k, rank, tiles, langs_ref, dest_ref, table_ref)
            back = jnp.zeros((TILE, RANK), F32)
            for c in range(0, QW, 512):
                cols = slice(c, c + 512)
                grad = slots_ref[k * TILE : (k + 1) * TILE, cols]
                scaled = (rate * grad.astype(F32)).astype(BF16)
                back = back + dot(scaled, up_ref[:, cols], NT)
            out_ref[...] = jnp.concatenate([low, back], axis=1).astype(BF16)

    @pl.when(place_ref[1] != 0)
    def _():
        for out_ref in (left_ref, own_ref, right_ref):
            out_ref[...] = jnp.zeros(out_ref.shape, BF16)


def terms_kernel(
    place_ref, langs_ref, dest_ref, table_ref, attn_ref, slots_ref, left_ref, own_ref, right_ref,
    scaled_ref, back_ref, low_ref, terms_ref, slot_scaled_ref,
):
    rank = place_ref[0]
    tiles = dest_ref.shape[1]

    @pl.when(place_ref[1] == 0)
    def _():
        went = dest_ref[1, rank] - rank
        back = jnp.where(went < 0, left_ref[...], jnp.where(went > 0, right_ref[...], own_ref[...]))
        lows = jnp.concatenate([left_ref[...], own_ref[...], right_ref[...]], axis=0)
        for c in range(0, QW, 512):
            cols = slice(c, c + 512)
            for k in range(3):
                rows = slice(k * TILE, (k + 1) * TILE)
                rate = slot_rate(k, rank, tiles, langs_ref, dest_ref, table_ref)
                slot_scaled_ref[rows, :] = (rate * slots_ref[rows, cols].astype(F32)).astype(BF16)
            one = dot(attn_ref[:, cols], back, TN)
            two = dot(slot_scaled_ref[...], lows, TN)
            terms = jnp.concatenate([one[:, RANK:], two[:, :RANK]], axis=1)
            terms_ref[cols, :] = terms.astype(terms_ref.dtype)

    @pl.when(place_ref[1] != 0)
    def _():
        for c in range(0, QW, 512):
            cols = slice(c, c + 512)
            one = dot(attn_ref[:, cols], back_ref[...], TN)
            two = dot(scaled_ref[:, cols], low_ref[...], TN)
            terms_ref[cols, :] = jnp.concatenate([one, two], axis=1).astype(terms_ref.dtype)


def backward_kernel(
    place_ref, langs_ref, dest_ref, table_ref, qkv_ref, left_ref, right_ref, last_left_ref,
    last_right_ref, slots_ref, probs_ref, down_ref, up_ref, grad_ref, scaled_ref, back_ref,
    gattn_ref, mid_ref, sem,
):
    rank = place_ref[0]
    rate = table_ref[langs_ref[1, rank]]
    went = dest_ref[1, rank] - rank
    last = place_ref[1] == place_ref[2] - 1

    fetch = pltpu.make_async_copy(slots_ref.at[pl.ds(TILE, TILE), :], mid_ref, sem)

    def chosen():
        fetch.start()
        fetch.wait()
        back = jnp.zeros((TILE, RANK), F32)
        for c in range(0, QW, 512):
            cols = slice(c, c + 512)
            left = jnp.where(last, last_left_ref[:, cols], left_ref[:, cols])
            right = jnp.where(last, last_right_ref[:, cols], right_ref[:, cols])
            mid = mid_ref[:, cols]
            grad = jnp.where(went < 0, left, jnp.where(went > 0, right, mid))
            gattn_ref[:, cols] = grad
            scaled = (rate * grad.astype(F32)).astype(BF16)
            scaled_ref[:, cols] = scaled
            back = back + dot(scaled, up_ref[:, cols], NT)
        return back.astype(BF16)

    @pl.when(place_ref[1] != 0)
    def _():
        back = chosen()
        back_ref[...] = back
        for j in range(KV):
            block = slice(j * GW, (j + 1) * GW)
            gattn = gattn_ref[:, block].astype(F32) + dot(back, down_ref[block, :], NT)
            gattn_ref[:, block] = gattn.astype(BF16)
            queries = stacked(qkv_ref, j * GW)
            keys = qkv_ref[:, QW + j * HEAD_DIM : QW + (j + 1) * HEAD_DIM]
            values = qkv_ref[:, QW + KW + j * HEAD_DIM : QW + KW + (j + 1) * HEAD_DIM]
            grads = stacked(gattn_ref, j * GW)
            grad_probs = dot(grads, values, NT)
            lows, scores = [], []
            for h in range(GROUP):
                probs = probs_ref[j * GW + h * TILE : j * GW + (h + 1) * TILE, :]
                lows.append(probs.astype(BF16))
                weighed = probs * grad_probs[h * TILE : (h + 1) * TILE]
                delta = jnp.sum(weighed, axis=-1, keepdims=True)
                scores.append(((weighed - probs * delta) * SCALE).astype(BF16))
            probs_low = jnp.concatenate(lows, axis=0)
            grad_scores = jnp.concatenate(scores, axis=0)
            grad_queries = dot(grad_scores, keys, NN).astype(BF16)
            for h in range(GROUP):
                cols = slice(j * GW + h * HEAD_DIM, j * GW + (h + 1) * HEAD_DIM)
                grad_ref[:, cols] = grad_queries[h * TILE : (h + 1) * TILE]
            cols = slice(QW + j * HEAD_DIM, QW + (j + 1) * HEAD_DIM)
            grad_ref[:, cols] = dot(grad_scores, queries, TN).astype(BF16)
            cols = slice(QW + KW + j * HEAD_DIM, QW + KW + (j + 1) * HEAD_DIM)
            grad_ref[:, cols] = dot(probs_low, grads, TN).astype(BF16)

    @pl.when(place_ref[1] == 0)
    def _():
        grad_ref[...] = jnp.zeros(grad_ref.shape, BF16)
        scaled_ref[...] = jnp.zeros(scaled_ref.shape, BF16)
        back_ref[...] = jnp.zeros(back_ref.shape, BF16)


COST = pl.CostEstimate(flops=2**20, bytes_accessed=2**20, transcendentals=0)
SMEM = pl.BlockSpec(memory_space=pltpu.SMEM)
VMEM = pl.BlockSpec(memory_space=pltpu.VMEM)


def run_forward(rank, lengths, languages, table, qkv, down, up):
    return pl.pallas_call(
        forward_kernel,
        out_shape=jax.ShapeDtypeStruct((TILE, QW), BF16),
        in_specs=[SMEM] * 4 + [VMEM] * 3,
        out_specs=VMEM,
        scratch_shapes=[pltpu.VMEM((GROUP * TILE, TILE), F32)],
        compiler_params=pltpu.CompilerParams(vmem_limit_bytes=24 * 2**20),
        cost_estimate=COST,
        name="forward_tile",
    )(rank, lengths, languages, table, qkv, down, up)


def run_prepare(place, lengths, languages, dest, table, qkv, slots, down, up):
    message = jax.ShapeDtypeStruct((TILE, 2 * RANK), BF16)
    return pl.pallas_call(
        prepare_kernel,
        out_shape=(
            jax.ShapeDtypeStruct((QW, TILE), F32),
            jax.ShapeDtypeStruct((TILE, QW), BF16),
            jax.ShapeDtypeStruct((TILE, RANK), BF16),
            message,
            message,
            message,
        ),
        in_specs=[SMEM] * 5 + [VMEM] * 4,
        out_specs=(VMEM,) * 6,
        compiler_params=pltpu.CompilerParams(vmem_limit_bytes=40 * 2**20),
        cost_estimate=COST,
        name="prepare_tile",
    )(place, lengths, languages, dest, table, qkv, slots, down, up)


def run_terms(place, languages, dest, table, attn, slots, left, own, right, scaled, back, low):
    return pl.pallas_call(
        terms_kernel,
        out_shape=jax.ShapeDtypeStruct((QW, 2 * RANK), BF16),
        in_specs=[SMEM] * 4 + [VMEM] * 8,
        out_specs=VMEM,
        scratch_shapes=[pltpu.VMEM((3 * TILE, 512), BF16)],
        compiler_params=pltpu.CompilerParams(vmem_limit_bytes=40 * 2**20),
        cost_estimate=COST,
        name="adapter_terms",
    )(place, languages, dest, table, attn, slots, left, own, right, scaled, back, low)


def run_backward(place, languages, dest, table, qkv, moved, slots, probs, down, up):
    return pl.pallas_call(
        backward_kernel,
        out_shape=(
            jax.ShapeDtypeStruct((TILE, QW + 2 * KW), BF16),
            jax.ShapeDtypeStruct((TILE, QW), BF16),
            jax.ShapeDtypeStruct((TILE, RANK), BF16),
        ),
        in_specs=[SMEM] * 4 + [VMEM] * 5 + [pl.BlockSpec(memory_space=pl.ANY)] + [VMEM] * 3,
        out_specs=(VMEM,) * 3,
        scratch_shapes=[
            pltpu.VMEM((TILE, QW), BF16),
            pltpu.VMEM((TILE, QW), BF16),
            pltpu.SemaphoreType.DMA,
        ],
        compiler_params=pltpu.CompilerParams(vmem_limit_bytes=48 * 2**20),
        cost_estimate=COST,
        name="backward_tile",
    )(place, languages, dest, table, qkv, *moved, slots, probs, down, up)


def place_kernel(
    place_ref, dest_ref, before_ref, near_ref, after_ref, far_before_ref, far_ref, far_after_ref,
    back_ref, placed_ref, handed_ref, zero_ref, sems,
):
    rank, section = place_ref[0], place_ref[1]
    tiles = dest_ref.shape[1]
    zero_ref[...] = jnp.zeros(zero_ref.shape, BF16)
    handed = pltpu.make_async_copy(back_ref, handed_ref, sems.at[0])
    handed.start()
    copies = []
    for k, (near, far) in enumerate(
        ((before_ref, far_before_ref), (near_ref, far_ref), (after_ref, far_after_ref))
    ):
        tile = rank + (k - 1)
        held = jnp.clip(tile, 0, tiles - 1)
        live = (tile == held) & (dest_ref[0, held] == rank) & (section > 0)
        slot = placed_ref.at[pl.ds(k * TILE, TILE), :]
        for source, chosen in (
            (near, live & (section != 2)),
            (far, live & (section == 2)),
            (zero_ref, jnp.logical_not(live)),
        ):
            copies.append((pltpu.make_async_copy(source, slot, sems.at[k + 1]), chosen))
    for copy, chosen in copies:
        pl.when(chosen)(copy.start)
    for copy, chosen in copies:
        pl.when(chosen)(copy.wait)
    handed.wait()


def run_place(place, dest, *tiles):
    return pl.pallas_call(
        place_kernel,
        out_shape=(
            jax.ShapeDtypeStruct((3 * TILE, QW), BF16),
            jax.ShapeDtypeStruct(tiles[-1].shape, BF16),
        ),
        in_specs=[SMEM] * 2 + [VMEM] * len(tiles),
        out_specs=(pl.BlockSpec(memory_space=pl.ANY),) * 2,
        scratch_shapes=[pltpu.VMEM((TILE, QW), BF16), pltpu.SemaphoreType.DMA((4,))],
        compiler_params=pltpu.CompilerParams(vmem_limit_bytes=24 * 2**20),
        cost_estimate=COST,
        name="place_outputs",
    )(place, dest, *tiles)


def sections():
    return lax.axis_size("section")


def shift(x, moves):
    size = lax.axis_size("dp")
    route = []
    for s_list, up, step, keep in moves:
        for s in s_list:
            for t in range(size):
                if 0 <= s + up < sections() and 0 <= t + step < size and keep(t):
                    route.append((s * size + t, (s + up) * size + t + step))
    return lax.ppermute(x, AXES, route)


def anywhere(t):
    return True


def run_start(t):
    return t % RUN == 0


def run_end(t):
    return t % RUN == RUN - 1


def not_run_start(t):
    return t % RUN != 0


def not_run_end(t):
    return t % RUN != RUN - 1


def scatter(x, groups):
    return lax.all_to_all(x, "dp", 0, 0, axis_index_groups=groups, tiled=True)


def shards(
    qkv_a, qkv_b, slot_grad_b, adapter_down, adapter_up, lang_scale, languages, lengths, destination
):
    rank, size = lax.axis_index("dp"), lax.axis_size("dp")
    section, last = lax.axis_index("section"), sections() - 1
    place = jnp.stack([rank, section, jnp.int32(sections())]).astype(jnp.int32)
    down, up = adapter_down[0], adapter_up[0]
    slots = slot_grad_b[0]
    every, early = range(sections()), range(1, last)
    to_up, to_down = slots[2 * TILE :], slots[:TILE]
    from_left = shift(to_up, [(early, 0, 1, anywhere)])
    from_right = shift(to_down, [(early, 0, -1, anywhere)])
    out = run_forward(place, lengths, languages, lang_scale, qkv_a[0], down, up)
    out, place = lax.optimization_barrier((out, place))
    near = shift(out, [([0, 2], 1, 0, anywhere)])
    far = shift(out, [([1], 1, 0, anywhere)])
    probs, attn, low, to_left, own, to_right = run_prepare(
        place, lengths, languages, destination, lang_scale, qkv_b[0], slots, down, up
    )
    from_left, from_right, low = lax.optimization_barrier((from_left, from_right, low))
    to_up, to_down, near, low = lax.optimization_barrier((to_up, to_down, near, low))
    last_left = shift(to_up, [([last], 0, 1, anywhere)])
    last_right = shift(to_down, [([last], 0, -1, anywhere)])
    grad_qkv, scaled, back = run_backward(
        place, languages, destination, lang_scale, qkv_b[0],
        (from_left, from_right, last_left, last_right), slots, probs, down, up,
    )
    grad_qkv, near, to_left, to_right = lax.optimization_barrier(
        (grad_qkv, near, to_left, to_right)
    )
    handed_back = shift(grad_qkv, [(every, -1, 0, anywhere)])[None]
    before = shift(near, [([1, 3], 0, 1, anywhere)])
    after = shift(near, [([1, 3], 0, -1, anywhere)])
    left = shift(to_right, [([0], 0, 1, anywhere)])
    right = shift(to_left, [([0], 0, -1, anywhere)])
    terms = run_terms(
        place, languages, destination, lang_scale, attn, slots, left, own, right, scaled, back, low
    )
    planes = [[RUN * k + z for k in range(size // RUN)] for z in range(RUN)]
    columns = [[RUN * k + z for z in range(RUN)] for k in range(size // RUN)]
    far, terms = lax.optimization_barrier((far, terms))
    pieces = scatter(terms.reshape(size // RUN, -1, 2 * RANK), planes)
    crossed = section == 2
    sent = jnp.where(crossed, far, out)
    far_before = shift(sent, [([1], 1, 1, run_end), ([2], 0, 1, not_run_end)])
    far_after = shift(sent, [([1], 1, -1, run_start), ([2], 0, -1, not_run_start)])
    pieces, handed_back, before, after = lax.optimization_barrier(
        (pieces, handed_back, before, after)
    )
    terms = jnp.sum(pieces.astype(F32), axis=0)
    terms = jnp.sum(scatter(terms.reshape(RUN, -1, 2 * RANK), columns), axis=0)
    handed_forward, handed_back = run_place(
        place, destination, before, near, after, far_before, far, far_after, handed_back[0]
    )
    return (handed_forward[None], handed_back[None], terms[None])


def solution(mesh):
    return jax.shard_map(
        shards,
        mesh=mesh,
        in_specs=(
            P("section", "dp", None),
            P("section", "dp", None),
            P("section", "dp", None),
            P("section", None, None),
            P("section", None, None),
            P(),
            P(),
            P(),
            P(),
        ),
        out_specs=(P("section", "dp", None), P("section", "dp", None), P("section", "dp", None)),
        check_vma=False,
    )
```
